32 devices in a mesh: stream: 2 (over x), batch: 16 (over z, y, core).
Axes of the slice: x: 2, y: 2, z: 4, core: 2. Of those that a mesh axis runs over, the one named last changes fastest.
Arguments:
- query_tokens: bfloat16 [4096, 768], P(('stream', 'batch')), may hold values from -6 to 6
- passage_tokens: bfloat16 [32768, 768], P(('stream', 'batch')), may hold values from -6 to 6
- query_lengths: int32 [64], P(('stream', 'batch')), may hold values from 8 to 64
- passage_lengths: int32 [64], P(('stream', 'batch')), may hold values from 64 to 512
- positives: int32 [64], replicated, may hold values from 0 to 63, each once
- w_query: bfloat16 [768, 768], replicated, may hold values from -0.21875 to 0.21875
- b_query: float32 [768], replicated, may hold values from -1.75 to 1.75
- w_key: bfloat16 [768, 768], replicated, may hold values from -0.21875 to 0.21875
- w_value: bfloat16 [768, 768], replicated, may hold values from -0.21875 to 0.21875
- b_value: float32 [768], replicated, may hold values from -0.0625 to 0.0625
- w_out: bfloat16 [768, 768], replicated, may hold values from -1.25 to 1.25
- b_out: float32 [768], replicated, may hold values from -0.1875 to 0.1875
- norm1_gain: float32 [768], replicated, may hold values from 0.5 to 1.5
- norm1_bias: float32 [768], replicated, may hold values from -0.1875 to 0.1875
- w_in: bfloat16 [768, 3072], replicated, may hold values from -0.21875 to 0.21875
- b_in: float32 [3072], replicated, may hold values from -0.625 to 0.625
- w_down: bfloat16 [3072, 768], replicated, may hold values from -0.109375 to 0.109375
- b_down: float32 [768], replicated, may hold values from -0.1875 to 0.1875
- norm2_gain: float32 [768], replicated, may hold values from 0.5 to 1.5
- norm2_bias: float32 [768], replicated, may hold values from -0.1875 to 0.1875
- query_out_grad: bfloat16 [4096, 768], P(('stream', 'batch')), may hold values from -6 to 6
- passage_out_grad: bfloat16 [32768, 768], P(('stream', 'batch')), may hold values from -6 to 6
Outputs:
- query_out: bfloat16 [4096, 768], P(('stream', 'batch'))
- passage_out: bfloat16 [32768, 768], P(('stream', 'batch'))
- query_input_grad: float32 [4096, 768], P(('stream', 'batch'))
- passage_input_grad: float32 [32768, 768], P(('stream', 'batch'))
- loss: float32 [], replicated
- grad_w_query: float32 [768, 768], replicated
- grad_b_query: float32 [768], replicated
- grad_w_key: float32 [768, 768], replicated
- grad_w_value: float32 [768, 768], replicated
- grad_b_value: float32 [768], replicated
- grad_w_out: float32 [768, 768], replicated
- grad_b_out: float32 [768], replicated
- grad_norm1_gain: float32 [768], replicated
- grad_norm1_bias: float32 [768], replicated
- grad_w_in: float32 [768, 3072], replicated
- grad_b_in: float32 [3072], replicated
- grad_w_down: float32 [3072, 768], replicated
- grad_b_down: float32 [768], replicated
- grad_norm2_gain: float32 [768], replicated
- grad_norm2_bias: float32 [768], replicated
The draws below stay inside these ranges and needn't reach their ends.
Inputs may be any that keep to these rules, and one draw needn't show every extreme that they name: positives names every passage exactly once.
All inputs are finite; a program needn't handle non-finite values.
Results may differ from the reference program's by a relative error of at most 0.014.
Values may be sent and summed in bfloat16 or wider, within the bound.
No kernel may reach another device: no remote copies, remote signals or barrier semaphores. Data moves between devices by JAX's collectives and lax.ppermute only.
A program may use at most 192 MiB of HBM per device.

```python
import jax
import jax.numpy as jnp
from jax import lax

D = 768
HEADS = 12
HEAD_DIM = 64
FF = 3072
QRY_LEN = 64
PASS_LEN = 512
NQ = 64
NP = 64
QTOKENS = 4096
PTOKENS = 32768


def place_ends(drawn, stream_key, smallest, largest):
    index_at = [jax.random.randint(jax.random.fold_in(stream_key, axis), (), 0, length) for axis, length in enumerate(drawn.shape)]
    longest = drawn.shape.index(max(drawn.shape))
    next_to = index_at[:longest] + [(index_at[longest] + 1) % drawn.shape[longest]] + index_at[longest + 1:]
    return drawn.at[tuple(index_at)].set(smallest).at[tuple(next_to)].set(largest)


def levels(stream_key, shape, pieces, least, largest):
    def one(position, blocks):
        draws = jax.random.uniform(jax.random.fold_in(jax.random.fold_in(stream_key, 6), position), (blocks,), jnp.float32, least / len(pieces), largest / len(pieces))
        return jnp.repeat(jnp.exp(draws), shape[position] // blocks).reshape((-1,) + (1,) * (len(shape) - position - 1))

    level = one(*pieces[0])
    for cut in pieces[1:]:
        level = level * one(*cut)
    return level


def bell_draw(key, dims, width, bound, pieces=(), kind=jnp.bfloat16):
    factor_of = levels(key, dims, pieces, -0.22, 0.18) if pieces else 1.0
    values = jax.random.normal(key, dims, jnp.float32) * width * factor_of
    return jnp.minimum(jnp.maximum(values, -bound), bound).astype(kind)


def setup_inputs(seed: int = 0) -> dict:
    splits = jax.random.split(jax.random.key(seed), 23)
    query_tokens = bell_draw(splits[0], (QTOKENS, D), 1.0, 6.0, ((0, 32),))
    passage_tokens = bell_draw(splits[1], (PTOKENS, D), 1.0, 6.0, ((0, 32),))
    query_lengths = place_ends(jax.random.randint(splits[2], (NQ,), max(1, QRY_LEN // 8), QRY_LEN + 1), jax.random.fold_in(splits[2], 1), max(1, QRY_LEN // 8), QRY_LEN).astype(jnp.int32)
    passage_lengths = place_ends(jax.random.randint(splits[3], (NP,), PASS_LEN // 8, PASS_LEN + 1), jax.random.fold_in(splits[3], 1), PASS_LEN // 8, PASS_LEN).astype(jnp.int32)
    positives = jax.random.permutation(splits[4], NP).astype(jnp.int32)
    w_query = bell_draw(splits[5], (D, D), D ** -0.5, 0.21875)
    b_query = bell_draw(splits[6], (D,), 0.3, 1.75, (), jnp.float32)
    w_key = bell_draw(splits[7], (D, D), D ** -0.5, 0.21875)
    w_value = bell_draw(splits[8], (D, D), D ** -0.5, 0.21875)
    b_value = bell_draw(splits[9], (D,), 0.01, 0.0625, (), jnp.float32)
    w_out = bell_draw(splits[10], (D, D), (D // 32) ** -0.5, 1.25)
    b_out = bell_draw(splits[11], (D,), 0.03, 0.1875, (), jnp.float32)
    norm1_gain = jnp.clip(1.0 + 0.1 * jax.random.normal(splits[12], (D,), jnp.float32), 0.5, 1.5)
    norm1_bias = bell_draw(splits[13], (D,), 0.03, 0.1875, (), jnp.float32)
    w_in = bell_draw(splits[14], (D, FF), D ** -0.5, 0.21875)
    b_in = bell_draw(splits[15], (FF,), 0.1, 0.625, (), jnp.float32)
    w_down = bell_draw(splits[16], (FF, D), FF ** -0.5, 0.109375)
    b_down = bell_draw(splits[17], (D,), 0.03, 0.1875, (), jnp.float32)
    norm2_gain = jnp.clip(1.0 + 0.1 * jax.random.normal(splits[18], (D,), jnp.float32), 0.5, 1.5)
    norm2_bias = bell_draw(splits[19], (D,), 0.03, 0.1875, (), jnp.float32)
    query_out_grad = bell_draw(splits[20], (QTOKENS, D), 1.0, 6.0, ((0, 32),))
    passage_out_grad = bell_draw(splits[21], (PTOKENS, D), 1.0, 6.0, ((0, 32),))
    return {"query_tokens": query_tokens, "passage_tokens": passage_tokens, "query_lengths": query_lengths, "passage_lengths": passage_lengths, "positives": positives, "w_query": w_query, "b_query": b_query, "w_key": w_key, "w_value": w_value, "b_value": b_value, "w_out": w_out, "b_out": b_out, "norm1_gain": norm1_gain, "norm1_bias": norm1_bias, "w_in": w_in, "b_in": b_in, "w_down": w_down, "b_down": b_down, "norm2_gain": norm2_gain, "norm2_bias": norm2_bias, "query_out_grad": query_out_grad, "passage_out_grad": passage_out_grad}


sharpness_divisor = 0.01
epsilon = 1e-06

@jax.custom_vjp
def low(v):
    return lax.optimization_barrier(v.astype(jnp.bfloat16)).astype(jnp.float32)

@jax.custom_vjp
def low_back(v):
    return v

def low_keep(v):
    return (low(v), None)

def low_pass(kept, grad):
    return (grad,)

def back_keep(v):
    return (v, None)

def back_low(kept, grad):
    return (low(grad),)
low.defvjp(low_keep, low_pass)
low_back.defvjp(back_keep, back_low)

def matmul_high(left, right):
    return jnp.dot(left, right, precision=lax.Precision.HIGHEST)

def layer_norm(value, gain, offset):
    centred = value - lax.optimization_barrier(jnp.mean(value, axis=-1, keepdims=True))
    variance = lax.optimization_barrier(jnp.mean(centred * centred, axis=-1, keepdims=True))
    return centred * lax.rsqrt(variance + epsilon) * gain + offset

def unit_rows(value):
    return value * lax.rsqrt(lax.optimization_barrier(jnp.sum(value * value, axis=-1, keepdims=True)) + epsilon)

def layer_rows(params, rows, key_mask):
    w_query, b_query, w_key, w_value, b_value, w_out, b_out, norm1_gain, norm1_bias, w_in, b_in, w_down, b_down, norm2_gain, norm2_bias = params
    score_scale = HEAD_DIM ** (-0.5)
    query_heads = low(low_back(matmul_high(rows, w_query) + b_query)).reshape(PASS_LEN, HEADS, HEAD_DIM)
    key_heads = low(low_back(matmul_high(rows, w_key))).reshape(PASS_LEN, HEADS, HEAD_DIM)
    value_heads = low(low_back(matmul_high(rows, w_value) + b_value)).reshape(PASS_LEN, HEADS, HEAD_DIM)
    raw_scores = jnp.einsum('qhd,khd->hqk', query_heads, key_heads, precision=lax.Precision.HIGHEST) * score_scale
    scores = jnp.where(key_mask[None], low_back(raw_scores), -1e+30)
    attn_prob = low(jax.nn.softmax(scores, axis=-1))
    mixed = jnp.einsum('hqk,khd->qhd', attn_prob, value_heads, precision=lax.Precision.HIGHEST)
    mixed = low(low_back(mixed.reshape(PASS_LEN, D)))
    attn = low_back(matmul_high(mixed, w_out) + b_out)
    hidden1 = layer_norm(rows + attn, norm1_gain, norm1_bias)
    pre_act = low_back(matmul_high(low(hidden1), w_in) + b_in)
    branch = low_back(matmul_high(low(jax.nn.gelu(pre_act, approximate=False)), w_down) + b_down)
    return layer_norm(hidden1 + branch, norm2_gain, norm2_bias)

def tower(params, rows, key_valid, seg_length):
    grouped = rows.reshape(-1, PASS_LEN, D)
    valid_blocks = key_valid.reshape(-1, PASS_LEN)
    matching_pair_index = jnp.arange(PASS_LEN, dtype=jnp.int32)
    same_seq = matching_pair_index[:, None] // seg_length == matching_pair_index[None, :] // seg_length

    def one_block(block_items):
        block_rows, valid_keys = block_items
        return layer_rows(params, block_rows, same_seq & valid_keys[None, :])
    return lax.map(jax.checkpoint(one_block), (grouped, valid_blocks)).reshape(-1, D)

def pooled(rows, lengths, seg_length):
    grouped = rows.reshape(-1, seg_length, D)
    keep_tok = (jnp.arange(seg_length, dtype=jnp.int32)[None, :] < lengths[:, None]).astype(rows.dtype)
    return lax.optimization_barrier(jnp.sum(grouped * keep_tok[:, :, None], axis=1)) / lengths[:, None].astype(rows.dtype)

def reference(query_tokens, passage_tokens, query_lengths, passage_lengths, positives, w_query, b_query, w_key, w_value, b_value, w_out, b_out, norm1_gain, norm1_bias, w_in, b_in, w_down, b_down, norm2_gain, norm2_bias, query_out_grad, passage_out_grad):
    params = tuple((p.astype(jnp.float32) for p in (w_query, b_query, w_key, w_value, b_value, w_out, b_out, norm1_gain, norm1_bias, w_in, b_in, w_down, b_down, norm2_gain, norm2_bias)))
    rows_query = query_tokens.astype(jnp.float32)
    rows_passage = passage_tokens.astype(jnp.float32)
    query_pos = jnp.arange(QTOKENS, dtype=jnp.int32)
    passage_pos = jnp.arange(PTOKENS, dtype=jnp.int32)
    valid_query = query_pos % QRY_LEN < jnp.repeat(query_lengths, QRY_LEN)
    valid_passage = passage_pos % PASS_LEN < jnp.repeat(passage_lengths, PASS_LEN)
    chosen_match_entry = (positives[:, None] == jnp.arange(NP, dtype=jnp.int32)[None, :]).astype(jnp.float32)

    def forward(weights, query_in, passage_in):
        out_query = tower(weights, query_in, valid_query, QRY_LEN)
        out_passage = tower(weights, passage_in, valid_passage, PASS_LEN)
        unit_query = low(unit_rows(pooled(out_query, query_lengths, QRY_LEN)))
        unit_passage = low(unit_rows(pooled(out_passage, passage_lengths, PASS_LEN)))
        angular_match_matrix = low_back(matmul_high(unit_query, unit_passage.T))
        scaled_match_scores = angular_match_matrix / sharpness_divisor
        loss_sum = jnp.sum(jax.nn.logsumexp(scaled_match_scores, axis=-1) - lax.optimization_barrier(jnp.sum(scaled_match_scores * chosen_match_entry, axis=-1)))
        return (out_query, out_passage, loss_sum)
    outputs, pullback = jax.vjp(forward, params, rows_query, rows_passage)
    out_query, out_passage, loss_sum = outputs
    grads, grad_query, grad_passage = pullback((query_out_grad.astype(jnp.float32), passage_out_grad.astype(jnp.float32), jnp.ones_like(loss_sum)))
    return (out_query.astype(jnp.bfloat16), out_passage.astype(jnp.bfloat16), grad_query, grad_passage, loss_sum / NQ, grads[0], grads[1], grads[2], grads[3], grads[4], grads[5], grads[6], grads[7], grads[8], grads[9], grads[10], grads[11], grads[12], grads[13], grads[14])
```

```python
import jax
import jax.numpy as jnp
from jax import lax
from jax.sharding import PartitionSpec as P

HEADS = 12
QRY_LEN = 64
PASS_LEN = 512


sharpness_divisor = 0.01
epsilon = 1e-06


def layer_norm(value, gain, offset):
    centred = value - jnp.mean(value, axis=-1, keepdims=True)
    variance = jnp.mean(centred * centred, axis=-1, keepdims=True)
    return centred * lax.rsqrt(variance + epsilon) * gain + offset


def unit_rows(value):
    return value * lax.rsqrt(jnp.sum(value * value, axis=-1, keepdims=True) + epsilon)


def gelu_exact(value):
    return jax.nn.gelu(value, approximate=False)


def right_mul(left, weight):
    return jnp.dot(left, weight, preferred_element_type=jnp.float32)


def weight_grad(left, right):
    return jnp.einsum("ta,tb->ab", left, right, preferred_element_type=jnp.float32)


def backward_product(grad_rows, weight):
    return jnp.einsum("tb,ab->ta", grad_rows, weight, preferred_element_type=jnp.float32)


def block_scores(query_rows, key_rows, key_mask, score_scale):
    raw_scores = (
        jnp.einsum("qhd,khd->hqk", query_rows, key_rows, preferred_element_type=jnp.float32)
        * score_scale
    )
    return jnp.where(key_mask[None], raw_scores, -1e30)


AXES = ("stream", "batch")


def swap_with(value, mask, device_count):
    return lax.ppermute(value, AXES, [(i, i ^ mask) for i in range(device_count)])


def bit_orders(device_count):
    top = device_count // 2
    rest = []
    mask = 4
    while mask < top:
        rest.append(mask)
        mask *= 2
    return ([1, top, 2] + rest, [1, 2, top] + rest)


def gather_relative(value, device_count):
    top = device_count // 2
    groups = [[1], [2, top]]
    rest = []
    mask = 4
    while mask < top:
        rest.append(mask)
        mask *= 2
    while rest:
        groups.append(rest[:2])
        rest = rest[2:]
    relative = [0]
    for group in groups:
        combos = [0]
        for mask in group:
            combos = combos + [c ^ mask for c in combos]
        got = [value] + [swap_with(value, c, device_count) for c in combos[1:]]
        value = jnp.concatenate(got, axis=0)
        relative = [c ^ r for c in combos for r in relative]
    return value, relative


def scatter_sum(part, masks, my_index, device_count):
    for mask in masks:
        half = part.shape[0] // 2
        bit = ((my_index & mask) != 0).astype(jnp.int32)
        send = lax.dynamic_slice_in_dim(part, (1 - bit) * half, half, 0)
        keep = lax.dynamic_slice_in_dim(part, bit * half, half, 0)
        got = swap_with(send, mask, device_count)
        part = (keep.astype(jnp.float32) + got.astype(jnp.float32)).astype(part.dtype)
    return part


def gather_back(part, masks, my_index, device_count):
    for mask in reversed(masks):
        bit = (my_index & mask) != 0
        got = swap_with(part, mask, device_count)
        part = jnp.where(
            bit, jnp.concatenate([got, part], 0), jnp.concatenate([part, got], 0)
        )
    return part


def sum_all(part, masks, my_index, device_count):
    part = scatter_sum(part, masks, my_index, device_count)
    return gather_back(part, masks, my_index, device_count)


def body(
    query_tokens,
    passage_tokens,
    query_lengths,
    passage_lengths,
    positives,
    w_query,
    b_query,
    w_key,
    w_value,
    b_value,
    w_out,
    b_out,
    norm1_gain,
    norm1_bias,
    w_in,
    b_in,
    w_down,
    b_down,
    norm2_gain,
    norm2_bias,
    query_out_grad,
    passage_out_grad,
):
    model_width = query_tokens.shape[1]
    head_size = model_width // HEADS
    score_scale = head_size ** (-0.5)

    def tower_forward(rows_in, lengths, seg_len):
        row_count = rows_in.shape[0]
        block_rows = min(row_count, PASS_LEN)
        block_count = row_count // block_rows
        position = jnp.arange(row_count, dtype=jnp.int32)
        len_tok = jnp.repeat(lengths, seg_len)
        key_valid = position % seg_len < len_tok
        valid_blocks = key_valid.reshape(block_count, block_rows)
        matching_pair_index = jnp.arange(block_rows, dtype=jnp.int32)
        same_seq = (
            matching_pair_index[:, None] // seg_len == matching_pair_index[None, :] // seg_len
        )

        def split_heads(rows):
            return rows.reshape(block_count, block_rows, HEADS, head_size)

        query_b = (right_mul(rows_in, w_query) + b_query).astype(jnp.bfloat16)
        key_b = right_mul(rows_in, w_key).astype(jnp.bfloat16)
        value_b = (right_mul(rows_in, w_value) + b_value).astype(jnp.bfloat16)

        def attend(block_items):
            query_rows, key_rows, value_rows, valid_keys = block_items
            scores = block_scores(query_rows, key_rows, same_seq & valid_keys[None, :], score_scale)
            row_top = jnp.max(scores, axis=-1, keepdims=True)
            exp_scores = jnp.exp(scores - row_top)
            row_total = jnp.sum(exp_scores, axis=-1, keepdims=True)
            attn_prob = (exp_scores / row_total).astype(jnp.bfloat16)
            mixed = jnp.einsum(
                "hqk,khd->qhd", attn_prob, value_rows, preferred_element_type=jnp.float32
            )
            return (mixed, (row_top + jnp.log(row_total))[:, :, 0])

        mixed_blocks, log_totals = lax.map(
            attend, (split_heads(query_b), split_heads(key_b), split_heads(value_b), valid_blocks)
        )
        mixed_b = mixed_blocks.reshape(row_count, model_width).astype(jnp.bfloat16)
        resid_one = rows_in.astype(jnp.float32) + right_mul(mixed_b, w_out) + b_out
        hidden_one, back_norm_one = jax.vjp(layer_norm, resid_one, norm1_gain, norm1_bias)
        hidden_one_b = hidden_one.astype(jnp.bfloat16)
        pre_act = right_mul(hidden_one_b, w_in) + b_in
        act_value, back_gelu = jax.vjp(gelu_exact, pre_act)
        act_b = act_value.astype(jnp.bfloat16)
        resid_two = hidden_one + right_mul(act_b, w_down) + b_down
        layer_out, back_norm_two = jax.vjp(layer_norm, resid_two, norm2_gain, norm2_bias)
        seq_slots = jnp.arange(lengths.shape[0], dtype=jnp.int32)
        member = ((position[None, :] // seg_len == seq_slots[:, None]) & key_valid[None, :]).astype(
            jnp.float32
        )
        member = member / lengths[:, None].astype(jnp.float32)
        pooled_rows = jnp.dot(member, layer_out, precision=lax.Precision.HIGHEST)
        unit_value, back_unit = jax.vjp(unit_rows, pooled_rows)
        return {
            "rows_in": rows_in,
            "query_b": query_b,
            "key_b": key_b,
            "value_b": value_b,
            "valid_blocks": valid_blocks,
            "same_seq": same_seq,
            "log_totals": log_totals,
            "mixed_b": mixed_b,
            "back_norm_one": back_norm_one,
            "hidden_one_b": hidden_one_b,
            "back_gelu": back_gelu,
            "act_b": act_b,
            "back_norm_two": back_norm_two,
            "layer_out": layer_out,
            "member": member,
            "unit_value": unit_value,
            "back_unit": back_unit,
            "split_heads": split_heads,
            "row_count": row_count,
        }

    def backward_ffn(saved, out_grad_rows, grad_unit):
        grad_pool = saved["back_unit"](grad_unit)[0]
        grad_layer = out_grad_rows.astype(jnp.float32) + jnp.dot(
            saved["member"].T, grad_pool, precision=lax.Precision.HIGHEST
        )
        grad_resid_two, second_norm_gain_gradient, grad_bias_two = saved["back_norm_two"](
            grad_layer
        )
        grad_branch_b = grad_resid_two.astype(jnp.bfloat16)
        grad_b_down = jnp.sum(grad_branch_b.astype(jnp.float32), axis=0)
        grad_w_down = weight_grad(saved["act_b"], grad_branch_b)
        grad_pre_b = saved["back_gelu"](backward_product(grad_branch_b, w_down))[0].astype(
            jnp.bfloat16
        )
        grad_b_in = jnp.sum(grad_pre_b.astype(jnp.float32), axis=0)
        grad_w_in = weight_grad(saved["hidden_one_b"], grad_pre_b)
        grad_hidden_one = grad_resid_two + backward_product(grad_pre_b, w_in)
        return (
            grad_hidden_one,
            (
                grad_w_in,
                grad_b_in,
                grad_w_down,
                grad_b_down,
                second_norm_gain_gradient,
                grad_bias_two,
            ),
        )

    def backward_attn(saved, grad_hidden_one):
        split_heads = saved["split_heads"]
        same_seq = saved["same_seq"]
        row_count = saved["row_count"]
        grad_resid_one, grad_gain_one, grad_bias_one = saved["back_norm_one"](grad_hidden_one)
        grad_attn_b = grad_resid_one.astype(jnp.bfloat16)
        grad_b_out = jnp.sum(grad_attn_b.astype(jnp.float32), axis=0)
        grad_w_out = weight_grad(saved["mixed_b"], grad_attn_b)
        grad_mixed_b = backward_product(grad_attn_b, w_out).astype(jnp.bfloat16)

        def attend_back(block_items):
            query_rows, key_rows, value_rows, valid_keys, log_total, grad_rows = block_items
            scores = block_scores(query_rows, key_rows, same_seq & valid_keys[None, :], score_scale)
            attn_prob = jnp.exp(scores - log_total[:, :, None])
            grad_prob = jnp.einsum(
                "qhd,khd->hqk", grad_rows, value_rows, preferred_element_type=jnp.float32
            )
            grad_value = jnp.einsum(
                "hqk,qhd->khd",
                attn_prob.astype(jnp.bfloat16),
                grad_rows,
                preferred_element_type=jnp.float32,
            )
            row_delta = jnp.sum(grad_prob * attn_prob, axis=-1, keepdims=True)
            grad_score_b = (attn_prob * (grad_prob - row_delta)).astype(jnp.bfloat16)
            grad_query = (
                jnp.einsum(
                    "hqk,khd->qhd", grad_score_b, key_rows, preferred_element_type=jnp.float32
                )
                * score_scale
            )
            grad_key = (
                jnp.einsum(
                    "hqk,qhd->khd", grad_score_b, query_rows, preferred_element_type=jnp.float32
                )
                * score_scale
            )
            return (grad_query, grad_key, grad_value)

        grad_query_blk, grad_key_blk, grad_value_blk = lax.map(
            attend_back,
            (
                split_heads(saved["query_b"]),
                split_heads(saved["key_b"]),
                split_heads(saved["value_b"]),
                saved["valid_blocks"],
                saved["log_totals"],
                split_heads(grad_mixed_b),
            ),
        )
        grad_query_b = grad_query_blk.reshape(row_count, model_width).astype(jnp.bfloat16)
        grad_key_b = grad_key_blk.reshape(row_count, model_width).astype(jnp.bfloat16)
        grad_value_b = grad_value_blk.reshape(row_count, model_width).astype(jnp.bfloat16)
        rows_in = saved["rows_in"]
        grad_b_query = jnp.sum(grad_query_b.astype(jnp.float32), axis=0)
        grad_b_value = jnp.sum(grad_value_b.astype(jnp.float32), axis=0)
        grad_w_query = weight_grad(rows_in, grad_query_b)
        grad_w_key = weight_grad(rows_in, grad_key_b)
        grad_w_value = weight_grad(rows_in, grad_value_b)
        input_grad = (
            grad_resid_one
            + backward_product(grad_query_b, w_query)
            + backward_product(grad_key_b, w_key)
            + backward_product(grad_value_b, w_value)
        )
        return (
            input_grad,
            (
                grad_w_query,
                grad_b_query,
                grad_w_key,
                grad_w_value,
                grad_b_value,
                grad_w_out,
                grad_b_out,
                grad_gain_one,
                grad_bias_one,
            ),
        )

    question_retained = tower_forward(query_tokens, query_lengths, QRY_LEN)
    passage_saved = tower_forward(passage_tokens, passage_lengths, PASS_LEN)
    unit_query_b = question_retained["unit_value"].astype(jnp.bfloat16)
    unit_passage_b = passage_saved["unit_value"].astype(jnp.bfloat16)
    query_count = query_lengths.shape[0]
    passage_count = passage_lengths.shape[0]
    device_count = lax.axis_size(AXES)
    my_index = lax.axis_index(AXES)
    units, relative = gather_relative(
        jnp.concatenate([unit_query_b, unit_passage_b], 0)[None], device_count
    )
    query_all = units[:, :query_count].reshape(device_count * query_count, model_width)
    passage_all = units[:, query_count:].reshape(device_count * passage_count, model_width)
    owner = jnp.array(relative, jnp.int32) ^ my_index
    query_ids = (owner[:, None] * query_count + jnp.arange(query_count)[None, :]).reshape(-1)
    passage_ids = (owner[:, None] * passage_count + jnp.arange(passage_count)[None, :]).reshape(-1)
    scaled_match_scores = (
        jnp.einsum("qd,pd->qp", query_all, passage_all, preferred_element_type=jnp.float32)
        / sharpness_divisor
    )
    logit_top = jnp.max(scaled_match_scores, axis=-1, keepdims=True)
    normalizer_logsum_value = logit_top + jnp.log(
        jnp.sum(jnp.exp(scaled_match_scores - logit_top), axis=-1, keepdims=True)
    )
    chosen_match_entry = (positives[query_ids][:, None] == passage_ids[None, :]).astype(jnp.float32)
    loss_sum = jnp.sum(
        normalizer_logsum_value[:, 0] - jnp.sum(scaled_match_scores * chosen_match_entry, axis=-1)
    )
    cosine_gradient = (
        (jnp.exp(scaled_match_scores - normalizer_logsum_value) - chosen_match_entry)
        / sharpness_divisor
    ).astype(jnp.bfloat16)
    grad_unit_query = right_mul(cosine_gradient[:query_count], passage_all)
    grad_unit_passage = weight_grad(cosine_gradient[:, :passage_count], query_all)
    hidden_query, ffn_query = backward_ffn(question_retained, query_out_grad, grad_unit_query)
    hidden_passage, ffn_passage = backward_ffn(passage_saved, passage_out_grad, grad_unit_passage)
    ffn_grads = jax.tree.map(jnp.add, ffn_query, ffn_passage)
    query_input_grad, attn_query = backward_attn(question_retained, hidden_query)
    passage_input_grad, attn_passage = backward_attn(passage_saved, hidden_passage)
    attn_local = jax.tree.map(jnp.add, attn_query, attn_passage)
    order_x, order_y = bit_orders(device_count)

    def reduce_pair(first, second):
        return (
            sum_all(first.astype(jnp.bfloat16), order_x, my_index, device_count).astype(jnp.float32),
            sum_all(second.astype(jnp.bfloat16), order_y, my_index, device_count).astype(jnp.float32),
        )

    down_half = ffn_grads[2].shape[0] // 2
    down_top, down_low = reduce_pair(ffn_grads[2][:down_half], ffn_grads[2][down_half:])
    in_half = ffn_grads[0].shape[1] // 2
    in_left, in_right = reduce_pair(ffn_grads[0][:, :in_half], ffn_grads[0][:, in_half:])
    proj_left, proj_right = reduce_pair(
        jnp.concatenate([attn_local[0], attn_local[2]], 1),
        jnp.concatenate([attn_local[3], attn_local[5]], 1),
    )
    smalls = (
        attn_local[1],
        attn_local[4],
        attn_local[6],
        attn_local[7],
        attn_local[8],
        ffn_grads[1],
        ffn_grads[3],
        ffn_grads[4],
        ffn_grads[5],
    )
    packed = jnp.concatenate([v.reshape(-1, model_width) for v in smalls], 0)
    for mask in order_x:
        packed = packed + swap_with(packed, mask, device_count)
    cut = []
    row = 0
    for v in smalls:
        rows = v.shape[0] // model_width
        cut.append(packed[row : row + rows].reshape(-1))
        row += rows
    attn_grads = (
        proj_left[:, :model_width],
        cut[0],
        proj_left[:, model_width:],
        proj_right[:, :model_width],
        cut[1],
        proj_right[:, model_width:],
        cut[2],
        cut[3],
        cut[4],
    )
    ffn_grads = (
        jnp.concatenate([in_left, in_right], 1),
        cut[5],
        jnp.concatenate([down_top, down_low], 0),
        cut[6],
        cut[7],
        cut[8],
    )
    loss = loss_sum / (query_count * device_count)
    return (
        question_retained["layer_out"].astype(jnp.bfloat16),
        passage_saved["layer_out"].astype(jnp.bfloat16),
        query_input_grad,
        passage_input_grad,
        loss,
        attn_grads[0],
        attn_grads[1],
        attn_grads[2],
        attn_grads[3],
        attn_grads[4],
        attn_grads[5],
        attn_grads[6],
        attn_grads[7],
        attn_grads[8],
        ffn_grads[0],
        ffn_grads[1],
        ffn_grads[2],
        ffn_grads[3],
        ffn_grads[4],
        ffn_grads[5],
    )


def solution(mesh):
    placed = (
        P(("stream", "batch"), None),
        P(("stream", "batch"), None),
        P(("stream", "batch")),
        P(("stream", "batch")),
        P(),
        P(),
        P(),
        P(),
        P(),
        P(),
        P(),
        P(),
        P(),
        P(),
        P(),
        P(),
        P(),
        P(),
        P(),
        P(),
        P(("stream", "batch"), None),
        P(("stream", "batch"), None),
    )
    return jax.shard_map(
        body,
        mesh=mesh,
        in_specs=placed,
        out_specs=(
            P(("stream", "batch"), None),
            P(("stream", "batch"), None),
            P(("stream", "batch"), None),
            P(("stream", "batch"), None),
            P(),
            P(),
            P(),
            P(),
            P(),
            P(),
            P(),
            P(),
            P(),
            P(),
            P(),
            P(),
            P(),
            P(),
            P(),
            P(),
        ),
        check_vma=False,
    )
```

```python
import jax
import jax.numpy as jnp
from jax import lax
from jax.experimental import pallas as pl
from jax.experimental.pallas import tpu as pltpu
from jax.sharding import PartitionSpec as P

HEADS = 12
QRY_LEN = 64
PASS_LEN = 512
PAIR_LEN = QRY_LEN + PASS_LEN
LOGIT_SCALE = 0.01
EPS = 1e-06
NEG = -1e30
F32 = jnp.float32
BF16 = jnp.bfloat16
AXES = ("stream", "batch")
VMEM_LIMIT = 60 * 1024 * 1024


def nn(a, b):
    return lax.dot_general(a, b, (((1,), (0,)), ((), ())), preferred_element_type=F32)


def nt(a, b):
    return lax.dot_general(a, b, (((1,), (1,)), ((), ())), preferred_element_type=F32)


def tn(a, b):
    return lax.dot_general(a, b, (((0,), (0,)), ((), ())), preferred_element_type=F32)


def gelu_parts(u):
    a = jnp.abs(u)
    t = 1.0 / (1.0 + (0.3275911 * 0.7071067811865476) * a)
    bell = jnp.exp(-0.5 * (u * u))
    poly = t * (
        0.5 * 0.254829592
        + t * (0.5 * -0.284496736 + t * (0.5 * 1.421413741 + t * (0.5 * -1.453152027 + t * (0.5 * 1.061405429))))
    )
    tail = poly * bell
    cdf = jnp.where(u >= 0, 1.0 - tail, tail)
    return u * cdf, cdf + u * (bell * 0.3989422804014327)


def forward_kernel(
    qlen, plen, xq, xp, wq_h, wk_h, wv_h, wo_h, wi_h, wd_h, bq, bv, bo, n1g, n1b, bi, bd, n2g, n2b,
    yq, yp, q_o, k_o, v_o, o_o, lse_o, xh1_o, rs1_o, h1b_o, g_o, gp_o, xh2_o, rs2_o, unit_o, mean_o,
    xs, wq, wk, wv, wo, wi, wd, acc, h1, kmask, sems,
):
    step = pl.program_id(0)
    width = xs.shape[1]
    copies = [
        pltpu.make_async_copy(src, dst, sems.at[n])
        for n, (src, dst) in enumerate(
            ((wq_h, wq), (wk_h, wk), (wv_h, wv), (wo_h, wo), (wi_h, wi), (wd_h, wd))
        )
    ]

    @pl.when(step == 0)
    def _():
        for c in copies:
            c.start()
        lse_o[...] = jnp.zeros_like(lse_o)

    def ready(n):
        @pl.when(step == 0)
        def _():
            copies[n].wait()

    xs[:QRY_LEN, :] = xq[...]
    xs[QRY_LEN:, :] = xp[...]
    ready(0)
    q_o[...] = (nn(xs[...], wq[...]) + bq[...]).astype(BF16)
    ready(1)
    k_o[...] = nn(xs[...], wk[...]).astype(BF16)
    ready(2)
    v_o[...] = (nn(xs[...], wv[...]) + bv[...]).astype(BF16)

    lane = lax.broadcasted_iota(jnp.int32, (1, 128), 1)
    low = (lane < 64).astype(F32)
    lanes = (low, 1.0 - low)
    ones = ((lane == 64).astype(F32), (lane == 0).astype(F32))
    q_gain = [(v * 0.125).astype(BF16) for v in lanes]
    keep = [v.astype(BF16) for v in lanes]
    one = [v.astype(BF16) for v in ones]

    q_valid = lax.broadcasted_iota(jnp.int32, (QRY_LEN, 128), 0) < qlen[step]
    p_valid = lax.broadcasted_iota(jnp.int32, (PASS_LEN, 128), 0) < plen[step]
    for side in range(2):
        kmask[side, :QRY_LEN, :] = jnp.where(q_valid, 0.0, NEG * ones[side]).astype(BF16)
        kmask[side, QRY_LEN:, :] = jnp.where(p_valid, 0.0, NEG * ones[side]).astype(BF16)

    def attend(pair, carry):
        cols = pl.ds(pl.multiple_of(pair * 128, 128), 128)
        for rows in (pl.ds(0, QRY_LEN), pl.ds(QRY_LEN, PASS_LEN)):
            qp, kp, vp = q_o[rows, cols], k_o[rows, cols], v_o[rows, cols]
            mixed = []
            for side in range(2):
                qe = qp * q_gain[side] + one[side]
                ke = kp * keep[side] + kmask[side, rows, :]
                ve = vp * keep[side] + one[side]
                s = nt(qe, ke)
                top = jnp.max(s, axis=1, keepdims=True)
                p = jnp.exp(s - top).astype(BF16)
                oe = nn(p, ve)
                total = oe[:, 64:65] if side == 0 else oe[:, 0:1]
                mixed.append(oe * (1.0 / total))
                lse = top + jnp.log(total)
                head = 2 * pair + side
                lse_o[rows, :] = jnp.where(lane == head, lse, lse_o[rows, :])
            o_o[rows, cols] = jnp.where(lane < 64, mixed[0], mixed[1]).astype(BF16)
        return carry

    lax.fori_loop(0, HEADS // 2, attend, 0)

    ready(3)
    acc[...] = nn(o_o[...], wo[...])

    def norm(value):
        mean = jnp.mean(value, axis=-1, keepdims=True)
        c = value - mean
        rstd = lax.rsqrt(jnp.mean(c * c, axis=-1, keepdims=True) + EPS)
        return c * rstd, rstd

    CH = 64

    def first_norm(n, carry):
        rows = pl.ds(pl.multiple_of(n * CH, CH), CH)
        xhat, rstd = norm(xs[rows, :].astype(F32) + acc[rows, :] + bo[...])
        hid = xhat * n1g[...] + n1b[...]
        xh1_o[rows, :] = xhat.astype(BF16)
        rs1_o[rows, :] = rstd
        h1[rows, :] = hid
        h1b_o[rows, :] = hid.astype(BF16)
        return carry

    lax.fori_loop(0, PAIR_LEN // CH, first_norm, 0)

    FB = 512
    ready(4)
    ready(5)

    def ffn(n, carry):
        cols = pl.ds(pl.multiple_of(n * FB, FB), FB)
        u = nn(h1b_o[...], wi[:, cols]) + bi[:, cols]
        g, gp = gelu_parts(u)
        gb = g.astype(BF16)
        g_o[:, cols] = gb
        gp_o[:, cols] = gp.astype(BF16)
        h1[...] += nn(gb, wd[cols, :])
        return carry

    lax.fori_loop(0, wi.shape[1] // FB, ffn, 0)

    def second_norm(row0, rows_n, out, valid_n):
        def run(n, total):
            at = pl.multiple_of(n * CH, CH)
            rows = pl.ds(row0 + at, CH)
            xhat, rstd = norm(h1[rows, :] + bd[...])
            y = xhat * n2g[...] + n2b[...]
            xh2_o[rows, :] = xhat.astype(BF16)
            rs2_o[rows, :] = rstd
            out[pl.ds(at, CH), :] = y.astype(BF16)
            live = (lax.broadcasted_iota(jnp.int32, (CH, 1), 0) + at) < valid_n
            return total + jnp.sum(jnp.where(live, y, 0.0), axis=0, keepdims=True)

        total = lax.fori_loop(0, rows_n // CH, run, jnp.zeros((1, width), F32))
        return total / valid_n.astype(F32)

    for kind, mean in enumerate(
        (
            second_norm(0, QRY_LEN, yq, qlen[step]),
            second_norm(QRY_LEN, PASS_LEN, yp, plen[step]),
        )
    ):
        at = pl.ds(2 * step + kind, 1)
        mean_o[at, :] = mean
        unit = mean * lax.rsqrt(jnp.sum(mean * mean, axis=-1, keepdims=True) + EPS)
        unit_o[at, :] = unit


def forward(xq, xp, qlen, plen, p):
    seqs = qlen.shape[0]
    width = xq.shape[1]
    ff = p["w_in"].shape[1]
    rows = seqs * PAIR_LEN
    whole = lambda shape: pl.BlockSpec(shape, lambda i: (0,) * len(shape))
    smem = pl.BlockSpec(memory_space=pltpu.SMEM)
    hbm = pl.BlockSpec(memory_space=pl.ANY)
    row_block = lambda n, w: pl.BlockSpec((n, w), lambda i: (i, 0))
    one_row = lambda v: v.reshape(1, -1)
    outs = [
        ((seqs * QRY_LEN, width), BF16, row_block(QRY_LEN, width)),
        ((seqs * PASS_LEN, width), BF16, row_block(PASS_LEN, width)),
        ((rows, width), BF16, row_block(PAIR_LEN, width)),
        ((rows, width), BF16, row_block(PAIR_LEN, width)),
        ((rows, width), BF16, row_block(PAIR_LEN, width)),
        ((rows, width), BF16, row_block(PAIR_LEN, width)),
        ((rows, 128), F32, row_block(PAIR_LEN, 128)),
        ((rows, width), BF16, row_block(PAIR_LEN, width)),
        ((rows, 1), F32, row_block(PAIR_LEN, 1)),
        ((rows, width), BF16, row_block(PAIR_LEN, width)),
        ((rows, ff), BF16, row_block(PAIR_LEN, ff)),
        ((rows, ff), BF16, row_block(PAIR_LEN, ff)),
        ((rows, width), BF16, row_block(PAIR_LEN, width)),
        ((rows, 1), F32, row_block(PAIR_LEN, 1)),
        ((2 * seqs, width), F32, whole((2 * seqs, width))),
        ((2 * seqs, width), F32, whole((2 * seqs, width))),
    ]
    return pl.pallas_call(
        forward_kernel,
        grid=(seqs,),
        in_specs=[smem, smem, row_block(QRY_LEN, width), row_block(PASS_LEN, width)]
        + [hbm] * 6
        + [whole((1, width))] * 5
        + [whole((1, ff))]
        + [whole((1, width))] * 3,
        out_specs=[o[2] for o in outs],
        out_shape=[jax.ShapeDtypeStruct(o[0], o[1]) for o in outs],
        scratch_shapes=[
            pltpu.VMEM((PAIR_LEN, width), BF16),
            pltpu.VMEM((width, width), BF16),
            pltpu.VMEM((width, width), BF16),
            pltpu.VMEM((width, width), BF16),
            pltpu.VMEM((width, width), BF16),
            pltpu.VMEM((width, ff), BF16),
            pltpu.VMEM((ff, width), BF16),
            pltpu.VMEM((PAIR_LEN, width), F32),
            pltpu.VMEM((PAIR_LEN, width), F32),
            pltpu.VMEM((2, PAIR_LEN, 128), BF16),
            pltpu.SemaphoreType.DMA((6,)),
        ],
        compiler_params=pltpu.CompilerParams(
            dimension_semantics=("arbitrary",), vmem_limit_bytes=VMEM_LIMIT
        ),
        name="forward_layer",
    )(
        qlen, plen, xq, xp, p["w_query"], p["w_key"], p["w_value"], p["w_out"], p["w_in"], p["w_down"],
        one_row(p["b_query"]), one_row(p["b_value"]), one_row(p["b_out"]), one_row(p["norm1_gain"]),
        one_row(p["norm1_bias"]), one_row(p["b_in"]), one_row(p["b_down"]), one_row(p["norm2_gain"]),
        one_row(p["norm2_bias"]),
    )


def loss_kernel(
    qlen, plen, units, target, column_id, mean, ogq, ogp, xh2, rs2, n2g,
    dz_o, dr2_o, small_o, loss_o,
    de,
):
    step = pl.program_id(0)
    seqs = pl.num_programs(0)
    width = xh2.shape[1]
    mine = mean.shape[0]

    @pl.when(step == 0)
    def _():
        u = units[...].astype(BF16)
        n = u.shape[0]
        row = lax.broadcasted_iota(jnp.int32, (n, n), 0)
        col = lax.broadcasted_iota(jnp.int32, (n, n), 1)
        pairs = ((row & 1) == 0) & ((col & 1) == 1)
        logits = jnp.where(pairs, nt(u, u) / LOGIT_SCALE, NEG)
        top = jnp.max(logits, axis=1, keepdims=True)
        lse = top + jnp.log(jnp.sum(jnp.exp(logits - top), axis=1, keepdims=True))
        hit = pairs & (target[...] == column_id[...])
        chosen = jnp.sum(jnp.where(hit, logits, 0.0), axis=1, keepdims=True)
        is_query = (lax.broadcasted_iota(jnp.int32, (n, 1), 0) & 1) == 0
        loss_o[...] = jnp.sum(jnp.where(is_query, lse - chosen, 0.0), axis=0, keepdims=True)
        dc = jnp.where(pairs, (jnp.exp(logits - lse) - hit.astype(F32)) / LOGIT_SCALE, 0.0)
        both = (dc + jnp.transpose(dc)).astype(BF16)
        dn = nn(both[:16], u)[:mine]
        e = mean[...]
        square = jnp.sum(e * e, axis=-1, keepdims=True) + EPS
        grad = (dn - e * (jnp.sum(e * dn, axis=-1, keepdims=True) / square)) * lax.rsqrt(square)
        de[...] = jnp.zeros_like(de)
        de[:mine, :] = grad
        small_o[...] = jnp.zeros_like(small_o)

    CH = 64

    def back(row0, rows_n, grads, valid_n, kind):
        shift = de[pl.ds(2 * step + kind, 1), :] / valid_n.astype(F32)

        def run(n, carry):
            at = pl.multiple_of(n * CH, CH)
            rows = pl.ds(row0 + at, CH)
            live = (lax.broadcasted_iota(jnp.int32, (CH, 1), 0) + at) < valid_n
            dy = grads[pl.ds(at, CH), :].astype(F32) + jnp.where(live, shift, 0.0)
            xhat = xh2[rows, :].astype(F32)
            dyg = dy * n2g[...]
            m1 = jnp.mean(dyg, axis=-1, keepdims=True)
            m2 = jnp.mean(dyg * xhat, axis=-1, keepdims=True)
            dr = rs2[rows, :] * (dyg - m1 - xhat * m2)
            db = dr.astype(BF16)
            dr2_o[rows, :] = dr
            dz_o[rows, :] = db
            small_o[0:1, :] += jnp.sum(dy * xhat, axis=0, keepdims=True)
            small_o[1:2, :] += jnp.sum(dy, axis=0, keepdims=True)
            small_o[2:3, :] += jnp.sum(db.astype(F32), axis=0, keepdims=True)
            return carry

        lax.fori_loop(0, rows_n // CH, run, 0)

    back(0, QRY_LEN, ogq, qlen[step], 0)
    back(QRY_LEN, PASS_LEN, ogp, plen[step], 1)


def loss_and_second_norm(units, target, column_id, mean, qlen, plen, ogq, ogp, xh2, rs2, n2g):
    seqs = qlen.shape[0]
    width = ogq.shape[1]
    rows = seqs * PAIR_LEN
    whole = lambda shape: pl.BlockSpec(shape, lambda i: (0,) * len(shape))
    smem = pl.BlockSpec(memory_space=pltpu.SMEM)
    row_block = lambda n, w: pl.BlockSpec((n, w), lambda i: (i, 0))
    return pl.pallas_call(
        loss_kernel,
        grid=(seqs,),
        in_specs=[
            smem, smem, whole(units.shape), whole(target.shape), whole(column_id.shape), whole(mean.shape),
            row_block(QRY_LEN, width), row_block(PASS_LEN, width), row_block(PAIR_LEN, width),
            row_block(PAIR_LEN, 1), whole((1, width)),
        ],
        out_specs=[row_block(PAIR_LEN, width), row_block(PAIR_LEN, width), whole((8, width)), whole((1, 1))],
        out_shape=[
            jax.ShapeDtypeStruct((rows, width), BF16),
            jax.ShapeDtypeStruct((rows, width), F32),
            jax.ShapeDtypeStruct((8, width), F32),
            jax.ShapeDtypeStruct((1, 1), F32),
        ],
        scratch_shapes=[pltpu.VMEM((8, width), F32)],
        compiler_params=pltpu.CompilerParams(
            dimension_semantics=("arbitrary",), vmem_limit_bytes=VMEM_LIMIT
        ),
        name="loss_norm_back",
    )(qlen, plen, units, target, column_id, mean, ogq, ogp, xh2, rs2, n2g.reshape(1, -1))


def ffn_back_kernel(
    dz, dr2, gp, wd, wi, xh1, rs1, n1g, wo,
    du_o, bi_o, dr1_o, da_o, do_o, small_o,
    acc,
):
    step = pl.program_id(0)
    du = (nt(dz[...], wd[...]) * gp[...].astype(F32)).astype(BF16)
    du_o[...] = du
    bi_o[...] = jnp.sum(du.astype(F32), axis=0, keepdims=True)
    part = nt(du, wi[...])

    @pl.when(step == 0)
    def _():
        acc[...] = dr2[...] + part

    @pl.when(step > 0)
    def _():
        acc[...] += part

    @pl.when(step == pl.num_programs(0) - 1)
    def _():
        CH = 64
        small_o[...] = jnp.zeros_like(small_o)

        def run(n, carry):
            rows = pl.ds(pl.multiple_of(n * CH, CH), CH)
            dh = acc[rows, :]
            xhat = xh1[rows, :].astype(F32)
            dyg = dh * n1g[...]
            m1 = jnp.mean(dyg, axis=-1, keepdims=True)
            m2 = jnp.mean(dyg * xhat, axis=-1, keepdims=True)
            dr = rs1[rows, :] * (dyg - m1 - xhat * m2)
            db = dr.astype(BF16)
            dr1_o[rows, :] = dr
            da_o[rows, :] = db
            small_o[0:1, :] += jnp.sum(dh * xhat, axis=0, keepdims=True)
            small_o[1:2, :] += jnp.sum(dh, axis=0, keepdims=True)
            small_o[2:3, :] += jnp.sum(db.astype(F32), axis=0, keepdims=True)
            return carry

        lax.fori_loop(0, acc.shape[0] // CH, run, 0)
        do_o[...] = nt(da_o[...], wo[...]).astype(BF16)


def ffn_back(dz, dr2, gp, wd, wi, xh1, rs1, n1g, wo):
    rows, width = dz.shape
    ff = gp.shape[1]
    fb = 512
    whole = lambda shape: pl.BlockSpec(shape, lambda i: (0,) * len(shape))
    return pl.pallas_call(
        ffn_back_kernel,
        grid=(ff // fb,),
        in_specs=[
            whole((rows, width)), whole((rows, width)),
            pl.BlockSpec((rows, fb), lambda i: (0, i)),
            pl.BlockSpec((fb, width), lambda i: (i, 0)),
            pl.BlockSpec((width, fb), lambda i: (0, i)),
            whole((rows, width)), whole((rows, 1)), whole((1, width)), whole((width, width)),
        ],
        out_specs=[
            pl.BlockSpec((rows, fb), lambda i: (0, i)),
            pl.BlockSpec((1, fb), lambda i: (0, i)),
            whole((rows, width)), whole((rows, width)), whole((rows, width)), whole((8, width)),
        ],
        out_shape=[
            jax.ShapeDtypeStruct((rows, ff), BF16),
            jax.ShapeDtypeStruct((1, ff), F32),
            jax.ShapeDtypeStruct((rows, width), F32),
            jax.ShapeDtypeStruct((rows, width), BF16),
            jax.ShapeDtypeStruct((rows, width), BF16),
            jax.ShapeDtypeStruct((8, width), F32),
        ],
        scratch_shapes=[pltpu.VMEM((rows, width), F32)],
        compiler_params=pltpu.CompilerParams(
            dimension_semantics=("arbitrary",), vmem_limit_bytes=VMEM_LIMIT
        ),
        name="ffn_back",
    )(dz, dr2, gp, wd, wi, xh1, rs1, n1g.reshape(1, -1), wo)


def attention_back_kernel(
    qlen, plen, q, k, v, o, do, lse,
    dq_o, dk_o, dv_o, small_o,
    kmask, lse_p, lse_q, delta_p, delta_q,
):
    step = pl.program_id(0)
    width = q.shape[1]
    lane = lax.broadcasted_iota(jnp.int32, (1, 128), 1)
    low = (lane < 64).astype(F32)
    lanes = (low, 1.0 - low)
    ones = ((lane == 64).astype(F32), (lane == 0).astype(F32))
    q_gain = [(t * 0.125).astype(BF16) for t in lanes]
    keep = [t.astype(BF16) for t in lanes]
    one = [t.astype(BF16) for t in ones]

    q_valid = lax.broadcasted_iota(jnp.int32, (QRY_LEN, 128), 0) < qlen[step]
    p_valid = lax.broadcasted_iota(jnp.int32, (PASS_LEN, 128), 0) < plen[step]
    for side in range(2):
        kmask[side, :QRY_LEN, :] = jnp.where(q_valid, 0.0, NEG * ones[side]).astype(BF16)
        kmask[side, QRY_LEN:, :] = jnp.where(p_valid, 0.0, NEG * ones[side]).astype(BF16)

    q_rows, p_rows = pl.ds(0, QRY_LEN), pl.ds(QRY_LEN, PASS_LEN)
    head_of = (
        lax.broadcasted_iota(jnp.int32, (16, width), 1) // 64
        == lax.broadcasted_iota(jnp.int32, (16, width), 0)
    ).astype(F32).astype(BF16)
    for rows, lse_t, delta_t in ((q_rows, lse_q, delta_q), (p_rows, lse_p, delta_p)):
        lse_t[...] = jnp.transpose(lse[rows, :])
        prod = do[rows, :].astype(F32) * o[rows, :].astype(F32)
        hi = prod.astype(BF16)
        lo = (prod - hi.astype(F32)).astype(BF16)
        delta_t[...] = nt(head_of, hi) + nt(head_of, lo)

    def attend(pair, carry):
        cols = pl.ds(pl.multiple_of(pair * 128, 128), 128)
        for rows, lse_t, delta_t in ((q_rows, lse_q, delta_q), (p_rows, lse_p, delta_p)):
            qp, kp, vp, dop = q[rows, cols], k[rows, cols], v[rows, cols], do[rows, cols]
            dq = dk = dv = None
            for side in range(2):
                head = pl.ds(2 * pair + side, 1)
                qm = qp * q_gain[side]
                km = kp * q_gain[side]
                dm = dop * keep[side]
                ke = kp * keep[side] + kmask[side, rows, :]
                st = nt(ke, qm + one[side])
                pt = jnp.exp(st - lse_t[head, :])
                dpt = nt(vp, dm)
                dst = (pt * (dpt - delta_t[head, :])).astype(BF16)
                dv_h = nn(pt.astype(BF16), dm)
                dk_h = nn(dst, qm)
                dq_h = tn(dst, km)
                dq = dq_h if dq is None else dq + dq_h
                dk = dk_h if dk is None else dk + dk_h
                dv = dv_h if dv is None else dv + dv_h
            dq_o[rows, cols] = dq.astype(BF16)
            dk_o[rows, cols] = dk.astype(BF16)
            dv_o[rows, cols] = dv.astype(BF16)
        return carry

    lax.fori_loop(0, HEADS // 2, attend, 0)

    @pl.when(step == 0)
    def _():
        small_o[...] = jnp.zeros_like(small_o)

    small_o[0:1, :] += jnp.sum(dq_o[...].astype(F32), axis=0, keepdims=True)
    small_o[1:2, :] += jnp.sum(dv_o[...].astype(F32), axis=0, keepdims=True)


def attention_back(qlen, plen, q, k, v, o, do, lse):
    seqs = qlen.shape[0]
    rows, width = q.shape
    whole = lambda shape: pl.BlockSpec(shape, lambda i: (0,) * len(shape))
    smem = pl.BlockSpec(memory_space=pltpu.SMEM)
    block = pl.BlockSpec((PAIR_LEN, width), lambda i: (i, 0))
    return pl.pallas_call(
        attention_back_kernel,
        grid=(seqs,),
        in_specs=[smem, smem] + [block] * 5 + [pl.BlockSpec((PAIR_LEN, 128), lambda i: (i, 0))],
        out_specs=[block, block, block, whole((8, width))],
        out_shape=[jax.ShapeDtypeStruct((rows, width), BF16)] * 3 + [jax.ShapeDtypeStruct((8, width), F32)],
        scratch_shapes=[
            pltpu.VMEM((2, PAIR_LEN, 128), BF16),
            pltpu.VMEM((128, PASS_LEN), F32),
            pltpu.VMEM((128, QRY_LEN), F32),
            pltpu.VMEM((16, PASS_LEN), F32),
            pltpu.VMEM((16, QRY_LEN), F32),
        ],
        compiler_params=pltpu.CompilerParams(
            dimension_semantics=("arbitrary",), vmem_limit_bytes=VMEM_LIMIT
        ),
        name="attention_back",
    )(qlen, plen, q, k, v, o, do, lse)


def input_grad_kernel(dr1, dq, dk, dv, wq, wk, wv, gq_o, gp_o):
    grad = dr1[...] + nt(dq[...], wq[...]) + nt(dk[...], wk[...]) + nt(dv[...], wv[...])
    gq_o[...] = grad[:QRY_LEN]
    gp_o[...] = grad[QRY_LEN:]


def input_grad(dr1, dq, dk, dv, wq, wk, wv):
    rows, width = dq.shape
    seqs = rows // PAIR_LEN
    block = pl.BlockSpec((PAIR_LEN, width), lambda i: (i, 0))
    weight = pl.BlockSpec((width, width), lambda i: (0, 0))
    return pl.pallas_call(
        input_grad_kernel,
        grid=(seqs,),
        in_specs=[block] * 4 + [weight] * 3,
        out_specs=[
            pl.BlockSpec((QRY_LEN, width), lambda i: (i, 0)),
            pl.BlockSpec((PASS_LEN, width), lambda i: (i, 0)),
        ],
        out_shape=[
            jax.ShapeDtypeStruct((seqs * QRY_LEN, width), F32),
            jax.ShapeDtypeStruct((seqs * PASS_LEN, width), F32),
        ],
        compiler_params=pltpu.CompilerParams(
            dimension_semantics=("arbitrary",), vmem_limit_bytes=VMEM_LIMIT
        ),
        name="input_grad",
    )(dr1, dq, dk, dv, wq, wk, wv)


def swap_with(value, mask, device_count):
    return lax.ppermute(value, AXES, [(i, i ^ mask) for i in range(device_count)])


def bit_orders(device_count):
    top = device_count // 2
    rest = []
    mask = 4
    while mask < top:
        rest.append(mask)
        mask *= 2
    return ([1, top, 2] + rest, [1, 2, top] + rest)


def gather_relative(value, device_count):
    top = device_count // 2
    groups = [[1], [2, top]]
    rest = []
    mask = 4
    while mask < top:
        rest.append(mask)
        mask *= 2
    while rest:
        groups.append(rest[:2])
        rest = rest[2:]
    relative = [0]
    for group in groups:
        combos = [0]
        for mask in group:
            combos = combos + [c ^ mask for c in combos]
        got = [value] + [swap_with(value, c, device_count) for c in combos[1:]]
        value = jnp.concatenate(got, axis=0)
        relative = [c ^ r for c in combos for r in relative]
    return value, relative


def scatter_sum(part, masks, my_index, device_count):
    for mask in masks:
        half = part.shape[0] // 2
        bit = ((my_index & mask) != 0).astype(jnp.int32)
        send = lax.dynamic_slice_in_dim(part, (1 - bit) * half, half, 0)
        keep = lax.dynamic_slice_in_dim(part, bit * half, half, 0)
        got = swap_with(send, mask, device_count)
        part = (keep.astype(jnp.float32) + got.astype(jnp.float32)).astype(part.dtype)
    return part


def gather_back(part, masks, my_index, device_count):
    for mask in reversed(masks):
        bit = (my_index & mask) != 0
        got = swap_with(part, mask, device_count)
        part = jnp.where(
            bit, jnp.concatenate([got, part], 0), jnp.concatenate([part, got], 0)
        )
    return part


def sum_all(part, masks, my_index, device_count):
    part = scatter_sum(part, masks, my_index, device_count)
    return gather_back(part, masks, my_index, device_count)


def body(
    query_tokens,
    passage_tokens,
    query_lengths,
    passage_lengths,
    positives,
    w_query,
    b_query,
    w_key,
    w_value,
    b_value,
    w_out,
    b_out,
    norm1_gain,
    norm1_bias,
    w_in,
    b_in,
    w_down,
    b_down,
    norm2_gain,
    norm2_bias,
    query_out_grad,
    passage_out_grad,
):
    seqs = query_lengths.shape[0]
    width = query_tokens.shape[1]
    device_count = lax.axis_size(AXES)
    my_index = lax.axis_index(AXES)
    params = dict(
        w_query=w_query, b_query=b_query, w_key=w_key, w_value=w_value, b_value=b_value, w_out=w_out,
        b_out=b_out, norm1_gain=norm1_gain, norm1_bias=norm1_bias, w_in=w_in, b_in=b_in, w_down=w_down,
        b_down=b_down, norm2_gain=norm2_gain, norm2_bias=norm2_bias,
    )
    (
        query_out, passage_out, q, k, v, o, lse, xhat1, rstd1, h1b, g, gelu_slope, xhat2, rstd2, unit, mean,
    ) = forward(query_tokens, passage_tokens, query_lengths, passage_lengths, params)
    x_rows = jnp.concatenate(
        [query_tokens.reshape(seqs, QRY_LEN, width), passage_tokens.reshape(seqs, PASS_LEN, width)], 1
    ).reshape(seqs * PAIR_LEN, width)

    units, relative = gather_relative(unit, device_count)
    owner = jnp.array(relative, jnp.int32) ^ my_index
    ids = (owner[:, None] * seqs + jnp.arange(seqs, dtype=jnp.int32)[None, :]).reshape(-1)
    ids = jnp.repeat(ids, 2)
    target = positives[ids][:, None]
    dz, dr2, small2, loss_sum = loss_and_second_norm(
        units, target, ids[None, :], mean, query_lengths, passage_lengths, query_out_grad, passage_out_grad,
        xhat2, rstd2, norm2_gain,
    )
    loss = loss_sum[0, 0] / (seqs * device_count)
    grad_w_down = tn(g, dz).astype(BF16)
    du, grad_b_in, dr1, da, do, small1 = ffn_back(dz, dr2, gelu_slope, w_down, w_in, xhat1, rstd1, norm1_gain, w_out)
    grad_w_in = tn(h1b, du).astype(BF16)
    dq, dk, dv, small0 = attention_back(query_lengths, passage_lengths, q, k, v, o, do, lse)
    grad_w_out = tn(o, da).astype(BF16)
    grad_w_query = tn(x_rows, dq).astype(BF16)
    grad_w_key = tn(x_rows, dk).astype(BF16)
    grad_w_value = tn(x_rows, dv).astype(BF16)
    query_input_grad, passage_input_grad = input_grad(dr1, dq, dk, dv, w_query, w_key, w_value)

    order_x, order_y = bit_orders(device_count)

    def reduce_pair(first, second):
        return (
            sum_all(first, order_x, my_index, device_count).astype(F32),
            sum_all(second, order_y, my_index, device_count).astype(F32),
        )

    down_half = grad_w_down.shape[0] // 2
    down_top, down_low = reduce_pair(grad_w_down[:down_half], grad_w_down[down_half:])
    in_half = grad_w_in.shape[1] // 2
    in_left, in_right = reduce_pair(grad_w_in[:, :in_half], grad_w_in[:, in_half:])
    proj_left, proj_right = reduce_pair(
        jnp.concatenate([grad_w_query, grad_w_key], 1), jnp.concatenate([grad_w_value, grad_w_out], 1)
    )
    packed = jnp.concatenate(
        [small0[:2], small1[:3], small2[:3], grad_b_in.reshape(-1, width)], 0
    )
    for mask in order_x:
        packed = packed + swap_with(packed, mask, device_count)
    return (
        query_out,
        passage_out,
        query_input_grad,
        passage_input_grad,
        loss,
        proj_left[:, :width],
        packed[0],
        proj_left[:, width:],
        proj_right[:, :width],
        packed[1],
        proj_right[:, width:],
        packed[4],
        packed[2],
        packed[3],
        jnp.concatenate([in_left, in_right], 1),
        packed[8:].reshape(-1),
        jnp.concatenate([down_top, down_low], 0),
        packed[7],
        packed[5],
        packed[6],
    )


def solution(mesh):
    placed = (
        P(("stream", "batch"), None),
        P(("stream", "batch"), None),
        P(("stream", "batch")),
        P(("stream", "batch")),
        P(),
        P(),
        P(),
        P(),
        P(),
        P(),
        P(),
        P(),
        P(),
        P(),
        P(),
        P(),
        P(),
        P(),
        P(),
        P(),
        P(("stream", "batch"), None),
        P(("stream", "batch"), None),
    )
    return jax.shard_map(
        body,
        mesh=mesh,
        in_specs=placed,
        out_specs=(
            P(("stream", "batch"), None),
            P(("stream", "batch"), None),
            P(("stream", "batch"), None),
            P(("stream", "batch"), None),
            P(),
            P(),
            P(),
            P(),
            P(),
            P(),
            P(),
            P(),
            P(),
            P(),
            P(),
            P(),
            P(),
            P(),
            P(),
            P(),
        ),
        check_vma=False,
    )
```

```python
import functools

import jax
import jax.numpy as jnp
from jax import lax
from jax.experimental import pallas as pl
from jax.experimental.pallas import tpu as pltpu
from jax.sharding import PartitionSpec as P

HEADS = 12
QRY_LEN = 64
PASS_LEN = 512
PAIR_LEN = QRY_LEN + PASS_LEN
LOGIT_SCALE = 0.01
EPS = 1e-06
NEG = -1e30
F32 = jnp.float32
BF16 = jnp.bfloat16
AXES = ("stream", "batch")
MIB = 1024 * 1024
VMEM_LIMIT = 60 * MIB


def kernel_cost(us):
    return pl.CostEstimate(flops=us * 1_000_000_000, bytes_accessed=1_000_000, transcendentals=0)


def nn(a, b):
    return lax.dot_general(a, b, (((1,), (0,)), ((), ())), preferred_element_type=F32)


def nt(a, b):
    return lax.dot_general(a, b, (((1,), (1,)), ((), ())), preferred_element_type=F32)


def tn(a, b):
    return lax.dot_general(a, b, (((0,), (0,)), ((), ())), preferred_element_type=F32)


def gelu_parts(u):
    a = jnp.abs(u)
    t = 1.0 / (1.0 + (0.3275911 * 0.7071067811865476) * a)
    bell = jnp.exp(-0.5 * (u * u))
    poly = t * (
        0.5 * 0.254829592
        + t * (0.5 * -0.284496736 + t * (0.5 * 1.421413741 + t * (0.5 * -1.453152027 + t * (0.5 * 1.061405429))))
    )
    tail = poly * bell
    cdf = jnp.where(u >= 0, 1.0 - tail, tail)
    return u * cdf, cdf + u * (bell * 0.3989422804014327)


def forward_kernel(
    qlen, plen, xq, xp, wq_h, wk_h, wv_h, wo_h, wi_h, wd_h, bq, bv, bo, n1g, n1b, bi, bd, n2g, n2b,
    yq, yp, q_o, k_o, v_o, o_o, lse_o, xh1_o, rs1_o, h1b_o, g_o, gp_o, xh2_o, rs2_o, unit_o, mean_o,
    xs, wq, wk, wv, wo, wi, wd, acc, h1, kmask, sems,
):
    step = pl.program_id(0)
    width = xs.shape[1]
    copies = [
        pltpu.make_async_copy(src, dst, sems.at[n])
        for n, (src, dst) in enumerate(
            ((wq_h, wq), (wk_h, wk), (wv_h, wv), (wo_h, wo), (wi_h, wi), (wd_h, wd))
        )
    ]

    @pl.when(step == 0)
    def _():
        for c in copies:
            c.start()
        lse_o[...] = jnp.zeros_like(lse_o)

    def ready(n):
        @pl.when(step == 0)
        def _():
            copies[n].wait()

    xs[:QRY_LEN, :] = xq[...]
    xs[QRY_LEN:, :] = xp[...]
    ready(0)
    q_o[...] = (nn(xs[...], wq[...]) + bq[...]).astype(BF16)
    ready(1)
    k_o[...] = nn(xs[...], wk[...]).astype(BF16)
    ready(2)
    v_o[...] = (nn(xs[...], wv[...]) + bv[...]).astype(BF16)

    lane = lax.broadcasted_iota(jnp.int32, (1, 128), 1)
    low = (lane < 64).astype(F32)
    lanes = (low, 1.0 - low)
    ones = ((lane == 64).astype(F32), (lane == 0).astype(F32))
    q_gain = [(v * 0.125).astype(BF16) for v in lanes]
    keep = [v.astype(BF16) for v in lanes]
    one = [v.astype(BF16) for v in ones]

    q_valid = lax.broadcasted_iota(jnp.int32, (QRY_LEN, 128), 0) < qlen[step]
    p_valid = lax.broadcasted_iota(jnp.int32, (PASS_LEN, 128), 0) < plen[step]
    for side in range(2):
        kmask[side, :QRY_LEN, :] = jnp.where(q_valid, 0.0, NEG * ones[side]).astype(BF16)
        kmask[side, QRY_LEN:, :] = jnp.where(p_valid, 0.0, NEG * ones[side]).astype(BF16)

    def attend(pair, carry):
        cols = pl.ds(pl.multiple_of(pair * 128, 128), 128)
        for rows in (pl.ds(0, QRY_LEN), pl.ds(QRY_LEN, PASS_LEN)):
            qp, kp, vp = q_o[rows, cols], k_o[rows, cols], v_o[rows, cols]
            mixed = []
            for side in range(2):
                qe = qp * q_gain[side] + one[side]
                ke = kp * keep[side] + kmask[side, rows, :]
                ve = vp * keep[side] + one[side]
                s = nt(qe, ke)
                top = jnp.max(s, axis=1, keepdims=True)
                p = jnp.exp(s - top).astype(BF16)
                oe = nn(p, ve)
                total = oe[:, 64:65] if side == 0 else oe[:, 0:1]
                mixed.append(oe * (1.0 / total))
                lse = top + jnp.log(total)
                head = 2 * pair + side
                lse_o[rows, :] = jnp.where(lane == head, lse, lse_o[rows, :])
            o_o[rows, cols] = jnp.where(lane < 64, mixed[0], mixed[1]).astype(BF16)
        return carry

    lax.fori_loop(0, HEADS // 2, attend, 0)

    ready(3)
    acc[...] = nn(o_o[...], wo[...])

    def norm(value):
        mean = jnp.mean(value, axis=-1, keepdims=True)
        c = value - mean
        rstd = lax.rsqrt(jnp.mean(c * c, axis=-1, keepdims=True) + EPS)
        return c * rstd, rstd

    CH = 64

    def first_norm(n, carry):
        rows = pl.ds(pl.multiple_of(n * CH, CH), CH)
        xhat, rstd = norm(xs[rows, :].astype(F32) + acc[rows, :] + bo[...])
        hid = xhat * n1g[...] + n1b[...]
        xh1_o[rows, :] = xhat.astype(BF16)
        rs1_o[rows, :] = rstd
        h1[rows, :] = hid
        h1b_o[rows, :] = hid.astype(BF16)
        return carry

    lax.fori_loop(0, PAIR_LEN // CH, first_norm, 0)

    FB = 512
    ready(4)
    ready(5)

    def ffn(n, carry):
        cols = pl.ds(pl.multiple_of(n * FB, FB), FB)
        u = nn(h1b_o[...], wi[:, cols]) + bi[cols]
        g, gp = gelu_parts(u)
        gb = g.astype(BF16)
        g_o[:, cols] = gb
        gp_o[:, cols] = gp.astype(BF16)
        h1[...] += nn(gb, wd[cols, :])
        return carry

    lax.fori_loop(0, wi.shape[1] // FB, ffn, 0)

    def second_norm(row0, rows_n, out, valid_n):
        def run(n, total):
            at = pl.multiple_of(n * CH, CH)
            rows = pl.ds(row0 + at, CH)
            xhat, rstd = norm(h1[rows, :] + bd[...])
            y = xhat * n2g[...] + n2b[...]
            xh2_o[rows, :] = xhat.astype(BF16)
            rs2_o[rows, :] = rstd
            out[pl.ds(at, CH), :] = y.astype(BF16)
            live = (lax.broadcasted_iota(jnp.int32, (CH, 1), 0) + at) < valid_n
            return total + jnp.sum(jnp.where(live, y, 0.0), axis=0, keepdims=True)

        total = lax.fori_loop(0, rows_n // CH, run, jnp.zeros((1, width), F32))
        return total / valid_n.astype(F32)

    for kind, mean in enumerate(
        (
            second_norm(0, QRY_LEN, yq, qlen[step]),
            second_norm(QRY_LEN, PASS_LEN, yp, plen[step]),
        )
    ):
        at = pl.ds(2 * step + kind, 1)
        mean_o[at, :] = mean
        unit = mean * lax.rsqrt(jnp.sum(mean * mean, axis=-1, keepdims=True) + EPS)
        unit_o[at, :] = unit


def forward(xq, xp, qlen, plen, p):
    seqs = qlen.shape[0]
    width = xq.shape[1]
    ff = p["w_in"].shape[1]
    rows = seqs * PAIR_LEN
    whole = lambda shape: pl.BlockSpec(shape, lambda i: (0,) * len(shape))
    smem = pl.BlockSpec(memory_space=pltpu.SMEM)
    hbm = pl.BlockSpec(memory_space=pl.ANY)
    row_block = lambda n, w: pl.BlockSpec((n, w), lambda i: (i, 0))
    outs = [
        ((seqs * QRY_LEN, width), BF16, row_block(QRY_LEN, width)),
        ((seqs * PASS_LEN, width), BF16, row_block(PASS_LEN, width)),
        ((rows, width), BF16, row_block(PAIR_LEN, width)),
        ((rows, width), BF16, row_block(PAIR_LEN, width)),
        ((rows, width), BF16, row_block(PAIR_LEN, width)),
        ((rows, width), BF16, row_block(PAIR_LEN, width)),
        ((rows, 128), F32, row_block(PAIR_LEN, 128)),
        ((rows, width), BF16, row_block(PAIR_LEN, width)),
        ((rows, 1), F32, row_block(PAIR_LEN, 1)),
        ((rows, width), BF16, row_block(PAIR_LEN, width)),
        ((rows, ff), BF16, row_block(PAIR_LEN, ff)),
        ((rows, ff), BF16, row_block(PAIR_LEN, ff)),
        ((rows, width), BF16, row_block(PAIR_LEN, width)),
        ((rows, 1), F32, row_block(PAIR_LEN, 1)),
        ((2 * seqs, width), F32, whole((2 * seqs, width))),
        ((2 * seqs, width), F32, whole((2 * seqs, width))),
    ]
    return pl.pallas_call(
        forward_kernel,
        grid=(seqs,),
        in_specs=[smem, smem, row_block(QRY_LEN, width), row_block(PASS_LEN, width)]
        + [hbm] * 6
        + [whole((width,))] * 5
        + [whole((ff,))]
        + [whole((width,))] * 3,
        out_specs=[o[2] for o in outs],
        out_shape=[jax.ShapeDtypeStruct(o[0], o[1]) for o in outs],
        scratch_shapes=[
            pltpu.VMEM((PAIR_LEN, width), BF16),
            pltpu.VMEM((width, width), BF16),
            pltpu.VMEM((width, width), BF16),
            pltpu.VMEM((width, width), BF16),
            pltpu.VMEM((width, width), BF16),
            pltpu.VMEM((width, ff), BF16),
            pltpu.VMEM((ff, width), BF16),
            pltpu.VMEM((PAIR_LEN, width), F32),
            pltpu.VMEM((PAIR_LEN, width), F32),
            pltpu.VMEM((2, PAIR_LEN, 128), BF16),
            pltpu.SemaphoreType.DMA((6,)),
        ],
        compiler_params=pltpu.CompilerParams(
            dimension_semantics=("arbitrary",), vmem_limit_bytes=VMEM_LIMIT
        ),
        cost_estimate=kernel_cost(60),
        name="forward_layer",
    )(
        qlen, plen, xq, xp, p["w_query"], p["w_key"], p["w_value"], p["w_out"], p["w_in"], p["w_down"],
        p["b_query"], p["b_value"], p["b_out"], p["norm1_gain"],
        p["norm1_bias"], p["b_in"], p["b_down"], p["norm2_gain"],
        p["norm2_bias"],
    )


def loss_kernel(
    qlen, plen, units_0, units_1, units_2, units_3, target, column_id, mean, ogq, ogp, xh2, rs2, n2g,
    dz_o, dr2_o, small_o, loss_o,
    de,
):
    step = pl.program_id(0)
    seqs = pl.num_programs(0)
    width = xh2.shape[1]
    mine = mean.shape[0]

    @pl.when(step == 0)
    def _():
        u = jnp.concatenate([t[...] for t in (units_0, units_1, units_2, units_3)], 0).astype(BF16)
        n = u.shape[0]
        row = lax.broadcasted_iota(jnp.int32, (n, n), 0)
        col = lax.broadcasted_iota(jnp.int32, (n, n), 1)
        pairs = ((row & 1) == 0) & ((col & 1) == 1)
        logits = jnp.where(pairs, nt(u, u) / LOGIT_SCALE, NEG)
        top = jnp.max(logits, axis=1, keepdims=True)
        lse = top + jnp.log(jnp.sum(jnp.exp(logits - top), axis=1, keepdims=True))
        hit = pairs & (target[...] == column_id[...])
        chosen = jnp.sum(jnp.where(hit, logits, 0.0), axis=1, keepdims=True)
        is_query = (lax.broadcasted_iota(jnp.int32, (n, 1), 0) & 1) == 0
        loss_o[...] = jnp.sum(jnp.where(is_query, lse - chosen, 0.0), axis=0, keepdims=True)
        dc = jnp.where(pairs, (jnp.exp(logits - lse) - hit.astype(F32)) / LOGIT_SCALE, 0.0)
        both = (dc + jnp.transpose(dc)).astype(BF16)
        dn = nn(both[:16], u)[:mine]
        e = mean[...]
        square = jnp.sum(e * e, axis=-1, keepdims=True) + EPS
        grad = (dn - e * (jnp.sum(e * dn, axis=-1, keepdims=True) / square)) * lax.rsqrt(square)
        de[...] = jnp.zeros_like(de)
        de[:mine, :] = grad
        small_o[...] = jnp.zeros_like(small_o)

    CH = 64

    def back(row0, rows_n, grads, valid_n, kind):
        shift = de[pl.ds(2 * step + kind, 1), :] / valid_n.astype(F32)

        def run(n, carry):
            at = pl.multiple_of(n * CH, CH)
            rows = pl.ds(row0 + at, CH)
            live = (lax.broadcasted_iota(jnp.int32, (CH, 1), 0) + at) < valid_n
            dy = grads[pl.ds(at, CH), :].astype(F32) + jnp.where(live, shift, 0.0)
            xhat = xh2[rows, :].astype(F32)
            dyg = dy * n2g[...]
            m1 = jnp.mean(dyg, axis=-1, keepdims=True)
            m2 = jnp.mean(dyg * xhat, axis=-1, keepdims=True)
            dr = rs2[rows, :] * (dyg - m1 - xhat * m2)
            db = dr.astype(BF16)
            dr2_o[rows, :] = dr
            dz_o[rows, :] = db
            small_o[0:1, :] += jnp.sum(dy * xhat, axis=0, keepdims=True)
            small_o[1:2, :] += jnp.sum(dy, axis=0, keepdims=True)
            small_o[2:3, :] += jnp.sum(db.astype(F32), axis=0, keepdims=True)
            return carry

        lax.fori_loop(0, rows_n // CH, run, 0)

    back(0, QRY_LEN, ogq, qlen[step], 0)
    back(QRY_LEN, PASS_LEN, ogp, plen[step], 1)


def loss_and_second_norm(units, target, column_id, mean, qlen, plen, ogq, ogp, xh2, rs2, n2g):
    seqs = qlen.shape[0]
    width = ogq.shape[1]
    rows = seqs * PAIR_LEN
    whole = lambda shape: pl.BlockSpec(shape, lambda i: (0,) * len(shape))
    smem = pl.BlockSpec(memory_space=pltpu.SMEM)
    row_block = lambda n, w: pl.BlockSpec((n, w), lambda i: (i, 0))
    return pl.pallas_call(
        loss_kernel,
        grid=(seqs,),
        in_specs=[
            smem, smem, *[whole(t.shape) for t in units], whole(target.shape), whole(column_id.shape), whole(mean.shape),
            row_block(QRY_LEN, width), row_block(PASS_LEN, width), row_block(PAIR_LEN, width),
            row_block(PAIR_LEN, 1), whole((width,)),
        ],
        out_specs=[row_block(PAIR_LEN, width), row_block(PAIR_LEN, width), whole((8, width)), whole((1, 1))],
        out_shape=[
            jax.ShapeDtypeStruct((rows, width), BF16),
            jax.ShapeDtypeStruct((rows, width), F32),
            jax.ShapeDtypeStruct((8, width), F32),
            jax.ShapeDtypeStruct((1, 1), F32),
        ],
        scratch_shapes=[pltpu.VMEM((8, width), F32)],
        compiler_params=pltpu.CompilerParams(
            dimension_semantics=("arbitrary",), vmem_limit_bytes=16 * MIB
        ),
        cost_estimate=kernel_cost(8),
        name="loss_norm_back",
    )(qlen, plen, *units, target, column_id, mean, ogq, ogp, xh2, rs2, n2g)


def ffn_back_kernel(dz, dr2, gp, wd, wi, du_o, bi_o, acc):
    step = pl.program_id(0)
    du = (nt(dz[...], wd[...]) * gp[...].astype(F32)).astype(BF16)
    du_o[...] = du
    bi_o[...] = jnp.sum(du.astype(F32), axis=0, keepdims=True)
    part = nt(du, wi[...])

    @pl.when(step == 0)
    def _():
        acc[...] = dr2[...] + part

    @pl.when(step > 0)
    def _():
        acc[...] += part


def ffn_back(dz, dr2, gp, wd, wi, part, parts):
    rows, width = dz.shape
    fb = 512
    steps = gp.shape[1] // fb // parts
    skip = part * steps
    whole = lambda shape: pl.BlockSpec(shape, lambda i: (0,) * len(shape))
    return pl.pallas_call(
        ffn_back_kernel,
        grid=(steps,),
        in_specs=[
            whole((rows, width)), whole((rows, width)),
            pl.BlockSpec((rows, fb), lambda i: (0, i + skip)),
            pl.BlockSpec((fb, width), lambda i: (i + skip, 0)),
            pl.BlockSpec((width, fb), lambda i: (0, i + skip)),
        ],
        out_specs=[
            pl.BlockSpec((rows, fb), lambda i: (0, i)),
            pl.BlockSpec((1, fb), lambda i: (0, i)),
            whole((rows, width)),
        ],
        out_shape=[
            jax.ShapeDtypeStruct((rows, steps * fb), BF16),
            jax.ShapeDtypeStruct((1, steps * fb), F32),
            jax.ShapeDtypeStruct((rows, width), F32),
        ],
        compiler_params=pltpu.CompilerParams(
            dimension_semantics=("arbitrary",), vmem_limit_bytes=28 * MIB
        ),
        cost_estimate=kernel_cost(9),
        name="ffn_back",
    )(dz, dr2, gp, wd, wi)


def first_norm_back_kernel(dh_ref, xh1, rs1, n1g, wo, dr1_o, da_o, do_o, small_o):
    CH = 64

    @pl.when(pl.program_id(0) == 0)
    def _():
        small_o[...] = jnp.zeros_like(small_o)

    def run(n, carry):
        rows = pl.ds(pl.multiple_of(n * CH, CH), CH)
        dh = dh_ref[rows, :]
        xhat = xh1[rows, :].astype(F32)
        dyg = dh * n1g[...]
        m1 = jnp.mean(dyg, axis=-1, keepdims=True)
        m2 = jnp.mean(dyg * xhat, axis=-1, keepdims=True)
        dr = rs1[rows, :] * (dyg - m1 - xhat * m2)
        db = dr.astype(BF16)
        dr1_o[rows, :] = dr
        da_o[rows, :] = db
        small_o[0:1, :] += jnp.sum(dh * xhat, axis=0, keepdims=True)
        small_o[1:2, :] += jnp.sum(dh, axis=0, keepdims=True)
        small_o[2:3, :] += jnp.sum(db.astype(F32), axis=0, keepdims=True)
        return carry

    lax.fori_loop(0, dh_ref.shape[0] // CH, run, 0)
    do_o[...] = nt(da_o[...], wo[...]).astype(BF16)


def first_norm_back(dh, xh1, rs1, n1g, wo):
    rows, width = dh.shape
    step = PAIR_LEN
    whole = lambda shape: pl.BlockSpec(shape, lambda i: (0,) * len(shape))
    block = lambda w: pl.BlockSpec((step, w), lambda i: (i, 0))
    return pl.pallas_call(
        first_norm_back_kernel,
        grid=(rows // step,),
        in_specs=[block(width), block(width), block(1), whole((width,)), whole((width, width))],
        out_specs=[block(width), block(width), block(width), whole((8, width))],
        out_shape=[
            jax.ShapeDtypeStruct((rows, width), F32),
            jax.ShapeDtypeStruct((rows, width), BF16),
            jax.ShapeDtypeStruct((rows, width), BF16),
            jax.ShapeDtypeStruct((8, width), F32),
        ],
        compiler_params=pltpu.CompilerParams(
            dimension_semantics=("arbitrary",), vmem_limit_bytes=24 * MIB
        ),
        cost_estimate=kernel_cost(8),
        name="first_norm_back",
    )(dh, xh1, rs1, n1g, wo)


def attention_back_kernel(
    qlen, plen, q, k, v, o, do, lse,
    dq_o, dk_o, dv_o, small_o,
    kmask, lse_p, lse_q, delta_p, delta_q,
    *, first_head,
):
    step = pl.program_id(0)
    width = q.shape[1]
    pairs = width // 128
    lane = lax.broadcasted_iota(jnp.int32, (1, 128), 1)
    low = (lane < 64).astype(F32)
    lanes = (low, 1.0 - low)
    ones = ((lane == 64).astype(F32), (lane == 0).astype(F32))
    q_gain = [(t * 0.125).astype(BF16) for t in lanes]
    keep = [t.astype(BF16) for t in lanes]
    one = [t.astype(BF16) for t in ones]

    q_valid = lax.broadcasted_iota(jnp.int32, (QRY_LEN, 128), 0) < qlen[step]
    p_valid = lax.broadcasted_iota(jnp.int32, (PASS_LEN, 128), 0) < plen[step]
    for side in range(2):
        kmask[side, :QRY_LEN, :] = jnp.where(q_valid, 0.0, NEG * ones[side]).astype(BF16)
        kmask[side, QRY_LEN:, :] = jnp.where(p_valid, 0.0, NEG * ones[side]).astype(BF16)

    q_rows, p_rows = pl.ds(0, QRY_LEN), pl.ds(QRY_LEN, PASS_LEN)
    head_of = (
        lax.broadcasted_iota(jnp.int32, (16, width), 1) // 64
        == lax.broadcasted_iota(jnp.int32, (16, width), 0)
    ).astype(F32).astype(BF16)
    for rows, lse_t, delta_t in ((q_rows, lse_q, delta_q), (p_rows, lse_p, delta_p)):
        lse_t[...] = jnp.transpose(lse[rows, :])
        prod = do[rows, :].astype(F32) * o[rows, :].astype(F32)
        hi = prod.astype(BF16)
        lo = (prod - hi.astype(F32)).astype(BF16)
        delta_t[...] = nt(head_of, hi) + nt(head_of, lo)

    def attend(pair, carry):
        cols = pl.ds(pl.multiple_of(pair * 128, 128), 128)
        for rows, lse_t, delta_t in ((q_rows, lse_q, delta_q), (p_rows, lse_p, delta_p)):
            qp, kp, vp, dop = q[rows, cols], k[rows, cols], v[rows, cols], do[rows, cols]
            dq = dk = dv = None
            for side in range(2):
                head = pl.ds(2 * pair + side, 1)
                qm = qp * q_gain[side]
                km = kp * q_gain[side]
                dm = dop * keep[side]
                ke = kp * keep[side] + kmask[side, rows, :]
                st = nt(ke, qm + one[side])
                pt = jnp.exp(st - lse_t[pl.ds(first_head + 2 * pair + side, 1), :])
                dpt = nt(vp, dm)
                dst = (pt * (dpt - delta_t[head, :])).astype(BF16)
                dv_h = nn(pt.astype(BF16), dm)
                dk_h = nn(dst, qm)
                dq_h = tn(dst, km)
                dq = dq_h if dq is None else dq + dq_h
                dk = dk_h if dk is None else dk + dk_h
                dv = dv_h if dv is None else dv + dv_h
            dq_o[rows, cols] = dq.astype(BF16)
            dk_o[rows, cols] = dk.astype(BF16)
            dv_o[rows, cols] = dv.astype(BF16)
        return carry

    lax.fori_loop(0, pairs, attend, 0)

    @pl.when(step == 0)
    def _():
        small_o[...] = jnp.zeros_like(small_o)

    small_o[0:1, :] += jnp.sum(dq_o[...].astype(F32), axis=0, keepdims=True)
    small_o[1:2, :] += jnp.sum(dv_o[...].astype(F32), axis=0, keepdims=True)


def attention_back(qlen, plen, q, k, v, o, do, lse, part, parts):
    seqs = qlen.shape[0]
    rows = q.shape[0]
    width = q.shape[1] // parts
    whole = lambda shape: pl.BlockSpec(shape, lambda i: (0,) * len(shape))
    smem = pl.BlockSpec(memory_space=pltpu.SMEM)
    taken = pl.BlockSpec((PAIR_LEN, width), lambda i: (i, part))
    block = pl.BlockSpec((PAIR_LEN, width), lambda i: (i, 0))
    return pl.pallas_call(
        functools.partial(attention_back_kernel, first_head=part * width // 64),
        grid=(seqs,),
        in_specs=[smem, smem] + [taken] * 5 + [pl.BlockSpec((PAIR_LEN, 128), lambda i: (i, 0))],
        out_specs=[block, block, block, whole((8, width))],
        out_shape=[jax.ShapeDtypeStruct((rows, width), BF16)] * 3 + [jax.ShapeDtypeStruct((8, width), F32)],
        scratch_shapes=[
            pltpu.VMEM((2, PAIR_LEN, 128), BF16),
            pltpu.VMEM((128, PASS_LEN), F32),
            pltpu.VMEM((128, QRY_LEN), F32),
            pltpu.VMEM((16, PASS_LEN), F32),
            pltpu.VMEM((16, QRY_LEN), F32),
        ],
        compiler_params=pltpu.CompilerParams(
            dimension_semantics=("arbitrary",), vmem_limit_bytes=52 * MIB
        ),
        cost_estimate=kernel_cost(28 // parts),
        name="attention_back",
    )(qlen, plen, q, k, v, o, do, lse)


def input_grad_kernel(dr1, *refs):
    third = (len(refs) - 5) // 3
    wq, wk, wv, gq_o, gp_o = refs[-5:]
    grad = dr1[...]
    for n, w in enumerate((wq, wk, wv)):
        for part in range(third):
            d = refs[n * third + part]
            size = d.shape[1]
            grad += nt(d[...], w[:, part * size : (part + 1) * size])
    gq_o[...] = grad[:QRY_LEN]
    gp_o[...] = grad[QRY_LEN:]


def input_grad(dr1, dq, dk, dv, wq, wk, wv):
    rows, width = dr1.shape
    seqs = rows // PAIR_LEN
    block = lambda w: pl.BlockSpec((PAIR_LEN, w), lambda i: (i, 0))
    weight = pl.BlockSpec((width, width), lambda i: (0, 0))
    pieces = list(dq) + list(dk) + list(dv)
    return pl.pallas_call(
        input_grad_kernel,
        grid=(seqs,),
        in_specs=[block(width)] + [block(d.shape[1]) for d in pieces] + [weight] * 3,
        out_specs=[
            pl.BlockSpec((QRY_LEN, width), lambda i: (i, 0)),
            pl.BlockSpec((PASS_LEN, width), lambda i: (i, 0)),
        ],
        out_shape=[
            jax.ShapeDtypeStruct((seqs * QRY_LEN, width), F32),
            jax.ShapeDtypeStruct((seqs * PASS_LEN, width), F32),
        ],
        compiler_params=pltpu.CompilerParams(
            dimension_semantics=("arbitrary",), vmem_limit_bytes=26 * MIB
        ),
        cost_estimate=kernel_cost(10),
        name="input_grad",
    )(dr1, *pieces, wq, wk, wv)


def widen(out, cols, value):
    out[:, cols[0] : cols[1]] = value.astype(F32)


def place_down_kernel(bit, mine, other, out):
    half = pl.program_id(0)

    @pl.when(half == 0)
    def _():
        out[...] = mine[...].astype(F32)

    @pl.when(half == 1)
    def _():
        out[...] = other[...].astype(F32)


def place_down(bit, mine, other):
    rows, cols = mine.shape
    chunks = 4
    step = rows // chunks
    return pl.pallas_call(
        place_down_kernel,
        grid_spec=pltpu.PrefetchScalarGridSpec(
            num_scalar_prefetch=1,
            grid=(2, chunks),
            in_specs=[
                pl.BlockSpec((step, cols), lambda h, n, bit: (jnp.where(h == 0, n, chunks - 1), 0)),
                pl.BlockSpec((step, cols), lambda h, n, bit: (jnp.where(h == 1, n, 0), 0)),
            ],
            out_specs=pl.BlockSpec((step, cols), lambda h, n, bit: ((h ^ bit[0]) * chunks + n, 0)),
        ),
        out_shape=jax.ShapeDtypeStruct((2 * rows, cols), F32),
        compiler_params=pltpu.CompilerParams(
            dimension_semantics=("arbitrary", "arbitrary"), vmem_limit_bytes=16 * MIB
        ),
        cost_estimate=kernel_cost(5),
        name="place_down",
    )(bit, mine, other)


def place_columns(bit, sums, widths, write, name):
    rows = sums[0][0].shape[0]
    chunks = 4
    step = rows // chunks
    arrays = [a for pair in sums for a in pair]

    def kernel(bit, *refs):
        ins, outs = refs[: len(arrays)], refs[len(arrays) :]
        pairs = [(ins[2 * n], ins[2 * n + 1]) for n in range(len(sums))]

        @pl.when(bit[0] == 0)
        def _():
            write(outs, pairs)

        @pl.when(bit[0] == 1)
        def _():
            write(outs, [p[::-1] for p in pairs])

    return pl.pallas_call(
        kernel,
        grid_spec=pltpu.PrefetchScalarGridSpec(
            num_scalar_prefetch=1,
            grid=(chunks,),
            in_specs=[pl.BlockSpec((step, a.shape[1]), lambda n, bit: (n, 0)) for a in arrays],
            out_specs=[pl.BlockSpec((step, w), lambda n, bit: (n, 0)) for w in widths],
        ),
        out_shape=[jax.ShapeDtypeStruct((rows, w), F32) for w in widths],
        compiler_params=pltpu.CompilerParams(
            dimension_semantics=("arbitrary",), vmem_limit_bytes=20 * MIB
        ),
        cost_estimate=kernel_cost(5),
        name=name,
    )(bit, *arrays)


def write_in(outs, pairs):
    for n, half in enumerate(pairs[0]):
        at = 0
        for out in outs:
            size = out.shape[1] // 2
            widen(out, (n * size, (n + 1) * size), half[:, at : at + size])
            at += size


def write_proj(outs, pairs):
    size = outs[0].shape[1]
    low, high = pairs[0]
    widen(outs[0], (0, size), low[:, :size])
    widen(outs[1], (0, size // 2), low[:, size:])
    widen(outs[1], (size // 2, size), high[:, : size // 2])
    widen(outs[2], (0, size), high[:, size // 2 :])


IN_FLIGHT = 5


def swap_with(value, mask, device_count):
    return lax.ppermute(value, AXES, [(i, i ^ mask) for i in range(device_count)])


def far_groups(device_count):
    masks, mask = [], 4
    while mask < device_count // 2:
        masks.append(mask)
        mask *= 2
    return [masks[n : n + 2] for n in range(0, len(masks), 2)]


def combos_of(group):
    combos = [0]
    for mask in reversed(group):
        combos = combos + [c ^ mask for c in combos]
    return combos


def gather_relative(value, device_count):
    groups = [[1], [device_count // 2, 2]] + far_groups(device_count)
    relative = [0]
    for n, group in enumerate(groups):
        combos = combos_of(group)
        got = [value] + [swap_with(value, c, device_count) for c in combos[1:]]
        relative = [c ^ r for c in combos for r in relative]
        if n < len(groups) - 1 or len(got) < 4:
            value = jnp.concatenate(got, axis=0)
    if len(got) < 4:
        quarter = value.shape[0] // 4
        got = [value[n * quarter : (n + 1) * quarter] for n in range(4)]
    return got, relative


def whole_call(kernel, scalars, arrays, outs, name):
    spec = lambda shape: pl.BlockSpec(shape, lambda i, s: (0, 0))
    return pl.pallas_call(
        kernel,
        grid_spec=pltpu.PrefetchScalarGridSpec(
            num_scalar_prefetch=1,
            grid=(1,),
            in_specs=[spec(a.shape) for a in arrays],
            out_specs=[spec(o) for o in outs],
        ),
        out_shape=[jax.ShapeDtypeStruct(o, BF16) for o in outs],
        compiler_params=pltpu.CompilerParams(vmem_limit_bytes=24 * MIB),
        cost_estimate=kernel_cost(1),
        name=name,
    )(scalars, *arrays)


def fold(pairs, places, parts):
    rows = pairs[0][0].shape[0]
    half = rows // 2
    widths = [sum(c1 - c0 for _, c0, c1 in p) for p in parts]

    def sums(ref_pairs, part, at, size):
        return [
            (k[pl.ds(at, size), c0:c1].astype(F32) + g[pl.ds(at, size), c0:c1].astype(F32)).astype(BF16)
            for k, g, c0, c1 in ((*ref_pairs[p], c0, c1) for p, c0, c1 in part)
        ]

    if half % 16:
        results = []
        for part, place in zip(parts, places):
            total = jnp.concatenate(
                [
                    (pairs[p][0][:, c0:c1].astype(F32) + pairs[p][1][:, c0:c1].astype(F32)).astype(BF16)
                    for p, c0, c1 in part
                ],
                1,
            )
            results.append(
                (
                    lax.dynamic_slice_in_dim(total, place * half, half, 0),
                    lax.dynamic_slice_in_dim(total, (1 - place) * half, half, 0),
                )
            )
        return results

    def kernel(place, *refs):
        ref_pairs = [(refs[2 * n], refs[2 * n + 1]) for n in range(len(pairs))]
        outs = refs[2 * len(pairs) :]
        for n, part in enumerate(parts):
            for side in range(2):
                at = pl.multiple_of((place[n] ^ side) * half, 16)
                col = 0
                for value in sums(ref_pairs, part, at, half):
                    outs[2 * n + side][:, col : col + value.shape[1]] = value
                    col += value.shape[1]

    got = whole_call(
        kernel,
        jnp.stack(places),
        [a for pair in pairs for a in pair],
        [(half, w) for w in widths for _ in range(2)],
        "fold",
    )
    return [(got[2 * n], got[2 * n + 1]) for n in range(len(parts))]


def unfold(pairs, places, parts):
    rows = pairs[0][0].shape[0]
    widths = [sum(c1 - c0 for _, c0, c1 in p) for p in parts]
    if rows % 16:
        joined = [
            jnp.where(s == 1, jnp.concatenate([g, m], 0), jnp.concatenate([m, g], 0))
            for (m, g), s in zip(pairs, places)
        ]
        return [jnp.concatenate([joined[p][:, c0:c1] for p, c0, c1 in part], 1) for part in parts]

    def kernel(place, *refs):
        outs = refs[2 * len(pairs) :]
        for n, part in enumerate(parts):
            col = 0
            for p, c0, c1 in part:
                for side in range(2):
                    at = pl.multiple_of((place[p] ^ side) * rows, 16)
                    outs[n][pl.ds(at, rows), col : col + c1 - c0] = refs[2 * p + side][:, c0:c1]
                col += c1 - c0

    return whole_call(
        kernel, jnp.stack(places), [a for pair in pairs for a in pair], [(2 * rows, w) for w in widths], "unfold"
    )


def reduction(halves, split, me, device_count):
    top = device_count // 2
    far = [mask for group in far_groups(device_count) for mask in group]
    cols = halves[0].shape[1]
    both = [[(0, 0, split)], [(0, split, cols)]]
    apart = [[(0, 0, split)], [(1, 0, cols - split)]]
    merged = [[(0, 0, split), (1, 0, cols - split)]]
    alone = [[(0, 0, cols)]]

    def place(mask):
        return ((me & mask) != 0).astype(jnp.int32)

    core = (me & 1) != 0
    send, keep = jnp.where(core, halves[0], halves[1]), jnp.where(core, halves[1], halves[0])
    got = yield [(send, 1)]
    pairs = [(keep, got[0])]
    for masks, parts in (((top, 2), both), ((2, top), apart)):
        cut = fold(pairs, [place(m) for m in masks], parts)
        got = yield [(c[1], m) for c, m in zip(cut, masks)]
        pairs = [(c[0], g) for c, g in zip(cut, got)]
    for n, mask in enumerate(far):
        (cut,) = fold(pairs, [place(mask)], alone if n else merged)
        got = yield [(cut[1], mask)]
        pairs = [(cut[0], got[0])]
    mine = (pairs[0][0].astype(F32) + pairs[0][1].astype(F32)).astype(BF16)
    for mask in reversed(far):
        (got,) = yield [(mine, mask)]
        last = mask == far[0]
        mine = unfold([(mine, got)], [place(mask)], both if last else alone)
        mine = mine if last else mine[0]
    for masks, parts in (((2, top), apart), ((top, 2), merged)):
        got = yield [(p, m) for p, m in zip(mine, masks)]
        mine = unfold(list(zip(mine, got)), [place(m) for m in masks], parts)
    (got,) = yield [(mine[0], 1)]
    return mine[0], got


def small_sum(values, device_count):
    mask = 1
    while mask < device_count:
        (got,) = yield [(values, mask)]
        values = values + got
        mask *= 2
    return values


class Line:
    def __init__(self, steps, device_count):
        self.steps = steps
        self.count = device_count
        self.sum = None
        self.want = next(steps)

    def take(self, got):
        try:
            self.want = self.steps.send(got)
        except StopIteration as end:
            self.want, self.sum = None, end.value


def slot(lines, work=None, values=()):
    flying = []
    for n in lines:
        if n.want is not None and sum(len(f.want) for f in flying) + len(n.want) <= IN_FLIGHT:
            flying.append(n)
    lines = flying
    arrays = [[a for a, _ in n.want] for n in lines]
    arrays, values = lax.optimization_barrier((arrays, tuple(values)))
    got = [[swap_with(a, m, n.count) for a, (_, m) in zip(sends, n.want)] for sends, n in zip(arrays, lines)]
    out = work(*values) if work is not None else ()
    got, out = lax.optimization_barrier((got, out))
    for n, g in zip(lines, got):
        n.take(g)
    return out


def body(
    query_tokens,
    passage_tokens,
    query_lengths,
    passage_lengths,
    positives,
    w_query,
    b_query,
    w_key,
    w_value,
    b_value,
    w_out,
    b_out,
    norm1_gain,
    norm1_bias,
    w_in,
    b_in,
    w_down,
    b_down,
    norm2_gain,
    norm2_bias,
    query_out_grad,
    passage_out_grad,
):
    seqs = query_lengths.shape[0]
    width = query_tokens.shape[1]
    device_count = lax.axis_size(AXES)
    my_index = lax.axis_index(AXES)
    params = dict(
        w_query=w_query, b_query=b_query, w_key=w_key, w_value=w_value, b_value=b_value, w_out=w_out,
        b_out=b_out, norm1_gain=norm1_gain, norm1_bias=norm1_bias, w_in=w_in, b_in=b_in, w_down=w_down,
        b_down=b_down, norm2_gain=norm2_gain, norm2_bias=norm2_bias,
    )
    (
        query_out, passage_out, q, k, v, o, lse, xhat1, rstd1, h1b, g, gelu_slope, xhat2, rstd2, unit, mean,
    ) = forward(query_tokens, passage_tokens, query_lengths, passage_lengths, params)
    x_rows = jnp.concatenate(
        [query_tokens.reshape(seqs, QRY_LEN, width), passage_tokens.reshape(seqs, PASS_LEN, width)], 1
    ).reshape(seqs * PAIR_LEN, width)

    units, relative = gather_relative(unit, device_count)
    owner = jnp.array(relative, jnp.int32) ^ my_index
    ids = (owner[:, None] * seqs + jnp.arange(seqs, dtype=jnp.int32)[None, :]).reshape(-1)
    ids = jnp.repeat(ids, 2)
    target = positives[ids][:, None]
    dz, dr2, small2, loss_sum = loss_and_second_norm(
        units, target, ids[None, :], mean, query_lengths, passage_lengths, query_out_grad, passage_out_grad,
        xhat2, rstd2, norm2_gain,
    )
    loss = loss_sum[0, 0] / (seqs * device_count)
    def line(halves, split):
        return Line(reduction(halves, split, my_index, device_count), device_count)

    def weight_grad(a, b):
        return tn(a, b).astype(BF16)

    def attend_back(part):
        return lambda *arrays: attention_back(query_lengths, passage_lengths, *arrays, part, 3)

    half_ff = g.shape[1] // 2
    half_w = width // 2
    down = line((weight_grad(g[:, :half_ff], dz), weight_grad(g[:, half_ff:], dz)), half_w)
    acc, du, grad_b_in = dr2, [], []
    for part in range(3):
        some, bias, acc = slot(
            [down], lambda *arrays: ffn_back(*arrays, part, 3), (dz, acc, gelu_slope, w_down, w_in)
        )
        du.append(some)
        grad_b_in.append(bias)
    dr1, da, do, small1 = slot([down], first_norm_back, (acc, xhat1, rstd1, norm1_gain, w_out))
    third = du[0].shape[1]

    def in_halves(h, o, da, d0, d1, d2):
        w_half = [weight_grad(o, da[:, n * half_w : (n + 1) * half_w]) for n in range(2)]
        low = [weight_grad(h, d0), weight_grad(h, d1[:, : third // 2]), w_half[0]]
        high = [weight_grad(h, d1[:, third // 2 :]), weight_grad(h, d2), w_half[1]]
        return [jnp.concatenate(low, 1), jnp.concatenate(high, 1)]

    halves = slot([down], in_halves, (h1b, o, da, *du))
    up = line(halves, (half_ff + half_w + 255) // 256 * 128)
    sources = (q, k, v, o, do, lse)
    heads = [slot([down, up], attend_back(part), sources) for part in range(3)]
    dq, dk, dv = [[h[n] for h in heads] for n in range(3)]
    fine = dk[0].shape[1] // 2

    def proj_halves(x, *d):
        low = [weight_grad(x, t) for t in (*d[:4], d[4][:, :fine])]
        high = [weight_grad(x, t) for t in (d[4][:, fine:], *d[5:])]
        return [jnp.concatenate(low, 1), jnp.concatenate(high, 1)]

    halves = slot([down, up], proj_halves, (x_rows, *dq, *dk, *dv))
    proj = line(halves, (3 * half_w + 255) // 256 * 128)
    small0 = jnp.concatenate([h[3] for h in heads], 1)
    packed = jnp.concatenate(
        [small0, small1, small2, jnp.concatenate(grad_b_in, 1).reshape(-1, width)], 0
    )
    small = Line(small_sum(packed, device_count), device_count)
    lines = [down, up, proj, small]
    query_input_grad, passage_input_grad = slot(lines, input_grad, (dr1, dq, dk, dv, w_query, w_key, w_value))
    bit = (my_index & 1)[None]
    grad_w_down = None
    grad_w_in = None
    while any(n.want is not None for n in lines):
        if down.sum is not None and grad_w_down is None:
            grad_w_down = slot(lines, place_down, (bit, *down.sum))
        elif up.sum is not None and grad_w_in is None:
            grad_w_in, grad_w_out = slot(
                lines,
                lambda bit, *pair: place_columns(bit, [pair], (2 * half_ff, width), write_in, "place_in"),
                (bit, *up.sum),
            )
        else:
            slot(lines)
    grad_w_query, grad_w_key, grad_w_value = place_columns(
        bit, [proj.sum], (width,) * 3, write_proj, "place_proj"
    )
    packed = small.sum
    return (
        query_out,
        passage_out,
        query_input_grad,
        passage_input_grad,
        loss,
        grad_w_query,
        packed[0],
        grad_w_key,
        grad_w_value,
        packed[1],
        grad_w_out,
        packed[10],
        packed[8],
        packed[9],
        grad_w_in,
        packed[24:].reshape(-1),
        grad_w_down,
        packed[18],
        packed[16],
        packed[17],
    )


def solution(mesh):
    placed = (
        P(("stream", "batch"), None),
        P(("stream", "batch"), None),
        P(("stream", "batch")),
        P(("stream", "batch")),
        P(),
        P(),
        P(),
        P(),
        P(),
        P(),
        P(),
        P(),
        P(),
        P(),
        P(),
        P(),
        P(),
        P(),
        P(),
        P(),
        P(("stream", "batch"), None),
        P(("stream", "batch"), None),
    )
    return jax.shard_map(
        body,
        mesh=mesh,
        in_specs=placed,
        out_specs=(
            P(("stream", "batch"), None),
            P(("stream", "batch"), None),
            P(("stream", "batch"), None),
            P(("stream", "batch"), None),
            P(),
            P(),
            P(),
            P(),
            P(),
            P(),
            P(),
            P(),
            P(),
            P(),
            P(),
            P(),
            P(),
            P(),
            P(),
            P(),
        ),
        check_vma=False,
    )
```

```python
import functools

import jax
import jax.numpy as jnp
from jax import lax
from jax.experimental import pallas as pl
from jax.experimental.pallas import tpu as pltpu
from jax.sharding import PartitionSpec as P

HEADS = 12
QRY_LEN = 64
PASS_LEN = 512
PAIR_LEN = QRY_LEN + PASS_LEN
LOGIT_SCALE = 0.01
EPS = 1e-06
NEG = -1e30
F32 = jnp.float32
BF16 = jnp.bfloat16
AXES = ("stream", "batch")
MIB = 1024 * 1024
VMEM_LIMIT = 60 * MIB


def kernel_cost(us):
    return pl.CostEstimate(flops=us * 1_000_000_000, bytes_accessed=1_000_000, transcendentals=0)


def nn(a, b):
    return lax.dot_general(a, b, (((1,), (0,)), ((), ())), preferred_element_type=F32)


def nt(a, b):
    return lax.dot_general(a, b, (((1,), (1,)), ((), ())), preferred_element_type=F32)


def tn(a, b):
    return lax.dot_general(a, b, (((0,), (0,)), ((), ())), preferred_element_type=F32)


def gelu_parts(u):
    cdf = 0.5 + 0.5 * lax.erf(u * 0.7071067811865476)
    bell = jnp.exp(-0.5 * (u * u))
    return u * cdf, cdf + u * (bell * 0.3989422804014327)


def forward_kernel(
    qlen, plen, xq, xp, wq_h, wk_h, wv_h, wo_h, wi_h, wd_h, bq, bv, bo, n1g, n1b, bi, bd, n2g, n2b,
    yq, yp, q_h, k_h, v_h, o_h, lse_o, xh1_h, rs1_o, h1b_h, g_h, gp_h, x_h, xh2_o, rs2_o, unit_o, mean_o,
    xs, wq, wk, wv, wo, wi, wd, acc, h1, kmask, q_o, k_o, v_o, o_o, xh1_o, h1b_o, g_o, gp_o, sems, out_sems,
):
    step = pl.program_id(0)
    width = xs.shape[1]
    copies = [
        pltpu.make_async_copy(src, dst, sems.at[n])
        for n, (src, dst) in enumerate(
            ((wq_h, wq), (wk_h, wk), (wv_h, wv), (wo_h, wo), (wi_h, wi), (wd_h, wd))
        )
    ]

    here = pl.ds(pl.multiple_of(step * PAIR_LEN, PAIR_LEN), PAIR_LEN)
    saved = (
        (q_o, q_h), (k_o, k_h), (v_o, v_h), (o_o, o_h), (xh1_o, xh1_h), (h1b_o, h1b_h), (g_o, g_h), (gp_o, gp_h),
        (xs, x_h),
    )
    saves = [pltpu.make_async_copy(src, dst.at[here], out_sems.at[n]) for n, (src, dst) in enumerate(saved)]

    def free(*which):
        @pl.when(step > 0)
        def _():
            for n in which:
                saves[n].wait()

    @pl.when(step == 0)
    def _():
        for c in copies:
            c.start()
        lse_o[...] = jnp.zeros_like(lse_o)

    def ready(n):
        @pl.when(step == 0)
        def _():
            copies[n].wait()

    free(0, 1, 2, 3, 8)
    xs[:QRY_LEN, :] = xq[...]
    xs[QRY_LEN:, :] = xp[...]
    saves[8].start()
    ready(0)
    q_o[...] = (nn(xs[...], wq[...]) + bq[...]).astype(BF16)
    ready(1)
    k_o[...] = nn(xs[...], wk[...]).astype(BF16)
    ready(2)
    v_o[...] = (nn(xs[...], wv[...]) + bv[...]).astype(BF16)
    for n in range(3):
        saves[n].start()

    lane = lax.broadcasted_iota(jnp.int32, (1, 128), 1)
    low = (lane < 64).astype(F32)
    lanes = (low, 1.0 - low)
    ones = ((lane == 64).astype(F32), (lane == 0).astype(F32))
    q_gain = [(v * 0.125).astype(BF16) for v in lanes]
    keep = [v.astype(BF16) for v in lanes]
    one = [v.astype(BF16) for v in ones]

    q_valid = lax.broadcasted_iota(jnp.int32, (QRY_LEN, 128), 0) < qlen[step]
    p_valid = lax.broadcasted_iota(jnp.int32, (PASS_LEN, 128), 0) < plen[step]
    for side in range(2):
        kmask[side, :QRY_LEN, :] = jnp.where(q_valid, 0.0, NEG * ones[side]).astype(BF16)
        kmask[side, QRY_LEN:, :] = jnp.where(p_valid, 0.0, NEG * ones[side]).astype(BF16)

    def attend(pair, carry):
        cols = pl.ds(pl.multiple_of(pair * 128, 128), 128)
        for rows in (pl.ds(0, QRY_LEN), pl.ds(QRY_LEN, PASS_LEN)):
            qp, kp, vp = q_o[rows, cols], k_o[rows, cols], v_o[rows, cols]
            mixed = []
            scores = [
                nt(qp * q_gain[side] + one[side], kp * keep[side] + kmask[side, rows, :]) for side in range(2)
            ]
            tops = [jnp.max(s, axis=1, keepdims=True) for s in scores]
            probs = [jnp.exp(s - top).astype(BF16) for s, top in zip(scores, tops)]
            outs = [nn(probs[side], vp * keep[side] + one[side]) for side in range(2)]
            for side in range(2):
                oe, top = outs[side], tops[side]
                total = oe[:, 64:65] if side == 0 else oe[:, 0:1]
                mixed.append(oe * (1.0 / total))
                lse = top + jnp.log(total)
                head = 2 * pair + side
                lse_o[rows, :] = jnp.where(lane == head, lse, lse_o[rows, :])
            o_o[rows, cols] = jnp.where(lane < 64, mixed[0], mixed[1]).astype(BF16)
        return carry

    lax.fori_loop(0, HEADS // 2, attend, 0, unroll=3)

    saves[3].start()
    ready(3)
    acc[...] = nn(o_o[...], wo[...])

    def norm(value):
        mean = jnp.mean(value, axis=-1, keepdims=True)
        c = value - mean
        rstd = lax.rsqrt(jnp.mean(c * c, axis=-1, keepdims=True) + EPS)
        return c * rstd, rstd

    CH = 64

    def first_norm(n, carry):
        rows = pl.ds(pl.multiple_of(n * CH, CH), CH)
        xhat, rstd = norm(xs[rows, :].astype(F32) + acc[rows, :] + bo[...])
        hid = xhat * n1g[...] + n1b[...]
        xh1_o[rows, :] = xhat.astype(BF16)
        rs1_o[rows, :] = rstd
        h1[rows, :] = hid
        h1b_o[rows, :] = hid.astype(BF16)
        return carry

    free(4, 5)
    lax.fori_loop(0, PAIR_LEN // CH, first_norm, 0, unroll=3)
    saves[4].start()
    saves[5].start()

    ready(4)
    ready(5)
    free(6, 7)
    g, slope = gelu_parts(nn(h1b_o[...], wi[...]) + bi[...])
    g_o[...] = g.astype(BF16)
    gp_o[...] = slope.astype(BF16)
    h1[...] += nn(g_o[...], wd[...])
    saves[6].start()
    saves[7].start()

    def second_norm(row0, rows_n, out, valid_n):
        def run(n, total):
            at = pl.multiple_of(n * CH, CH)
            rows = pl.ds(row0 + at, CH)
            xhat, rstd = norm(h1[rows, :] + bd[...])
            y = xhat * n2g[...] + n2b[...]
            xh2_o[rows, :] = xhat.astype(BF16)
            rs2_o[rows, :] = rstd
            out[pl.ds(at, CH), :] = y.astype(BF16)
            live = (lax.broadcasted_iota(jnp.int32, (CH, 1), 0) + at) < valid_n
            return total + jnp.sum(jnp.where(live, y, 0.0), axis=0, keepdims=True)

        total = lax.fori_loop(
            0, rows_n // CH, run, jnp.zeros((1, width), F32), unroll=min(4, rows_n // CH)
        )
        return total / valid_n.astype(F32)

    for kind, mean in enumerate(
        (
            second_norm(0, QRY_LEN, yq, qlen[step]),
            second_norm(QRY_LEN, PASS_LEN, yp, plen[step]),
        )
    ):
        at = pl.ds(2 * step + kind, 1)
        mean_o[at, :] = mean
        unit = mean * lax.rsqrt(jnp.sum(mean * mean, axis=-1, keepdims=True) + EPS)
        unit_o[at, :] = unit

    @pl.when(step == pl.num_programs(0) - 1)
    def _():
        for c in saves:
            c.wait()


def forward(xq, xp, qlen, plen, p):
    seqs = qlen.shape[0]
    width = xq.shape[1]
    ff = p["w_in"].shape[1]
    rows = seqs * PAIR_LEN
    whole = lambda shape: pl.BlockSpec(shape, lambda i: (0,) * len(shape))
    smem = pl.BlockSpec(memory_space=pltpu.SMEM)
    hbm = pl.BlockSpec(memory_space=pl.ANY)
    row_block = lambda n, w: pl.BlockSpec((n, w), lambda i: (i, 0))
    outs = [
        ((seqs * QRY_LEN, width), BF16, row_block(QRY_LEN, width)),
        ((seqs * PASS_LEN, width), BF16, row_block(PASS_LEN, width)),
        ((rows, width), BF16, hbm),
        ((rows, width), BF16, hbm),
        ((rows, width), BF16, hbm),
        ((rows, width), BF16, hbm),
        ((rows, 128), F32, row_block(PAIR_LEN, 128)),
        ((rows, width), BF16, hbm),
        ((rows, 1), F32, row_block(PAIR_LEN, 1)),
        ((rows, width), BF16, hbm),
        ((rows, ff), BF16, hbm),
        ((rows, ff), BF16, hbm),
        ((rows, width), BF16, hbm),
        ((rows, width), BF16, row_block(PAIR_LEN, width)),
        ((rows, 1), F32, row_block(PAIR_LEN, 1)),
        ((2 * seqs, width), F32, whole((2 * seqs, width))),
        ((2 * seqs, width), F32, whole((2 * seqs, width))),
    ]
    return pl.pallas_call(
        forward_kernel,
        grid=(seqs,),
        in_specs=[smem, smem, row_block(QRY_LEN, width), row_block(PASS_LEN, width)]
        + [hbm] * 6
        + [whole((width,))] * 5
        + [whole((ff,))]
        + [whole((width,))] * 3,
        out_specs=[o[2] for o in outs],
        out_shape=[jax.ShapeDtypeStruct(o[0], o[1]) for o in outs],
        scratch_shapes=[
            pltpu.VMEM((PAIR_LEN, width), BF16),
            pltpu.VMEM((width, width), BF16),
            pltpu.VMEM((width, width), BF16),
            pltpu.VMEM((width, width), BF16),
            pltpu.VMEM((width, width), BF16),
            pltpu.VMEM((width, ff), BF16),
            pltpu.VMEM((ff, width), BF16),
            pltpu.VMEM((PAIR_LEN, width), F32),
            pltpu.VMEM((PAIR_LEN, width), F32),
            pltpu.VMEM((2, PAIR_LEN, 128), BF16),
            *[pltpu.VMEM((PAIR_LEN, width), BF16) for _ in range(6)],
            *[pltpu.VMEM((PAIR_LEN, ff), BF16) for _ in range(2)],
            pltpu.SemaphoreType.DMA((6,)),
            pltpu.SemaphoreType.DMA((9,)),
        ],
        compiler_params=pltpu.CompilerParams(
            dimension_semantics=("arbitrary",), vmem_limit_bytes=VMEM_LIMIT
        ),
        cost_estimate=kernel_cost(45),
        name="forward_layer",
    )(
        qlen, plen, xq, xp, p["w_query"], p["w_key"], p["w_value"], p["w_out"], p["w_in"], p["w_down"],
        p["b_query"], p["b_value"], p["b_out"], p["norm1_gain"],
        p["norm1_bias"], p["b_in"], p["b_down"], p["norm2_gain"],
        p["norm2_bias"],
    )


def loss_kernel(
    qlen, plen, units_0, units_1, units_2, units_3, target, column_id, mean, ogq, ogp, xh2, rs2, n2g,
    dz_o, dr2_o, small_o, loss_o,
    de,
):
    step = pl.program_id(0)
    seqs = pl.num_programs(0)
    width = xh2.shape[1]
    mine = mean.shape[0]

    @pl.when(step == 0)
    def _():
        u = jnp.concatenate([t[...] for t in (units_0, units_1, units_2, units_3)], 0).astype(BF16)
        n = u.shape[0]
        row = lax.broadcasted_iota(jnp.int32, (n, n), 0)
        col = lax.broadcasted_iota(jnp.int32, (n, n), 1)
        pairs = ((row & 1) == 0) & ((col & 1) == 1)
        logits = jnp.where(pairs, nt(u, u) / LOGIT_SCALE, NEG)
        top = jnp.max(logits, axis=1, keepdims=True)
        lse = top + jnp.log(jnp.sum(jnp.exp(logits - top), axis=1, keepdims=True))
        hit = pairs & (target[...] == column_id[...])
        chosen = jnp.sum(jnp.where(hit, logits, 0.0), axis=1, keepdims=True)
        is_query = (lax.broadcasted_iota(jnp.int32, (n, 1), 0) & 1) == 0
        loss_o[...] = jnp.sum(jnp.where(is_query, lse - chosen, 0.0), axis=0, keepdims=True)
        dc = jnp.where(pairs, (jnp.exp(logits - lse) - hit.astype(F32)) / LOGIT_SCALE, 0.0)
        both = (dc + jnp.transpose(dc)).astype(BF16)
        dn = nn(both[:16], u)[:mine]
        e = mean[...]
        square = jnp.sum(e * e, axis=-1, keepdims=True) + EPS
        grad = (dn - e * (jnp.sum(e * dn, axis=-1, keepdims=True) / square)) * lax.rsqrt(square)
        de[...] = jnp.zeros_like(de)
        de[:mine, :] = grad
        small_o[...] = jnp.zeros_like(small_o)

    CH = 64

    def back(row0, rows_n, grads, valid_n, kind):
        shift = de[pl.ds(2 * step + kind, 1), :] / valid_n.astype(F32)

        def run(n, carry):
            at = pl.multiple_of(n * CH, CH)
            rows = pl.ds(row0 + at, CH)
            live = (lax.broadcasted_iota(jnp.int32, (CH, 1), 0) + at) < valid_n
            dy = grads[pl.ds(at, CH), :].astype(F32) + jnp.where(live, shift, 0.0)
            xhat = xh2[rows, :].astype(F32)
            dyg = dy * n2g[...]
            m1 = jnp.mean(dyg, axis=-1, keepdims=True)
            m2 = jnp.mean(dyg * xhat, axis=-1, keepdims=True)
            dr = rs2[rows, :] * (dyg - m1 - xhat * m2)
            db = dr.astype(BF16)
            dr2_o[rows, :] = dr
            dz_o[rows, :] = db
            small_o[0:1, :] += jnp.sum(dy * xhat, axis=0, keepdims=True)
            small_o[1:2, :] += jnp.sum(dy, axis=0, keepdims=True)
            small_o[2:3, :] += jnp.sum(db.astype(F32), axis=0, keepdims=True)
            return carry

        lax.fori_loop(0, rows_n // CH, run, 0, unroll=min(4, rows_n // CH))

    back(0, QRY_LEN, ogq, qlen[step], 0)
    back(QRY_LEN, PASS_LEN, ogp, plen[step], 1)


def loss_and_second_norm(units, target, column_id, mean, qlen, plen, ogq, ogp, xh2, rs2, n2g):
    seqs = qlen.shape[0]
    width = ogq.shape[1]
    rows = seqs * PAIR_LEN
    whole = lambda shape: pl.BlockSpec(shape, lambda i: (0,) * len(shape))
    smem = pl.BlockSpec(memory_space=pltpu.SMEM)
    row_block = lambda n, w: pl.BlockSpec((n, w), lambda i: (i, 0))
    return pl.pallas_call(
        loss_kernel,
        grid=(seqs,),
        in_specs=[
            smem, smem, *[whole(t.shape) for t in units], whole(target.shape), whole(column_id.shape), whole(mean.shape),
            row_block(QRY_LEN, width), row_block(PASS_LEN, width), row_block(PAIR_LEN, width),
            row_block(PAIR_LEN, 1), whole((width,)),
        ],
        out_specs=[row_block(PAIR_LEN, width), row_block(PAIR_LEN, width), whole((8, width)), whole((1, 1))],
        out_shape=[
            jax.ShapeDtypeStruct((rows, width), BF16),
            jax.ShapeDtypeStruct((rows, width), F32),
            jax.ShapeDtypeStruct((8, width), F32),
            jax.ShapeDtypeStruct((1, 1), F32),
        ],
        scratch_shapes=[pltpu.VMEM((8, width), F32)],
        compiler_params=pltpu.CompilerParams(
            dimension_semantics=("arbitrary",), vmem_limit_bytes=16 * MIB
        ),
        cost_estimate=kernel_cost(8),
        name="loss_norm_back",
    )(qlen, plen, *units, target, column_id, mean, ogq, ogp, xh2, rs2, n2g)


def in_hbm(array):
    return pltpu.with_memory_space_constraint(array, pltpu.HBM)


def ffn_back_kernel(dz, dr2, gp, wd, wi, du_o, bi_o, acc):
    step = pl.program_id(0)
    du = (nt(dz[...], wd[...]) * gp[...].astype(F32)).astype(BF16)
    du_o[...] = du
    bi_o[...] = jnp.sum(du.astype(F32), axis=0, keepdims=True)
    part = nt(du, wi[...])

    @pl.when(step == 0)
    def _():
        acc[...] = dr2[...] + part

    @pl.when(step > 0)
    def _():
        acc[...] += part


def ffn_back(dz, dr2, gp, wd, wi, part, parts):
    rows, width = dz.shape
    fb = 512
    steps = gp.shape[1] // fb // parts
    skip = part * steps
    whole = lambda shape: pl.BlockSpec(shape, lambda i: (0,) * len(shape))
    return pl.pallas_call(
        ffn_back_kernel,
        grid=(steps,),
        in_specs=[
            whole((rows, width)), whole((rows, width)),
            pl.BlockSpec((rows, fb), lambda i: (0, i + skip)),
            pl.BlockSpec((fb, width), lambda i: (i + skip, 0)),
            pl.BlockSpec((width, fb), lambda i: (0, i + skip)),
        ],
        out_specs=[
            pl.BlockSpec((rows, fb), lambda i: (0, i)),
            pl.BlockSpec((1, fb), lambda i: (0, i)),
            whole((rows, width)),
        ],
        out_shape=[
            jax.ShapeDtypeStruct((rows, steps * fb), BF16),
            jax.ShapeDtypeStruct((1, steps * fb), F32),
            jax.ShapeDtypeStruct((rows, width), F32),
        ],
        compiler_params=pltpu.CompilerParams(
            dimension_semantics=("arbitrary",), vmem_limit_bytes=28 * MIB
        ),
        cost_estimate=kernel_cost(10),
        name="ffn_back",
    )(dz, dr2, in_hbm(gp), in_hbm(wd), in_hbm(wi))


def first_norm_back_kernel(dh_ref, xh1, rs1, n1g, wo, dr1_o, da_o, do_o, small_o):
    CH = 64

    @pl.when(pl.program_id(0) == 0)
    def _():
        small_o[...] = jnp.zeros_like(small_o)

    def run(n, carry):
        rows = pl.ds(pl.multiple_of(n * CH, CH), CH)
        dh = dh_ref[rows, :]
        xhat = xh1[rows, :].astype(F32)
        dyg = dh * n1g[...]
        m1 = jnp.mean(dyg, axis=-1, keepdims=True)
        m2 = jnp.mean(dyg * xhat, axis=-1, keepdims=True)
        dr = rs1[rows, :] * (dyg - m1 - xhat * m2)
        db = dr.astype(BF16)
        dr1_o[rows, :] = dr
        da_o[rows, :] = db
        small_o[0:1, :] += jnp.sum(dh * xhat, axis=0, keepdims=True)
        small_o[1:2, :] += jnp.sum(dh, axis=0, keepdims=True)
        small_o[2:3, :] += jnp.sum(db.astype(F32), axis=0, keepdims=True)
        return carry

    lax.fori_loop(0, dh_ref.shape[0] // CH, run, 0, unroll=3)
    do_o[...] = nt(da_o[...], wo[...]).astype(BF16)


def first_norm_back(dh, xh1, rs1, n1g, wo):
    rows, width = dh.shape
    step = PAIR_LEN
    whole = lambda shape: pl.BlockSpec(shape, lambda i: (0,) * len(shape))
    block = lambda w: pl.BlockSpec((step, w), lambda i: (i, 0))
    return pl.pallas_call(
        first_norm_back_kernel,
        grid=(rows // step,),
        in_specs=[block(width), block(width), block(1), whole((width,)), whole((width, width))],
        out_specs=[block(width), block(width), block(width), whole((8, width))],
        out_shape=[
            jax.ShapeDtypeStruct((rows, width), F32),
            jax.ShapeDtypeStruct((rows, width), BF16),
            jax.ShapeDtypeStruct((rows, width), BF16),
            jax.ShapeDtypeStruct((8, width), F32),
        ],
        compiler_params=pltpu.CompilerParams(
            dimension_semantics=("arbitrary",), vmem_limit_bytes=24 * MIB
        ),
        cost_estimate=kernel_cost(8),
        name="first_norm_back",
    )(dh, xh1, rs1, n1g, wo)


def down_grad_kernel(half, g, dz, out):
    out[...] = tn(g[...], dz[...]).astype(BF16)


def down_grad(half, g, dz):
    rows, width = dz.shape
    ff = g.shape[1]
    blocks = 2
    size = ff // 2 // blocks
    return pl.pallas_call(
        down_grad_kernel,
        grid_spec=pltpu.PrefetchScalarGridSpec(
            num_scalar_prefetch=1,
            grid=(blocks,),
            in_specs=[
                pl.BlockSpec((rows, size), lambda n, half: (0, half[0] * blocks + n)),
                pl.BlockSpec((rows, width), lambda n, half: (0, 0)),
            ],
            out_specs=pl.BlockSpec((size, width), lambda n, half: (n, 0)),
        ),
        out_shape=jax.ShapeDtypeStruct((ff // 2, width), BF16),
        compiler_params=pltpu.CompilerParams(
            dimension_semantics=("arbitrary",), vmem_limit_bytes=30 * MIB
        ),
        cost_estimate=kernel_cost(5),
        name="down_grad",
    )(half, g, dz)


def in_grad_kernel(half, h, o, da, d0, d1, out):
    width = h.shape[1]

    for n, du in enumerate((d0, d1)):

        @pl.when(half[0] == n)
        def _():
            for at in range(0, du.shape[1], width):
                out[:, at : at + width] = tn(h[...], du[:, at : at + width]).astype(BF16)
            out[:, du.shape[1] :] = tn(o[...], da[:, n * width // 2 : (n + 1) * width // 2]).astype(BF16)


def in_grad(half, h, o, da, du):
    rows, width = h.shape
    cols = du[0].shape[1] + width // 2
    whole = lambda shape: pl.BlockSpec(shape, lambda i, half: (0, 0))
    return pl.pallas_call(
        in_grad_kernel,
        grid_spec=pltpu.PrefetchScalarGridSpec(
            num_scalar_prefetch=1,
            grid=(1,),
            in_specs=[whole((rows, width))] * 3 + [whole(d.shape) for d in du],
            out_specs=whole((width, cols)),
        ),
        out_shape=jax.ShapeDtypeStruct((width, cols), BF16),
        compiler_params=pltpu.CompilerParams(
            dimension_semantics=("arbitrary",), vmem_limit_bytes=34 * MIB
        ),
        cost_estimate=kernel_cost(6),
        name="in_grad",
    )(half, h, o, da, *du)


def proj_grad_kernel(half, x, dq, dk, dv, out):
    width = x.shape[1]
    mid = width // 2

    @pl.when(half[0] == 0)
    def _():
        out[:, :width] = tn(x[...], dq[...]).astype(BF16)
        out[:, width:] = tn(x[...], dk[:, :mid]).astype(BF16)

    @pl.when(half[0] == 1)
    def _():
        out[:, :mid] = tn(x[...], dk[:, mid:]).astype(BF16)
        out[:, mid:] = tn(x[...], dv[...]).astype(BF16)


def proj_grad(half, x, dq, dk, dv):
    rows, width = x.shape
    cols = 3 * width // 2
    whole = lambda shape: pl.BlockSpec(shape, lambda i, half: (0, 0))
    return pl.pallas_call(
        proj_grad_kernel,
        grid_spec=pltpu.PrefetchScalarGridSpec(
            num_scalar_prefetch=1,
            grid=(1,),
            in_specs=[whole((rows, width))] * 4,
            out_specs=whole((width, cols)),
        ),
        out_shape=jax.ShapeDtypeStruct((width, cols), BF16),
        compiler_params=pltpu.CompilerParams(
            dimension_semantics=("arbitrary",), vmem_limit_bytes=28 * MIB
        ),
        cost_estimate=kernel_cost(4),
        name="proj_grad",
    )(half, x, dq, dk, dv)


def attention_back_kernel(
    qlen, plen, q, k, v, o, do, lse,
    dq_o, dk_o, dv_o, small_o,
    kmask, lse_p, lse_q, delta_p, delta_q,
    *, first_head,
):
    step = pl.program_id(0)
    width = q.shape[1]
    pairs = width // 128
    lane = lax.broadcasted_iota(jnp.int32, (1, 128), 1)
    low = (lane < 64).astype(F32)
    lanes = (low, 1.0 - low)
    ones = ((lane == 64).astype(F32), (lane == 0).astype(F32))
    q_gain = [(t * 0.125).astype(BF16) for t in lanes]
    keep = [t.astype(BF16) for t in lanes]
    one = [t.astype(BF16) for t in ones]

    q_valid = lax.broadcasted_iota(jnp.int32, (QRY_LEN, 128), 0) < qlen[step]
    p_valid = lax.broadcasted_iota(jnp.int32, (PASS_LEN, 128), 0) < plen[step]
    for side in range(2):
        kmask[side, :QRY_LEN, :] = jnp.where(q_valid, 0.0, NEG * ones[side]).astype(BF16)
        kmask[side, QRY_LEN:, :] = jnp.where(p_valid, 0.0, NEG * ones[side]).astype(BF16)

    q_rows, p_rows = pl.ds(0, QRY_LEN), pl.ds(QRY_LEN, PASS_LEN)
    head_of = (
        lax.broadcasted_iota(jnp.int32, (16, width), 1) // 64
        == lax.broadcasted_iota(jnp.int32, (16, width), 0)
    ).astype(F32).astype(BF16)
    for rows, lse_t, delta_t in ((q_rows, lse_q, delta_q), (p_rows, lse_p, delta_p)):
        lse_t[...] = jnp.transpose(lse[rows, :])
        prod = do[rows, :].astype(F32) * o[rows, :].astype(F32)
        hi = prod.astype(BF16)
        lo = (prod - hi.astype(F32)).astype(BF16)
        delta_t[...] = nt(head_of, hi) + nt(head_of, lo)

    def attend(pair, carry):
        cols = pl.ds(pl.multiple_of(pair * 128, 128), 128)
        for rows, lse_t, delta_t in ((q_rows, lse_q, delta_q), (p_rows, lse_p, delta_p)):
            qp, kp, vp, dop = q[rows, cols], k[rows, cols], v[rows, cols], do[rows, cols]
            dq = dk = dv = None
            for side in range(2):
                head = pl.ds(2 * pair + side, 1)
                qm = qp * q_gain[side]
                km = kp * q_gain[side]
                dm = dop * keep[side]
                ke = kp * keep[side] + kmask[side, rows, :]
                st = nt(ke, qm + one[side])
                pt = jnp.exp(st - lse_t[pl.ds(first_head + 2 * pair + side, 1), :])
                dpt = nt(vp, dm)
                dst = (pt * (dpt - delta_t[head, :])).astype(BF16)
                dv_h = nn(pt.astype(BF16), dm)
                dk_h = nn(dst, qm)
                dq_h = tn(dst, km)
                dq = dq_h if dq is None else dq + dq_h
                dk = dk_h if dk is None else dk + dk_h
                dv = dv_h if dv is None else dv + dv_h
            dq_o[rows, cols] = dq.astype(BF16)
            dk_o[rows, cols] = dk.astype(BF16)
            dv_o[rows, cols] = dv.astype(BF16)
        return carry

    lax.fori_loop(0, pairs, attend, 0, unroll=pairs)

    @pl.when(step == 0)
    def _():
        small_o[...] = jnp.zeros_like(small_o)

    small_o[0:1, :] += jnp.sum(dq_o[...].astype(F32), axis=0, keepdims=True)
    small_o[1:2, :] += jnp.sum(dv_o[...].astype(F32), axis=0, keepdims=True)


def attention_back(qlen, plen, q, k, v, o, do, lse, part, parts, into):
    seqs = qlen.shape[0]
    rows, full = q.shape
    width = full // parts
    whole = lambda shape: pl.BlockSpec(shape, lambda i: (0,) * len(shape))
    smem = pl.BlockSpec(memory_space=pltpu.SMEM)
    block = pl.BlockSpec((PAIR_LEN, width), lambda i: (i, part))
    kernel = functools.partial(attention_back_kernel, first_head=part * width // 64)
    earlier = list(into) if into else []

    def body(*refs):
        kernel(*refs[:8], *refs[8 + len(earlier) :])

    return pl.pallas_call(
        body,
        grid=(seqs,),
        in_specs=[smem, smem]
        + [block] * 5
        + [pl.BlockSpec((PAIR_LEN, 128), lambda i: (i, 0))]
        + [pl.BlockSpec(memory_space=pl.ANY)] * len(earlier),
        out_specs=[block, block, block, whole((8, width))],
        out_shape=[jax.ShapeDtypeStruct((rows, full), BF16)] * 3 + [jax.ShapeDtypeStruct((8, width), F32)],
        input_output_aliases={8 + n: n for n in range(len(earlier))},
        scratch_shapes=[
            pltpu.VMEM((2, PAIR_LEN, 128), BF16),
            pltpu.VMEM((128, PASS_LEN), F32),
            pltpu.VMEM((128, QRY_LEN), F32),
            pltpu.VMEM((16, PASS_LEN), F32),
            pltpu.VMEM((16, QRY_LEN), F32),
        ],
        compiler_params=pltpu.CompilerParams(
            dimension_semantics=("arbitrary",), vmem_limit_bytes=52 * MIB
        ),
        cost_estimate=kernel_cost(10),
        name="attention_back",
    )(qlen, plen, q, k, v, o, do, lse, *earlier)


def input_grad_kernel(dr1, dq, dk, dv, wq, wk, wv, gq_o, gp_o):
    grad = dr1[...] + nt(dq[...], wq[...]) + nt(dk[...], wk[...]) + nt(dv[...], wv[...])
    gq_o[...] = grad[:QRY_LEN]
    gp_o[...] = grad[QRY_LEN:]


def input_grad(dr1, dq, dk, dv, wq, wk, wv):
    rows, width = dr1.shape
    seqs = rows // PAIR_LEN
    block = pl.BlockSpec((PAIR_LEN, width), lambda i: (i, 0))
    weight = pl.BlockSpec((width, width), lambda i: (0, 0))
    return pl.pallas_call(
        input_grad_kernel,
        grid=(seqs,),
        in_specs=[block] * 4 + [weight] * 3,
        out_specs=[
            pl.BlockSpec((QRY_LEN, width), lambda i: (i, 0)),
            pl.BlockSpec((PASS_LEN, width), lambda i: (i, 0)),
        ],
        out_shape=[
            jax.ShapeDtypeStruct((seqs * QRY_LEN, width), F32),
            jax.ShapeDtypeStruct((seqs * PASS_LEN, width), F32),
        ],
        compiler_params=pltpu.CompilerParams(
            dimension_semantics=("arbitrary",), vmem_limit_bytes=26 * MIB
        ),
        cost_estimate=kernel_cost(10),
        name="input_grad",
    )(dr1, dq, dk, dv, wq, wk, wv)


def widen(out, cols, value):
    out[:, cols[0] : cols[1]] = value.astype(F32)


def place_down_kernel(bit, mine, other, out):
    half = pl.program_id(0)

    @pl.when(half == 0)
    def _():
        out[...] = mine[...].astype(F32)

    @pl.when(half == 1)
    def _():
        out[...] = other[...].astype(F32)


def place_down(bit, mine, other):
    rows, cols = mine.shape
    chunks = 4
    step = rows // chunks
    return pl.pallas_call(
        place_down_kernel,
        grid_spec=pltpu.PrefetchScalarGridSpec(
            num_scalar_prefetch=1,
            grid=(2, chunks),
            in_specs=[
                pl.BlockSpec((step, cols), lambda h, n, bit: (jnp.where(h == 0, n, chunks - 1), 0)),
                pl.BlockSpec((step, cols), lambda h, n, bit: (jnp.where(h == 1, n, 0), 0)),
            ],
            out_specs=pl.BlockSpec((step, cols), lambda h, n, bit: ((h ^ bit[0]) * chunks + n, 0)),
        ),
        out_shape=jax.ShapeDtypeStruct((2 * rows, cols), F32),
        compiler_params=pltpu.CompilerParams(
            dimension_semantics=("arbitrary", "arbitrary"), vmem_limit_bytes=16 * MIB
        ),
        cost_estimate=kernel_cost(5),
        name="place_down",
    )(bit, mine, other)


def place_columns(bit, sums, widths, write, name):
    rows = sums[0][0].shape[0]
    chunks = 4
    step = rows // chunks
    arrays = [a for pair in sums for a in pair]

    def kernel(bit, *refs):
        ins, outs = refs[: len(arrays)], refs[len(arrays) :]
        pairs = [(ins[2 * n], ins[2 * n + 1]) for n in range(len(sums))]

        @pl.when(bit[0] == 0)
        def _():
            write(outs, pairs)

        @pl.when(bit[0] == 1)
        def _():
            write(outs, [p[::-1] for p in pairs])

    return pl.pallas_call(
        kernel,
        grid_spec=pltpu.PrefetchScalarGridSpec(
            num_scalar_prefetch=1,
            grid=(chunks,),
            in_specs=[pl.BlockSpec((step, a.shape[1]), lambda n, bit: (n, 0)) for a in arrays],
            out_specs=[pl.BlockSpec((step, w), lambda n, bit: (n, 0)) for w in widths],
        ),
        out_shape=[jax.ShapeDtypeStruct((rows, w), F32) for w in widths],
        compiler_params=pltpu.CompilerParams(
            dimension_semantics=("arbitrary",), vmem_limit_bytes=20 * MIB
        ),
        cost_estimate=kernel_cost(5),
        name=name,
    )(bit, *arrays)


def write_in(outs, pairs):
    for n, half in enumerate(pairs[0]):
        at = 0
        for out in outs:
            size = out.shape[1] // 2
            widen(out, (n * size, (n + 1) * size), half[:, at : at + size])
            at += size


def write_proj(outs, pairs):
    size = outs[0].shape[1]
    low, high = pairs[0]
    widen(outs[0], (0, size), low[:, :size])
    widen(outs[1], (0, size // 2), low[:, size:])
    widen(outs[1], (size // 2, size), high[:, : size // 2])
    widen(outs[2], (0, size), high[:, size // 2 :])


IN_FLIGHT = 5


def swap_with(value, mask, device_count):
    return lax.ppermute(value, AXES, [(i, i ^ mask) for i in range(device_count)])


def far_groups(device_count):
    masks, mask = [], 4
    while mask < device_count // 2:
        masks.append(mask)
        mask *= 2
    return [masks[n : n + 2] for n in range(0, len(masks), 2)]


def combos_of(group):
    combos = [0]
    for mask in reversed(group):
        combos = combos + [c ^ mask for c in combos]
    return combos


def gather_relative(value, device_count):
    groups = [[1], [device_count // 2, 2]] + far_groups(device_count)
    relative = [0]
    for n, group in enumerate(groups):
        combos = combos_of(group)
        got = [value] + [swap_with(value, c, device_count) for c in combos[1:]]
        relative = [c ^ r for c in combos for r in relative]
        if n < len(groups) - 1 or len(got) < 4:
            value = jnp.concatenate(got, axis=0)
    if len(got) < 4:
        quarter = value.shape[0] // 4
        got = [value[n * quarter : (n + 1) * quarter] for n in range(4)]
    return got, relative


def whole_call(kernel, scalars, arrays, outs, name):
    spec = lambda shape: pl.BlockSpec(shape, lambda i, s: (0, 0))
    return pl.pallas_call(
        kernel,
        grid_spec=pltpu.PrefetchScalarGridSpec(
            num_scalar_prefetch=1,
            grid=(1,),
            in_specs=[spec(a.shape) for a in arrays],
            out_specs=[spec(o) for o in outs],
        ),
        out_shape=[jax.ShapeDtypeStruct(o, BF16) for o in outs],
        compiler_params=pltpu.CompilerParams(vmem_limit_bytes=24 * MIB),
        cost_estimate=kernel_cost(1),
        name=name,
    )(scalars, *arrays)


def fold(tuples, places, parts, ways=2):
    rows = tuples[0][0].shape[0] // ways
    widths = [sum(c1 - c0 for _, c0, c1 in p) for p in parts]
    arrays = [a for one in tuples for a in one]

    def add(values):
        total = values[0].astype(F32)
        for value in values[1:]:
            total = total + value.astype(F32)
        return total.astype(BF16)

    if rows % 16:
        results = []
        for part, place in zip(parts, places):
            total = jnp.concatenate([add([a[:, c0:c1] for a in tuples[p]]) for p, c0, c1 in part], 1)
            results.append(
                [lax.dynamic_slice_in_dim(total, (place ^ n) * rows, rows, 0) for n in range(ways)]
            )
        return results

    def kernel(place, *refs):
        taken, ref_tuples = 0, []
        for one in tuples:
            ref_tuples.append(refs[taken : taken + len(one)])
            taken += len(one)
        outs = refs[taken:]
        for m, part in enumerate(parts):
            for n in range(ways):
                at = pl.ds(pl.multiple_of((place[m] ^ n) * rows, 16), rows)
                col = 0
                for p, c0, c1 in part:
                    outs[ways * m + n][:, col : col + c1 - c0] = add([r[at, c0:c1] for r in ref_tuples[p]])
                    col += c1 - c0

    got = whole_call(
        kernel, jnp.stack(places), arrays, [(rows, w) for w in widths for _ in range(ways)], "fold"
    )
    return [got[ways * m : ways * (m + 1)] for m in range(len(parts))]


def unfold(tuples, places, parts):
    rows = tuples[0][0].shape[0]
    ways = len(tuples[0])
    widths = [sum(c1 - c0 for _, c0, c1 in p) for p in parts]
    if rows % 16:
        joined = [
            jnp.concatenate([lax.select_n(s, *[t[b ^ n] for n in range(ways)]) for b in range(ways)], 0)
            if ways > 2
            else jnp.where(s == 1, jnp.concatenate([t[1], t[0]], 0), jnp.concatenate([t[0], t[1]], 0))
            for t, s in zip(tuples, places)
        ]
        return [jnp.concatenate([joined[p][:, c0:c1] for p, c0, c1 in part], 1) for part in parts]

    def kernel(place, *refs):
        outs = refs[ways * len(tuples) :]
        for m, part in enumerate(parts):
            col = 0
            for p, c0, c1 in part:
                for n in range(ways):
                    at = pl.ds(pl.multiple_of((place[p] ^ n) * rows, 16), rows)
                    outs[m][at, col : col + c1 - c0] = refs[ways * p + n][:, c0:c1]
                col += c1 - c0

    return whole_call(
        kernel, jnp.stack(places), [a for t in tuples for a in t], [(ways * rows, w) for w in widths], "unfold"
    )


def reduction(send, kept, split, wide, me, device_count):
    top = device_count // 2
    far = far_groups(device_count)
    if not wide:
        far = [[mask] for group in far for mask in group]
    cols = send.shape[1]
    both = [[(0, 0, split)], [(0, split, cols)]]
    apart = [[(0, 0, split)], [(1, 0, cols - split)]]
    merged = [[(0, 0, split), (1, 0, cols - split)]]
    alone = [[(0, 0, cols)]]

    def place(group):
        pos = jnp.int32(0)
        for mask in group:
            pos = 2 * pos + ((me & mask) != 0).astype(jnp.int32)
        return pos

    got = yield [(send, 1)]
    sums = [(kept[0], got[0])]
    for masks, parts in (((top, 2), both), ((2, top), apart)):
        cut = fold(sums, [place([m]) for m in masks], parts)
        got = yield [(c[1], m) for c, m in zip(cut, masks)]
        sums = [(c[0], g) for c, g in zip(cut, got)]
    for n, group in enumerate(far):
        combos = combos_of(group)
        (cut,) = fold(sums, [place(group)], alone if n else merged, len(combos))
        got = yield list(zip(cut[1:], combos[1:]))
        sums = [(cut[0], *got)]
    total = sums[0][0].astype(F32)
    for value in sums[0][1:]:
        total = total + value.astype(F32)
    mine = total.astype(BF16)
    for group in reversed(far):
        got = yield [(mine, c) for c in combos_of(group)[1:]]
        last = group is far[0]
        mine = unfold([(mine, *got)], [place(group)], both if last else alone)
        mine = mine if last else mine[0]
    for masks, parts in (((2, top), apart), ((top, 2), merged)):
        got = yield [(p, m) for p, m in zip(mine, masks)]
        mine = unfold(list(zip(mine, got)), [place([m]) for m in masks], parts)
    (got,) = yield [(mine[0], 1)]
    return mine[0], got


def small_sum(values, device_count):
    mask = 1
    while mask < device_count:
        (got,) = yield [(values, mask)]
        values = values + got
        mask *= 2
    return values


class Line:
    def __init__(self, steps, device_count):
        self.steps = steps
        self.count = device_count
        self.sum = None
        self.want = next(steps)

    def take(self, got):
        try:
            self.want = self.steps.send(got)
        except StopIteration as end:
            self.want, self.sum = None, end.value


def slot(lines, work=None, values=(), kept=None):
    flying = []
    for n in lines:
        if n.want is not None and sum(len(f.want) for f in flying) + len(n.want) <= IN_FLIGHT:
            flying.append(n)
    lines = flying
    arrays = [[a for a, _ in n.want] for n in lines]
    arrays, values = lax.optimization_barrier((arrays, tuple(values)))
    got = [[swap_with(a, m, n.count) for a, (_, m) in zip(sends, n.want)] for sends, n in zip(arrays, lines)]
    out = work(*values) if work is not None else ()
    got, out = lax.optimization_barrier((got, out))
    if kept is not None:
        kept.append(out)
    for n, g in zip(lines, got):
        n.take(g)
    return out


def body(
    query_tokens,
    passage_tokens,
    query_lengths,
    passage_lengths,
    positives,
    w_query,
    b_query,
    w_key,
    w_value,
    b_value,
    w_out,
    b_out,
    norm1_gain,
    norm1_bias,
    w_in,
    b_in,
    w_down,
    b_down,
    norm2_gain,
    norm2_bias,
    query_out_grad,
    passage_out_grad,
):
    seqs = query_lengths.shape[0]
    width = query_tokens.shape[1]
    device_count = lax.axis_size(AXES)
    my_index = lax.axis_index(AXES)
    params = dict(
        w_query=w_query, b_query=b_query, w_key=w_key, w_value=w_value, b_value=b_value, w_out=w_out,
        b_out=b_out, norm1_gain=norm1_gain, norm1_bias=norm1_bias, w_in=w_in, b_in=b_in, w_down=w_down,
        b_down=b_down, norm2_gain=norm2_gain, norm2_bias=norm2_bias,
    )
    (
        query_out, passage_out, q, k, v, o, lse, xhat1, rstd1, h1b, g, gelu_slope, x_rows, xhat2, rstd2, unit, mean,
    ) = forward(query_tokens, passage_tokens, query_lengths, passage_lengths, params)
    units, relative = gather_relative(unit, device_count)
    owner = jnp.array(relative, jnp.int32) ^ my_index
    ids = (owner[:, None] * seqs + jnp.arange(seqs, dtype=jnp.int32)[None, :]).reshape(-1)
    ids = jnp.repeat(ids, 2)
    target = positives[ids][:, None]
    dz, dr2, small2, loss_sum = loss_and_second_norm(
        units, target, ids[None, :], mean, query_lengths, passage_lengths, query_out_grad, passage_out_grad,
        xhat2, rstd2, norm2_gain,
    )
    loss = loss_sum[0, 0] / (seqs * device_count)
    core = (my_index & 1).astype(jnp.int32)[None]
    other = 1 - core

    def start_line(lines, make, values, wide=False):
        kept = []
        send = slot(lines, lambda *v: make(other, *v), values)
        split = (send.shape[1] + 255) // 256 * 128
        new = Line(reduction(send, kept, split, wide, my_index, device_count), device_count)
        slot(lines + [new], lambda *v: make(core, *v), values, kept)
        return new

    down = start_line([], lambda half, d: down_grad(half, g, d), (dz,))
    acc, du, grad_b_in = dr2, [], []
    for part in range(2):
        some, bias, acc = slot(
            [down], lambda *arrays: ffn_back(*arrays, part, 2), (dz, acc, gelu_slope, w_down, w_in)
        )
        du.append(some)
        grad_b_in.append(bias)
    dr1, da, do, small1 = slot([down], first_norm_back, (acc, xhat1, rstd1, norm1_gain, w_out))
    up = start_line([down], lambda half, h, o, da, *du: in_grad(half, h, o, da, du), (h1b, o, da, *du))
    grads, smalls = None, []
    for part in range(3):
        *grads, some = slot(
            [down, up],
            lambda *arrays: attention_back(
                query_lengths, passage_lengths, *arrays[:6], part, 3, arrays[6:] if part else None
            ),
            (q, k, v, o, do, lse, *(grads if part else ())),
        )
        smalls.append(some)
    dq, dk, dv = grads
    small0 = jnp.concatenate(smalls, 1)
    packed = jnp.concatenate(
        [small0, small1, small2, jnp.concatenate(grad_b_in, 1).reshape(-1, width)], 0
    )
    small = Line(small_sum(packed, device_count), device_count)
    proj = start_line([down, up, small], proj_grad, (x_rows, dq, dk, dv), wide=True)
    lines = [down, up, proj, small]
    query_input_grad, passage_input_grad = slot(lines, input_grad, (dr1, dq, dk, dv, w_query, w_key, w_value))
    bit = core
    grad_w_down = None
    grad_w_in = None
    while any(n.want is not None for n in lines):
        if down.sum is not None and grad_w_down is None:
            grad_w_down = slot(lines, place_down, (bit, *down.sum))
        elif up.sum is not None and grad_w_in is None:
            grad_w_in, grad_w_out = slot(
                lines,
                lambda bit, *pair: place_columns(bit, [pair], (g.shape[1], width), write_in, "place_in"),
                (bit, *up.sum),
            )
        else:
            slot(lines)
    grad_w_query, grad_w_key, grad_w_value = place_columns(
        bit, [proj.sum], (width,) * 3, write_proj, "place_proj"
    )
    packed = small.sum
    return (
        query_out,
        passage_out,
        query_input_grad,
        passage_input_grad,
        loss,
        grad_w_query,
        packed[0],
        grad_w_key,
        grad_w_value,
        packed[1],
        grad_w_out,
        packed[10],
        packed[8],
        packed[9],
        grad_w_in,
        packed[24:].reshape(-1),
        grad_w_down,
        packed[18],
        packed[16],
        packed[17],
    )


def solution(mesh):
    placed = (
        P(("stream", "batch"), None),
        P(("stream", "batch"), None),
        P(("stream", "batch")),
        P(("stream", "batch")),
        P(),
        P(),
        P(),
        P(),
        P(),
        P(),
        P(),
        P(),
        P(),
        P(),
        P(),
        P(),
        P(),
        P(),
        P(),
        P(),
        P(("stream", "batch"), None),
        P(("stream", "batch"), None),
    )
    return jax.shard_map(
        body,
        mesh=mesh,
        in_specs=placed,
        out_specs=(
            P(("stream", "batch"), None),
            P(("stream", "batch"), None),
            P(("stream", "batch"), None),
            P(("stream", "batch"), None),
            P(),
            P(),
            P(),
            P(),
            P(),
            P(),
            P(),
            P(),
            P(),
            P(),
            P(),
            P(),
            P(),
            P(),
            P(),
            P(),
        ),
        check_vma=False,
    )
```

```python
import functools

import jax
import jax.numpy as jnp
from jax import lax
from jax.experimental import pallas as pl
from jax.experimental.pallas import tpu as pltpu
from jax.sharding import PartitionSpec as P

HEADS = 12
QRY_LEN = 64
PASS_LEN = 512
PAIR_LEN = QRY_LEN + PASS_LEN
LOGIT_SCALE = 0.01
EPS = 1e-06
NEG = -1e30
F32 = jnp.float32
BF16 = jnp.bfloat16
AXES = ("stream", "batch")
MIB = 1024 * 1024
VMEM_LIMIT = 60 * MIB


def kernel_cost(us):
    return pl.CostEstimate(flops=us * 1_000_000_000, bytes_accessed=1_000_000, transcendentals=0)


def nn(a, b):
    return lax.dot_general(a, b, (((1,), (0,)), ((), ())), preferred_element_type=F32)


def nt(a, b):
    return lax.dot_general(a, b, (((1,), (1,)), ((), ())), preferred_element_type=F32)


def tn(a, b):
    return lax.dot_general(a, b, (((0,), (0,)), ((), ())), preferred_element_type=F32)


def gelu_parts(u):
    cdf = 0.5 + 0.5 * lax.erf(u * 0.7071067811865476)
    bell = jnp.exp(-0.5 * (u * u))
    return u * cdf, cdf + u * (bell * 0.3989422804014327)


def forward_kernel(
    qlen, plen, xq, xp, wq_h, wk_h, wv_h, wo_h, wi_h, wd_h, bq, bv, bo, n1g, n1b, bi, bd, n2g, n2b,
    yq, yp, q_h, k_h, v_h, o_h, lse_o, xh1_h, rs1_o, h1b_h, g_h, gp_h, x_h, xh2_o, rs2_o, unit_o, mean_o,
    xs, wq, wk, wv, wo, wi, wd, acc, h1, kmask, units, q_o, k_o, v_o, o_o, xh1_o, h1b_o, g_o, gp_o, sems, out_sems,
):
    step = pl.program_id(0)
    width = xs.shape[1]
    copies = [
        pltpu.make_async_copy(src, dst, sems.at[n])
        for n, (src, dst) in enumerate(
            ((wq_h, wq), (wk_h, wk), (wv_h, wv), (wo_h, wo), (wi_h, wi), (wd_h, wd))
        )
    ]

    here = pl.ds(pl.multiple_of(step * PAIR_LEN, PAIR_LEN), PAIR_LEN)
    saved = (
        (q_o, q_h), (k_o, k_h), (v_o, v_h), (o_o, o_h), (xh1_o, xh1_h), (h1b_o, h1b_h), (g_o, g_h), (gp_o, gp_h),
        (xs, x_h),
    )
    saves = [pltpu.make_async_copy(src, dst.at[here], out_sems.at[n]) for n, (src, dst) in enumerate(saved)]

    def free(*which):
        @pl.when(step > 0)
        def _():
            for n in which:
                saves[n].wait()

    @pl.when(step == 0)
    def _():
        for c in copies:
            c.start()
        lse_o[...] = jnp.zeros_like(lse_o)

    def ready(n):
        @pl.when(step == 0)
        def _():
            copies[n].wait()

    free(0, 1, 2, 3, 8)
    xs[:QRY_LEN, :] = xq[...]
    xs[QRY_LEN:, :] = xp[...]
    saves[8].start()
    ready(0)
    q_o[...] = (nn(xs[...], wq[...]) + bq[...]).astype(BF16)
    ready(1)
    k_o[...] = nn(xs[...], wk[...]).astype(BF16)
    ready(2)
    v_o[...] = (nn(xs[...], wv[...]) + bv[...]).astype(BF16)
    for n in range(3):
        saves[n].start()

    lane = lax.broadcasted_iota(jnp.int32, (1, 128), 1)
    low = (lane < 64).astype(F32)
    lanes = (low, 1.0 - low)
    ones = ((lane == 64).astype(F32), (lane == 0).astype(F32))
    q_gain = [(v * 0.125).astype(BF16) for v in lanes]
    keep = [v.astype(BF16) for v in lanes]
    one = [v.astype(BF16) for v in ones]

    q_valid = lax.broadcasted_iota(jnp.int32, (QRY_LEN, 128), 0) < qlen[step]
    p_valid = lax.broadcasted_iota(jnp.int32, (PASS_LEN, 128), 0) < plen[step]
    for side in range(2):
        kmask[side, :QRY_LEN, :] = jnp.where(q_valid, 0.0, NEG * ones[side]).astype(BF16)
        kmask[side, QRY_LEN:, :] = jnp.where(p_valid, 0.0, NEG * ones[side]).astype(BF16)

    def attend(pair, carry):
        cols = pl.ds(pl.multiple_of(pair * 128, 128), 128)
        for rows in (pl.ds(0, QRY_LEN), pl.ds(QRY_LEN, PASS_LEN)):
            qp, kp, vp = q_o[rows, cols], k_o[rows, cols], v_o[rows, cols]
            mixed = []
            scores = [
                nt(qp * q_gain[side] + one[side], kp * keep[side] + kmask[side, rows, :]) for side in range(2)
            ]
            tops = [jnp.max(s, axis=1, keepdims=True) for s in scores]
            probs = [jnp.exp(s - top).astype(BF16) for s, top in zip(scores, tops)]
            outs = [nn(probs[side], vp * keep[side] + one[side]) for side in range(2)]
            for side in range(2):
                oe, top = outs[side], tops[side]
                total = oe[:, 64:65] if side == 0 else oe[:, 0:1]
                mixed.append(oe * (1.0 / total))
                lse = top + jnp.log(total)
                head = 2 * pair + side
                lse_o[rows, :] = jnp.where(lane == head, lse, lse_o[rows, :])
            o_o[rows, cols] = jnp.where(lane < 64, mixed[0], mixed[1]).astype(BF16)
        return carry

    lax.fori_loop(0, HEADS // 2, attend, 0, unroll=3)

    saves[3].start()
    ready(3)
    acc[...] = nn(o_o[...], wo[...])

    def norm(value):
        mean = jnp.mean(value, axis=-1, keepdims=True)
        c = value - mean
        rstd = lax.rsqrt(jnp.mean(c * c, axis=-1, keepdims=True) + EPS)
        return c * rstd, rstd

    CH = 64

    def first_norm(n, carry):
        rows = pl.ds(pl.multiple_of(n * CH, CH), CH)
        xhat, rstd = norm(xs[rows, :].astype(F32) + acc[rows, :] + bo[...])
        hid = xhat * n1g[...] + n1b[...]
        xh1_o[rows, :] = xhat.astype(BF16)
        rs1_o[rows, :] = rstd
        h1[rows, :] = hid
        h1b_o[rows, :] = hid.astype(BF16)
        return carry

    free(4, 5)
    lax.fori_loop(0, PAIR_LEN // CH, first_norm, 0, unroll=3)
    saves[4].start()
    saves[5].start()

    ready(4)
    ready(5)
    free(6, 7)
    g, slope = gelu_parts(nn(h1b_o[...], wi[...]) + bi[...])
    g_o[...] = g.astype(BF16)
    gp_o[...] = slope.astype(BF16)
    h1[...] += nn(g_o[...], wd[...])
    saves[6].start()
    saves[7].start()

    def second_norm(row0, rows_n, out, valid_n):
        def run(n, total):
            at = pl.multiple_of(n * CH, CH)
            rows = pl.ds(row0 + at, CH)
            xhat, rstd = norm(h1[rows, :] + bd[...])
            y = xhat * n2g[...] + n2b[...]
            xh2_o[rows, :] = xhat.astype(BF16)
            rs2_o[rows, :] = rstd
            out[pl.ds(at, CH), :] = y.astype(BF16)
            live = (lax.broadcasted_iota(jnp.int32, (CH, 1), 0) + at) < valid_n
            return total + jnp.sum(jnp.where(live, y, 0.0), axis=0, keepdims=True)

        total = lax.fori_loop(
            0, rows_n // CH, run, jnp.zeros((1, width), F32), unroll=min(4, rows_n // CH)
        )
        return total / valid_n.astype(F32)

    for kind, mean in enumerate(
        (
            second_norm(0, QRY_LEN, yq, qlen[step]),
            second_norm(QRY_LEN, PASS_LEN, yp, plen[step]),
        )
    ):
        at = pl.ds(2 * step + kind, 1)
        mean_o[at, :] = mean
        unit = mean * lax.rsqrt(jnp.sum(mean * mean, axis=-1, keepdims=True) + EPS)
        units[at, :] = unit

    @pl.when(step == pl.num_programs(0) - 1)
    def _():
        unit_o[...] = units[...].astype(BF16)
        for c in saves:
            c.wait()


def forward(xq, xp, qlen, plen, p):
    seqs = qlen.shape[0]
    width = xq.shape[1]
    ff = p["w_in"].shape[1]
    rows = seqs * PAIR_LEN
    whole = lambda shape: pl.BlockSpec(shape, lambda i: (0,) * len(shape))
    smem = pl.BlockSpec(memory_space=pltpu.SMEM)
    hbm = pl.BlockSpec(memory_space=pl.ANY)
    row_block = lambda n, w: pl.BlockSpec((n, w), lambda i: (i, 0))
    outs = [
        ((seqs * QRY_LEN, width), BF16, row_block(QRY_LEN, width)),
        ((seqs * PASS_LEN, width), BF16, row_block(PASS_LEN, width)),
        ((rows, width), BF16, hbm),
        ((rows, width), BF16, hbm),
        ((rows, width), BF16, hbm),
        ((rows, width), BF16, hbm),
        ((rows, 128), F32, row_block(PAIR_LEN, 128)),
        ((rows, width), BF16, hbm),
        ((rows, 1), F32, row_block(PAIR_LEN, 1)),
        ((rows, width), BF16, hbm),
        ((rows, ff), BF16, hbm),
        ((rows, ff), BF16, hbm),
        ((rows, width), BF16, hbm),
        ((rows, width), BF16, row_block(PAIR_LEN, width)),
        ((rows, 1), F32, row_block(PAIR_LEN, 1)),
        ((2 * seqs, width), BF16, whole((2 * seqs, width))),
        ((2 * seqs, width), F32, whole((2 * seqs, width))),
    ]
    return pl.pallas_call(
        forward_kernel,
        grid=(seqs,),
        in_specs=[smem, smem, row_block(QRY_LEN, width), row_block(PASS_LEN, width)]
        + [hbm] * 6
        + [whole((width,))] * 5
        + [whole((ff,))]
        + [whole((width,))] * 3,
        out_specs=[o[2] for o in outs],
        out_shape=[jax.ShapeDtypeStruct(o[0], o[1]) for o in outs],
        scratch_shapes=[
            pltpu.VMEM((PAIR_LEN, width), BF16),
            pltpu.VMEM((width, width), BF16),
            pltpu.VMEM((width, width), BF16),
            pltpu.VMEM((width, width), BF16),
            pltpu.VMEM((width, width), BF16),
            pltpu.VMEM((width, ff), BF16),
            pltpu.VMEM((ff, width), BF16),
            pltpu.VMEM((PAIR_LEN, width), F32),
            pltpu.VMEM((PAIR_LEN, width), F32),
            pltpu.VMEM((2, PAIR_LEN, 128), BF16),
            pltpu.VMEM((2 * seqs, width), F32),
            *[pltpu.VMEM((PAIR_LEN, width), BF16) for _ in range(6)],
            *[pltpu.VMEM((PAIR_LEN, ff), BF16) for _ in range(2)],
            pltpu.SemaphoreType.DMA((6,)),
            pltpu.SemaphoreType.DMA((9,)),
        ],
        compiler_params=pltpu.CompilerParams(
            dimension_semantics=("arbitrary",), vmem_limit_bytes=VMEM_LIMIT
        ),
        cost_estimate=kernel_cost(45),
        name="forward_layer",
    )(
        qlen, plen, xq, xp, p["w_query"], p["w_key"], p["w_value"], p["w_out"], p["w_in"], p["w_down"],
        p["b_query"], p["b_value"], p["b_out"], p["norm1_gain"],
        p["norm1_bias"], p["b_in"], p["b_down"], p["norm2_gain"],
        p["norm2_bias"],
    )


def in_hbm(array):
    return pltpu.with_memory_space_constraint(array, pltpu.HBM)


def loss_kernel(
    qlen, plen, units_0, units_1, target, column_id, mean, ogq, ogp, xh2, rs2, n2g,
    dz_o, dr2_o, small_o, loss_o,
    de,
):
    step = pl.program_id(0)
    seqs = pl.num_programs(0)
    width = xh2.shape[1]
    mine = mean.shape[0]

    @pl.when(step == 0)
    def _():
        u = jnp.concatenate([units_0[...], units_1[...]], 0)
        n = u.shape[0]
        row = lax.broadcasted_iota(jnp.int32, (n, n), 0)
        col = lax.broadcasted_iota(jnp.int32, (n, n), 1)
        pairs = ((row & 1) == 0) & ((col & 1) == 1)
        logits = jnp.where(pairs, nt(u, u) / LOGIT_SCALE, NEG)
        top = jnp.max(logits, axis=1, keepdims=True)
        lse = top + jnp.log(jnp.sum(jnp.exp(logits - top), axis=1, keepdims=True))
        hit = pairs & (target[...] == column_id[...])
        chosen = jnp.sum(jnp.where(hit, logits, 0.0), axis=1, keepdims=True)
        is_query = (lax.broadcasted_iota(jnp.int32, (n, 1), 0) & 1) == 0
        loss_o[...] = jnp.sum(jnp.where(is_query, lse - chosen, 0.0), axis=0, keepdims=True)
        dc = jnp.where(pairs, (jnp.exp(logits - lse) - hit.astype(F32)) / LOGIT_SCALE, 0.0)
        both = (dc + jnp.transpose(dc)).astype(BF16)
        dn = nn(both[:16], u)[:mine]
        e = mean[...]
        square = jnp.sum(e * e, axis=-1, keepdims=True) + EPS
        grad = (dn - e * (jnp.sum(e * dn, axis=-1, keepdims=True) / square)) * lax.rsqrt(square)
        de[...] = jnp.zeros_like(de)
        de[:mine, :] = grad
        small_o[...] = jnp.zeros_like(small_o)

    CH = 64

    def back(row0, rows_n, grads, valid_n, kind):
        shift = de[pl.ds(2 * step + kind, 1), :] / valid_n.astype(F32)

        def run(n, carry):
            at = pl.multiple_of(n * CH, CH)
            rows = pl.ds(row0 + at, CH)
            live = (lax.broadcasted_iota(jnp.int32, (CH, 1), 0) + at) < valid_n
            dy = grads[pl.ds(at, CH), :].astype(F32) + jnp.where(live, shift, 0.0)
            xhat = xh2[rows, :].astype(F32)
            dyg = dy * n2g[...]
            m1 = jnp.mean(dyg, axis=-1, keepdims=True)
            m2 = jnp.mean(dyg * xhat, axis=-1, keepdims=True)
            dr = rs2[rows, :] * (dyg - m1 - xhat * m2)
            db = dr.astype(BF16)
            dr2_o[rows, :] = dr
            dz_o[rows, :] = db
            small_o[0:1, :] += jnp.sum(dy * xhat, axis=0, keepdims=True)
            small_o[1:2, :] += jnp.sum(dy, axis=0, keepdims=True)
            small_o[2:3, :] += jnp.sum(db.astype(F32), axis=0, keepdims=True)
            return carry

        lax.fori_loop(0, rows_n // CH, run, 0, unroll=min(4, rows_n // CH))

    back(0, QRY_LEN, ogq, qlen[step], 0)
    back(QRY_LEN, PASS_LEN, ogp, plen[step], 1)


def loss_and_second_norm(units, target, column_id, mean, qlen, plen, ogq, ogp, xh2, rs2, n2g):
    seqs = qlen.shape[0]
    width = ogq.shape[1]
    rows = seqs * PAIR_LEN
    whole = lambda shape: pl.BlockSpec(shape, lambda i: (0,) * len(shape))
    smem = pl.BlockSpec(memory_space=pltpu.SMEM)
    row_block = lambda n, w: pl.BlockSpec((n, w), lambda i: (i, 0))
    return pl.pallas_call(
        loss_kernel,
        grid=(seqs,),
        in_specs=[
            smem, smem, *[whole(t.shape) for t in units], whole(target.shape), whole(column_id.shape), whole(mean.shape),
            row_block(QRY_LEN, width), row_block(PASS_LEN, width), row_block(PAIR_LEN, width),
            row_block(PAIR_LEN, 1), whole((width,)),
        ],
        out_specs=[row_block(PAIR_LEN, width), row_block(PAIR_LEN, width), whole((8, width)), whole((1, 1))],
        out_shape=[
            pltpu.HBM((rows, width), BF16),
            pltpu.HBM((rows, width), F32),
            jax.ShapeDtypeStruct((8, width), F32),
            jax.ShapeDtypeStruct((1, 1), F32),
        ],
        scratch_shapes=[pltpu.VMEM((8, width), F32)],
        compiler_params=pltpu.CompilerParams(
            dimension_semantics=("arbitrary",), vmem_limit_bytes=16 * MIB
        ),
        cost_estimate=kernel_cost(8),
        name="loss_norm_back",
    )(qlen, plen, *units, target, column_id, mean, *map(in_hbm, (ogq, ogp, xh2)), rs2, n2g)


def ffn_back_kernel(dz, dr2, gp, wd, wi, du_o, bi_o, acc):
    step = pl.program_id(0)
    du = (nt(dz[...], wd[...]) * gp[...].astype(F32)).astype(BF16)
    du_o[...] = du
    bi_o[...] = jnp.sum(du.astype(F32), axis=0, keepdims=True)
    part = nt(du, wi[...])

    @pl.when(step == 0)
    def _():
        acc[...] = dr2[...] + part

    @pl.when(step > 0)
    def _():
        acc[...] += part


def ffn_back(dz, dr2, gp, wd, wi, first, last, into):
    rows, width = dz.shape
    fb = gp.shape[1] // 6
    steps = last - first
    skip = first
    whole = lambda shape: pl.BlockSpec(shape, lambda i: (0,) * len(shape))
    earlier = [] if into is None else [into]

    def body(*refs):
        ffn_back_kernel(*refs[:5], *refs[5 + len(earlier) :])

    return pl.pallas_call(
        body,
        grid=(steps,),
        in_specs=[
            whole((rows, width)), whole((rows, width)),
            pl.BlockSpec((rows, fb), lambda i: (0, i + skip)),
            pl.BlockSpec((fb, width), lambda i: (i + skip, 0)),
            pl.BlockSpec((width, fb), lambda i: (0, i + skip)),
        ]
        + [pl.BlockSpec(memory_space=pl.ANY)] * len(earlier),
        out_specs=[
            pl.BlockSpec((rows, fb), lambda i: (0, i + skip)),
            pl.BlockSpec((1, fb), lambda i: (0, i)),
            whole((rows, width)),
        ],
        out_shape=[
            pltpu.HBM(gp.shape, BF16),
            jax.ShapeDtypeStruct((1, steps * fb), F32),
            jax.ShapeDtypeStruct((rows, width), F32),
        ],
        input_output_aliases={5 + n: n for n in range(len(earlier))},
        compiler_params=pltpu.CompilerParams(
            dimension_semantics=("arbitrary",), vmem_limit_bytes=28 * MIB
        ),
        cost_estimate=kernel_cost(10),
        name="ffn_back",
    )(dz, dr2, in_hbm(gp), in_hbm(wd), in_hbm(wi), *earlier)


def first_norm_back_kernel(dh_ref, xh1, rs1, n1g, wo, dr1_o, da_o, do_o, small_o):
    CH = 64

    @pl.when(pl.program_id(0) == 0)
    def _():
        small_o[...] = jnp.zeros_like(small_o)

    def run(n, carry):
        rows = pl.ds(pl.multiple_of(n * CH, CH), CH)
        dh = dh_ref[rows, :]
        xhat = xh1[rows, :].astype(F32)
        dyg = dh * n1g[...]
        m1 = jnp.mean(dyg, axis=-1, keepdims=True)
        m2 = jnp.mean(dyg * xhat, axis=-1, keepdims=True)
        dr = rs1[rows, :] * (dyg - m1 - xhat * m2)
        db = dr.astype(BF16)
        dr1_o[rows, :] = dr
        da_o[rows, :] = db
        small_o[0:1, :] += jnp.sum(dh * xhat, axis=0, keepdims=True)
        small_o[1:2, :] += jnp.sum(dh, axis=0, keepdims=True)
        small_o[2:3, :] += jnp.sum(db.astype(F32), axis=0, keepdims=True)
        return carry

    lax.fori_loop(0, dh_ref.shape[0] // CH, run, 0, unroll=3)
    do_o[...] = nt(da_o[...], wo[...]).astype(BF16)


def first_norm_back(dh, xh1, rs1, n1g, wo):
    rows, width = dh.shape
    step = PAIR_LEN
    whole = lambda shape: pl.BlockSpec(shape, lambda i: (0,) * len(shape))
    block = lambda w: pl.BlockSpec((step, w), lambda i: (i, 0))
    return pl.pallas_call(
        first_norm_back_kernel,
        grid=(rows // step,),
        in_specs=[block(width), block(width), block(1), whole((width,)), whole((width, width))],
        out_specs=[block(width), block(width), block(width), whole((8, width))],
        out_shape=[
            pltpu.HBM((rows, width), F32),
            pltpu.HBM((rows, width), BF16),
            pltpu.HBM((rows, width), BF16),
            jax.ShapeDtypeStruct((8, width), F32),
        ],
        compiler_params=pltpu.CompilerParams(
            dimension_semantics=("arbitrary",), vmem_limit_bytes=24 * MIB
        ),
        cost_estimate=kernel_cost(8),
        name="first_norm_back",
    )(dh, in_hbm(xh1), rs1, n1g, in_hbm(wo))


def down_grad_kernel(half, g, dz, out):
    out[...] = tn(g[...], dz[...]).astype(BF16)


def down_grad(half, g, dz):
    rows, width = dz.shape
    ff = g.shape[1]
    blocks = 2
    size = ff // 2 // blocks
    return pl.pallas_call(
        down_grad_kernel,
        grid_spec=pltpu.PrefetchScalarGridSpec(
            num_scalar_prefetch=1,
            grid=(blocks,),
            in_specs=[
                pl.BlockSpec((rows, size), lambda n, half: (0, half[0] * blocks + n)),
                pl.BlockSpec((rows, width), lambda n, half: (0, 0)),
            ],
            out_specs=pl.BlockSpec((size, width), lambda n, half: (n, 0)),
        ),
        out_shape=jax.ShapeDtypeStruct((ff // 2, width), BF16),
        compiler_params=pltpu.CompilerParams(
            dimension_semantics=("arbitrary",), vmem_limit_bytes=30 * MIB
        ),
        cost_estimate=kernel_cost(5),
        name="down_grad",
    )(half, in_hbm(g), in_hbm(dz))


def in_grad_kernel(half, h, o, du, da, out):
    width = h.shape[1]
    steps = (out.shape[1] - width // 2) // width
    for n in range(steps):

        @pl.when(pl.program_id(0) == n)
        def _():
            out[:, n * width : (n + 1) * width] = tn(h[...], du[...]).astype(BF16)

    @pl.when(pl.program_id(0) == steps)
    def _():
        out[:, steps * width :] = tn(o[...], da[...]).astype(BF16)


def in_grad(half, h, o, du, da):
    rows, width = h.shape
    steps = du.shape[1] // 2 // width
    cols = steps * width + width // 2
    whole = lambda shape: pl.BlockSpec(shape, lambda n, half: (0, 0))
    return pl.pallas_call(
        in_grad_kernel,
        grid_spec=pltpu.PrefetchScalarGridSpec(
            num_scalar_prefetch=1,
            grid=(steps + 1,),
            in_specs=[
                whole((rows, width)),
                whole((rows, width)),
                pl.BlockSpec((rows, width), lambda n, half: (0, half[0] * steps + jnp.minimum(n, steps - 1))),
                pl.BlockSpec((rows, width // 2), lambda n, half: (0, half[0])),
            ],
            out_specs=whole((width, cols)),
        ),
        out_shape=jax.ShapeDtypeStruct((width, cols), BF16),
        compiler_params=pltpu.CompilerParams(
            dimension_semantics=("arbitrary",), vmem_limit_bytes=34 * MIB
        ),
        cost_estimate=kernel_cost(6),
        name="in_grad",
    )(half, *map(in_hbm, (h, o, du, da)))


def proj_grad_kernel(half, x, d, dk, out):
    width = x.shape[1]
    out[:, width:] = tn(x[...], dk[0]).astype(BF16)
    out[:, :width] = tn(x[...], d[0]).astype(BF16)


def proj_grad(half, x, d):
    rows, width = x.shape
    size = width // 2
    return pl.pallas_call(
        proj_grad_kernel,
        grid_spec=pltpu.PrefetchScalarGridSpec(
            num_scalar_prefetch=1,
            grid=(1,),
            in_specs=[
                pl.BlockSpec((rows, width), lambda n, half: (0, 0)),
                pl.BlockSpec((1, rows, width), lambda n, half: (2 * half[0], 0, 0)),
                pl.BlockSpec((1, rows, size), lambda n, half: (1, 0, half[0])),
            ],
            out_specs=pl.BlockSpec((width, 3 * size), lambda n, half: (0, 0)),
        ),
        out_shape=jax.ShapeDtypeStruct((width, 3 * size), BF16),
        compiler_params=pltpu.CompilerParams(
            dimension_semantics=("arbitrary",), vmem_limit_bytes=28 * MIB
        ),
        cost_estimate=kernel_cost(4),
        name="proj_grad",
    )(half, in_hbm(x), in_hbm(d), in_hbm(d))


def attention_back_kernel(
    qlen, plen, q, k, v, o, do, lse,
    d_o, small_o,
    kmask, lse_p, lse_q, delta_p, delta_q,
    *, first_head,
):
    step = pl.program_id(0)
    width = q.shape[1]
    pairs = width // 128
    lane = lax.broadcasted_iota(jnp.int32, (1, 128), 1)
    low = (lane < 64).astype(F32)
    lanes = (low, 1.0 - low)
    ones = ((lane == 64).astype(F32), (lane == 0).astype(F32))
    q_gain = [(t * 0.125).astype(BF16) for t in lanes]
    keep = [t.astype(BF16) for t in lanes]
    one = [t.astype(BF16) for t in ones]

    q_valid = lax.broadcasted_iota(jnp.int32, (QRY_LEN, 128), 0) < qlen[step]
    p_valid = lax.broadcasted_iota(jnp.int32, (PASS_LEN, 128), 0) < plen[step]
    for side in range(2):
        kmask[side, :QRY_LEN, :] = jnp.where(q_valid, 0.0, NEG * ones[side]).astype(BF16)
        kmask[side, QRY_LEN:, :] = jnp.where(p_valid, 0.0, NEG * ones[side]).astype(BF16)

    q_rows, p_rows = pl.ds(0, QRY_LEN), pl.ds(QRY_LEN, PASS_LEN)
    head_of = (
        lax.broadcasted_iota(jnp.int32, (16, width), 1) // 64
        == lax.broadcasted_iota(jnp.int32, (16, width), 0)
    ).astype(F32).astype(BF16)
    for rows, lse_t, delta_t in ((q_rows, lse_q, delta_q), (p_rows, lse_p, delta_p)):
        lse_t[...] = jnp.transpose(lse[rows, :])
        prod = do[rows, :].astype(F32) * o[rows, :].astype(F32)
        hi = prod.astype(BF16)
        lo = (prod - hi.astype(F32)).astype(BF16)
        delta_t[...] = nt(head_of, hi) + nt(head_of, lo)

    def attend(pair, carry):
        cols = pl.ds(pl.multiple_of(pair * 128, 128), 128)
        for rows, lse_t, delta_t in ((q_rows, lse_q, delta_q), (p_rows, lse_p, delta_p)):
            qp, kp, vp, dop = q[rows, cols], k[rows, cols], v[rows, cols], do[rows, cols]
            qm = [qp * q_gain[side] for side in range(2)]
            km = [kp * q_gain[side] for side in range(2)]
            dm = [dop * keep[side] for side in range(2)]
            st = [nt(kp * keep[side] + kmask[side, rows, :], qm[side] + one[side]) for side in range(2)]
            dpt = [nt(vp, dm[side]) for side in range(2)]
            pt = [
                jnp.exp(st[side] - lse_t[pl.ds(first_head + 2 * pair + side, 1), :]) for side in range(2)
            ]
            dst = [
                (pt[side] * (dpt[side] - delta_t[pl.ds(2 * pair + side, 1), :])).astype(BF16) for side in range(2)
            ]
            d_o[2, rows, cols] = sum(nn(pt[side].astype(BF16), dm[side]) for side in range(2)).astype(BF16)
            d_o[1, rows, cols] = sum(nn(dst[side], qm[side]) for side in range(2)).astype(BF16)
            d_o[0, rows, cols] = sum(tn(dst[side], km[side]) for side in range(2)).astype(BF16)
        return carry

    lax.fori_loop(0, pairs, attend, 0, unroll=pairs)

    @pl.when(step == 0)
    def _():
        small_o[...] = jnp.zeros_like(small_o)

    small_o[0:1, :] += jnp.sum(d_o[0].astype(F32), axis=0, keepdims=True)
    small_o[1:2, :] += jnp.sum(d_o[2].astype(F32), axis=0, keepdims=True)


def attention_back(qlen, plen, q, k, v, o, do, lse, part, parts, into):
    seqs = qlen.shape[0]
    rows, full = q.shape
    width = full // parts
    whole = lambda shape: pl.BlockSpec(shape, lambda i: (0,) * len(shape))
    smem = pl.BlockSpec(memory_space=pltpu.SMEM)
    block = pl.BlockSpec((PAIR_LEN, width), lambda i: (i, part))
    kernel = functools.partial(attention_back_kernel, first_head=part * width // 64)
    earlier = [] if into is None else [into]

    def body(*refs):
        kernel(*refs[:8], *refs[8 + len(earlier) :])

    return pl.pallas_call(
        body,
        grid=(seqs,),
        in_specs=[smem, smem]
        + [block] * 5
        + [pl.BlockSpec((PAIR_LEN, 128), lambda i: (i, 0))]
        + [pl.BlockSpec(memory_space=pl.ANY)] * len(earlier),
        out_specs=[pl.BlockSpec((3, PAIR_LEN, width), lambda i: (0, i, part)), whole((8, width))],
        out_shape=[pltpu.HBM((3, rows, full), BF16), jax.ShapeDtypeStruct((8, width), F32)],
        input_output_aliases={8 + n: n for n in range(len(earlier))},
        scratch_shapes=[
            pltpu.VMEM((2, PAIR_LEN, 128), BF16),
            pltpu.VMEM((128, PASS_LEN), F32),
            pltpu.VMEM((128, QRY_LEN), F32),
            pltpu.VMEM((16, PASS_LEN), F32),
            pltpu.VMEM((16, QRY_LEN), F32),
        ],
        compiler_params=pltpu.CompilerParams(
            dimension_semantics=("arbitrary",), vmem_limit_bytes=52 * MIB
        ),
        cost_estimate=kernel_cost(10),
        name="attention_back",
    )(qlen, plen, q, k, v, o, do, lse, *earlier)


def input_grad_kernel(dr1, d, wq, wk, wv, gq_o, gp_o):
    grad = dr1[...] + nt(d[0], wq[...]) + nt(d[1], wk[...]) + nt(d[2], wv[...])
    gq_o[...] = grad[:QRY_LEN]
    gp_o[...] = grad[QRY_LEN:]


def input_grad(dr1, d, wq, wk, wv):
    rows, width = dr1.shape
    seqs = rows // PAIR_LEN
    block = pl.BlockSpec((PAIR_LEN, width), lambda i: (i, 0))
    weight = pl.BlockSpec((width, width), lambda i: (0, 0))
    return pl.pallas_call(
        input_grad_kernel,
        grid=(seqs,),
        in_specs=[block, pl.BlockSpec((3, PAIR_LEN, width), lambda i: (0, i, 0))] + [weight] * 3,
        out_specs=[
            pl.BlockSpec((QRY_LEN, width), lambda i: (i, 0)),
            pl.BlockSpec((PASS_LEN, width), lambda i: (i, 0)),
        ],
        out_shape=[
            jax.ShapeDtypeStruct((seqs * QRY_LEN, width), F32),
            jax.ShapeDtypeStruct((seqs * PASS_LEN, width), F32),
        ],
        compiler_params=pltpu.CompilerParams(
            dimension_semantics=("arbitrary",), vmem_limit_bytes=26 * MIB
        ),
        cost_estimate=kernel_cost(10),
        name="input_grad",
    )(*map(in_hbm, (dr1, d, wq, wk, wv)))


def widen(out, cols, value):
    out[:, cols[0] : cols[1]] = value.astype(F32)


def place_down_kernel(bit, mine, other, out):
    half = pl.program_id(0)

    @pl.when(half == 0)
    def _():
        out[...] = mine[...].astype(F32)

    @pl.when(half == 1)
    def _():
        out[...] = other[...].astype(F32)


def place_down(bit, mine, other):
    rows, cols = mine.shape
    chunks = 4
    step = rows // chunks
    return pl.pallas_call(
        place_down_kernel,
        grid_spec=pltpu.PrefetchScalarGridSpec(
            num_scalar_prefetch=1,
            grid=(2, chunks),
            in_specs=[
                pl.BlockSpec((step, cols), lambda h, n, bit: (jnp.where(h == 0, n, chunks - 1), 0)),
                pl.BlockSpec((step, cols), lambda h, n, bit: (jnp.where(h == 1, n, 0), 0)),
            ],
            out_specs=pl.BlockSpec((step, cols), lambda h, n, bit: ((h ^ bit[0]) * chunks + n, 0)),
        ),
        out_shape=jax.ShapeDtypeStruct((2 * rows, cols), F32),
        compiler_params=pltpu.CompilerParams(
            dimension_semantics=("arbitrary", "arbitrary"), vmem_limit_bytes=16 * MIB
        ),
        cost_estimate=kernel_cost(5),
        name="place_down",
    )(bit, mine, other)


def place_columns(bit, sums, widths, write, name):
    rows = sums[0][0].shape[0]
    chunks = 4
    step = rows // chunks
    arrays = [a for pair in sums for a in pair]

    def kernel(bit, *refs):
        ins, outs = refs[: len(arrays)], refs[len(arrays) :]
        pairs = [(ins[2 * n], ins[2 * n + 1]) for n in range(len(sums))]

        @pl.when(bit[0] == 0)
        def _():
            write(outs, pairs)

        @pl.when(bit[0] == 1)
        def _():
            write(outs, [p[::-1] for p in pairs])

    return pl.pallas_call(
        kernel,
        grid_spec=pltpu.PrefetchScalarGridSpec(
            num_scalar_prefetch=1,
            grid=(chunks,),
            in_specs=[pl.BlockSpec((step, a.shape[1]), lambda n, bit: (n, 0)) for a in arrays],
            out_specs=[pl.BlockSpec((step, w), lambda n, bit: (n, 0)) for w in widths],
        ),
        out_shape=[jax.ShapeDtypeStruct((rows, w), F32) for w in widths],
        compiler_params=pltpu.CompilerParams(
            dimension_semantics=("arbitrary",), vmem_limit_bytes=20 * MIB
        ),
        cost_estimate=kernel_cost(5),
        name=name,
    )(bit, *arrays)


def write_in(outs, pairs):
    for n, half in enumerate(pairs[0]):
        at = 0
        for out in outs:
            size = out.shape[1] // 2
            widen(out, (n * size, (n + 1) * size), half[:, at : at + size])
            at += size


def write_proj(outs, pairs):
    size = outs[0].shape[1]
    for n, half in enumerate(pairs[0]):
        widen(outs[2 * n], (0, size), half[:, :size])
        widen(outs[1], (n * size // 2, (n + 1) * size // 2), half[:, size:])


IN_FLIGHT = 5


def swap_with(value, mask, device_count):
    return lax.ppermute(value, AXES, [(i, i ^ mask) for i in range(device_count)])


def far_groups(device_count):
    masks, mask = [], 4
    while mask < device_count // 2:
        masks.append(mask)
        mask *= 2
    return [masks[n : n + 2] for n in range(0, len(masks), 2)]


def combos_of(group):
    combos = [0]
    for mask in reversed(group):
        combos = combos + [c ^ mask for c in combos]
    return combos


def gather_relative(value, device_count):
    groups = [[device_count // 2, 2]] + far_groups(device_count) + [[1]]
    relative = [0]
    for n, group in enumerate(groups):
        combos = combos_of(group)
        got = [value] + [swap_with(value, c, device_count) for c in combos[1:]]
        relative = [c ^ r for c in combos for r in relative]
        if n < len(groups) - 1:
            value = jnp.concatenate(got, axis=0)
    return got, relative


def whole_call(kernel, scalars, arrays, outs, name):
    spec = lambda shape: pl.BlockSpec(shape, lambda i, s: (0, 0))
    return pl.pallas_call(
        kernel,
        grid_spec=pltpu.PrefetchScalarGridSpec(
            num_scalar_prefetch=1,
            grid=(1,),
            in_specs=[spec(a.shape) for a in arrays],
            out_specs=[spec(o) for o in outs],
        ),
        out_shape=[jax.ShapeDtypeStruct(o, BF16) for o in outs],
        compiler_params=pltpu.CompilerParams(vmem_limit_bytes=24 * MIB),
        cost_estimate=kernel_cost(1),
        name=name,
    )(scalars, *arrays)


def fold(tuples, places, parts, ways=2):
    rows = tuples[0][0].shape[0] // ways
    widths = [sum(c1 - c0 for _, c0, c1 in p) for p in parts]
    arrays = [a for one in tuples for a in one]

    def add(values):
        total = values[0].astype(F32)
        for value in values[1:]:
            total = total + value.astype(F32)
        return total.astype(BF16)

    if rows % 16:
        results = []
        for part, place in zip(parts, places):
            total = jnp.concatenate([add([a[:, c0:c1] for a in tuples[p]]) for p, c0, c1 in part], 1)
            results.append(
                [lax.dynamic_slice_in_dim(total, (place ^ n) * rows, rows, 0) for n in range(ways)]
            )
        return results

    def kernel(place, *refs):
        taken, ref_tuples = 0, []
        for one in tuples:
            ref_tuples.append(refs[taken : taken + len(one)])
            taken += len(one)
        outs = refs[taken:]
        for m, part in enumerate(parts):
            for n in range(ways):
                at = pl.ds(pl.multiple_of((place[m] ^ n) * rows, 16), rows)
                col = 0
                for p, c0, c1 in part:
                    outs[ways * m + n][:, col : col + c1 - c0] = add([r[at, c0:c1] for r in ref_tuples[p]])
                    col += c1 - c0

    got = whole_call(
        kernel, jnp.stack(places), arrays, [(rows, w) for w in widths for _ in range(ways)], "fold"
    )
    return [got[ways * m : ways * (m + 1)] for m in range(len(parts))]


def unfold(tuples, places, parts):
    rows = tuples[0][0].shape[0]
    ways = len(tuples[0])
    widths = [sum(c1 - c0 for _, c0, c1 in p) for p in parts]
    if rows % 16:
        joined = [
            jnp.concatenate([lax.select_n(s, *[t[b ^ n] for n in range(ways)]) for b in range(ways)], 0)
            if ways > 2
            else jnp.where(s == 1, jnp.concatenate([t[1], t[0]], 0), jnp.concatenate([t[0], t[1]], 0))
            for t, s in zip(tuples, places)
        ]
        return [jnp.concatenate([joined[p][:, c0:c1] for p, c0, c1 in part], 1) for part in parts]

    def kernel(place, *refs):
        outs = refs[ways * len(tuples) :]
        for m, part in enumerate(parts):
            col = 0
            for p, c0, c1 in part:
                for n in range(ways):
                    at = pl.ds(pl.multiple_of((place[p] ^ n) * rows, 16), rows)
                    outs[m][at, col : col + c1 - c0] = refs[ways * p + n][:, c0:c1]
                col += c1 - c0

    return whole_call(
        kernel, jnp.stack(places), [a for t in tuples for a in t], [(ways * rows, w) for w in widths], "unfold"
    )


def reduction(send, kept, split, wide, me, device_count):
    top = device_count // 2
    far = far_groups(device_count)
    if not wide:
        far = [[mask] for group in far for mask in group]
    cols = send.shape[1]
    both = [[(0, 0, split)], [(0, split, cols)]]
    apart = [[(0, 0, split)], [(1, 0, cols - split)]]
    merged = [[(0, 0, split), (1, 0, cols - split)]]
    alone = [[(0, 0, cols)]]

    def place(group):
        pos = jnp.int32(0)
        for mask in group:
            pos = 2 * pos + ((me & mask) != 0).astype(jnp.int32)
        return pos

    got = yield [(send, 1)]
    sums = [(kept[0], got[0])]
    for masks, parts in (((top, 2), both), ((2, top), apart)):
        cut = fold(sums, [place([m]) for m in masks], parts)
        got = yield [(c[1], m) for c, m in zip(cut, masks)]
        sums = [(c[0], g) for c, g in zip(cut, got)]
    for n, group in enumerate(far):
        combos = combos_of(group)
        (cut,) = fold(sums, [place(group)], alone if n else merged, len(combos))
        got = yield list(zip(cut[1:], combos[1:]))
        sums = [(cut[0], *got)]
    total = sums[0][0].astype(F32)
    for value in sums[0][1:]:
        total = total + value.astype(F32)
    mine = total.astype(BF16)
    for group in reversed(far):
        got = yield [(mine, c) for c in combos_of(group)[1:]]
        last = group is far[0]
        mine = unfold([(mine, *got)], [place(group)], both if last else alone)
        mine = mine if last else mine[0]
    for masks, parts in (((2, top), apart), ((top, 2), merged)):
        got = yield [(p, m) for p, m in zip(mine, masks)]
        mine = unfold(list(zip(mine, got)), [place([m]) for m in masks], parts)
    (got,) = yield [(mine[0], 1)]
    return mine[0], got


def small_sum(values, device_count):
    mask = 1
    while mask < device_count:
        (got,) = yield [(values, mask)]
        values = values + got
        mask *= 2
    return values


class Line:
    def __init__(self, steps, device_count):
        self.steps = steps
        self.count = device_count
        self.sum = None
        self.want = next(steps)

    def take(self, got):
        try:
            self.want = self.steps.send(got)
        except StopIteration as end:
            self.want, self.sum = None, end.value


def slot(lines, work=None, values=(), kept=None):
    flying = []
    for n in lines:
        if n.want is not None and sum(len(f.want) for f in flying) + len(n.want) <= IN_FLIGHT:
            flying.append(n)
    lines = flying
    arrays = [[a for a, _ in n.want] for n in lines]
    arrays, values = lax.optimization_barrier((arrays, tuple(values)))
    got = [[swap_with(a, m, n.count) for a, (_, m) in zip(sends, n.want)] for sends, n in zip(arrays, lines)]
    out = work(*values) if work is not None else ()
    got, out = lax.optimization_barrier((got, out))
    if kept is not None:
        kept.append(out)
    for n, g in zip(lines, got):
        n.take(g)
    return out


def body(
    query_tokens,
    passage_tokens,
    query_lengths,
    passage_lengths,
    positives,
    w_query,
    b_query,
    w_key,
    w_value,
    b_value,
    w_out,
    b_out,
    norm1_gain,
    norm1_bias,
    w_in,
    b_in,
    w_down,
    b_down,
    norm2_gain,
    norm2_bias,
    query_out_grad,
    passage_out_grad,
):
    seqs = query_lengths.shape[0]
    width = query_tokens.shape[1]
    device_count = lax.axis_size(AXES)
    my_index = lax.axis_index(AXES)
    params = dict(
        w_query=w_query, b_query=b_query, w_key=w_key, w_value=w_value, b_value=b_value, w_out=w_out,
        b_out=b_out, norm1_gain=norm1_gain, norm1_bias=norm1_bias, w_in=w_in, b_in=b_in, w_down=w_down,
        b_down=b_down, norm2_gain=norm2_gain, norm2_bias=norm2_bias,
    )
    (
        query_out, passage_out, q, k, v, o, lse, xhat1, rstd1, h1b, g, gelu_slope, x_rows, xhat2, rstd2, unit, mean,
    ) = forward(query_tokens, passage_tokens, query_lengths, passage_lengths, params)
    units, relative = gather_relative(unit, device_count)
    owner = jnp.array(relative, jnp.int32) ^ my_index
    ids = (owner[:, None] * seqs + jnp.arange(seqs, dtype=jnp.int32)[None, :]).reshape(-1)
    ids = jnp.repeat(ids, 2)
    target = positives[ids][:, None]
    dz, dr2, small2, loss_sum = loss_and_second_norm(
        units, target, ids[None, :], mean, query_lengths, passage_lengths, query_out_grad, passage_out_grad,
        xhat2, rstd2, norm2_gain,
    )
    loss = loss_sum[0, 0] / (seqs * device_count)
    core = (my_index & 1).astype(jnp.int32)[None]
    other = 1 - core

    def start_line(lines, make, values, wide=False):
        kept = []
        send = slot(lines, lambda *v: make(other, *v), values)
        split = (send.shape[1] + 255) // 256 * 128
        new = Line(reduction(send, kept, split, wide, my_index, device_count), device_count)
        slot(lines + [new], lambda *v: make(core, *v), values, kept)
        return new

    down = start_line([], lambda half, d: down_grad(half, g, d), (dz,))
    acc, du, grad_b_in = dr2, None, []
    for first, last in ((0, 4), (4, 6)):
        du, bias, acc = slot(
            [down],
            lambda *arrays: ffn_back(*arrays[:5], first, last, arrays[5] if first else None),
            (dz, acc, gelu_slope, w_down, w_in, *([du] if first else [])),
        )
        grad_b_in.append(bias)
    dr1, da, do, small1 = slot([down], first_norm_back, (acc, xhat1, rstd1, norm1_gain, w_out))
    up = start_line([down], in_grad, (h1b, o, du, da))
    grads, smalls = None, []
    for part in range(3):
        grads, some = slot(
            [down, up],
            lambda *arrays: attention_back(
                query_lengths, passage_lengths, *arrays[:6], part, 3, arrays[6] if part else None
            ),
            (q, k, v, o, do, lse, *([grads] if part else [])),
        )
        smalls.append(some)
    small0 = jnp.concatenate(smalls, 1)
    packed = jnp.concatenate(
        [small0, small1, small2, jnp.concatenate(grad_b_in, 1).reshape(-1, width)], 0
    )
    small = Line(small_sum(packed, device_count), device_count)
    proj = start_line([down, up, small], proj_grad, (x_rows, grads), wide=True)
    lines = [down, up, proj, small]
    query_input_grad, passage_input_grad = slot(lines, input_grad, (dr1, grads, w_query, w_key, w_value))
    bit = core
    grad_w_down = None
    grad_w_in = None
    while any(n.want is not None for n in lines):
        if down.sum is not None and grad_w_down is None:
            grad_w_down = slot(lines, place_down, (bit, *down.sum))
        elif up.sum is not None and grad_w_in is None:
            grad_w_in, grad_w_out = slot(
                lines,
                lambda bit, *pair: place_columns(bit, [pair], (g.shape[1], width), write_in, "place_in"),
                (bit, *up.sum),
            )
        else:
            slot(lines)
    grad_w_query, grad_w_key, grad_w_value = place_columns(
        bit, [proj.sum], (width,) * 3, write_proj, "place_proj"
    )
    packed = small.sum
    return (
        query_out,
        passage_out,
        query_input_grad,
        passage_input_grad,
        loss,
        grad_w_query,
        packed[0],
        grad_w_key,
        grad_w_value,
        packed[1],
        grad_w_out,
        packed[10],
        packed[8],
        packed[9],
        grad_w_in,
        packed[24:].reshape(-1),
        grad_w_down,
        packed[18],
        packed[16],
        packed[17],
    )


def solution(mesh):
    placed = (
        P(("stream", "batch"), None),
        P(("stream", "batch"), None),
        P(("stream", "batch")),
        P(("stream", "batch")),
        P(),
        P(),
        P(),
        P(),
        P(),
        P(),
        P(),
        P(),
        P(),
        P(),
        P(),
        P(),
        P(),
        P(),
        P(),
        P(),
        P(("stream", "batch"), None),
        P(("stream", "batch"), None),
    )
    return jax.shard_map(
        body,
        mesh=mesh,
        in_specs=placed,
        out_specs=(
            P(("stream", "batch"), None),
            P(("stream", "batch"), None),
            P(("stream", "batch"), None),
            P(("stream", "batch"), None),
            P(),
            P(),
            P(),
            P(),
            P(),
            P(),
            P(),
            P(),
            P(),
            P(),
            P(),
            P(),
            P(),
            P(),
            P(),
            P(),
        ),
        check_vma=False,
    )
```

```python
import functools

import jax
import jax.numpy as jnp
from jax import lax
from jax.experimental import pallas as pl
from jax.experimental.pallas import tpu as pltpu
from jax.sharding import PartitionSpec as P

HEADS = 12
QRY_LEN = 64
PASS_LEN = 512
PAIR_LEN = QRY_LEN + PASS_LEN
LOGIT_SCALE = 0.01
EPS = 1e-06
NEG = -1e30
F32 = jnp.float32
BF16 = jnp.bfloat16
AXES = ("stream", "batch")
MIB = 1024 * 1024
VMEM_LIMIT = 60 * MIB


def kernel_cost(us):
    return pl.CostEstimate(flops=us * 1_000_000_000, bytes_accessed=1_000_000, transcendentals=0)


def nn(a, b):
    return lax.dot_general(a, b, (((1,), (0,)), ((), ())), preferred_element_type=F32)


def nt(a, b):
    return lax.dot_general(a, b, (((1,), (1,)), ((), ())), preferred_element_type=F32)


def tn(a, b):
    return lax.dot_general(a, b, (((0,), (0,)), ((), ())), preferred_element_type=F32)


def gelu_parts(u):
    cdf = 0.5 + 0.5 * lax.erf(u * 0.7071067811865476)
    bell = jnp.exp(-0.5 * (u * u))
    return u * cdf, cdf + u * (bell * 0.3989422804014327)


def forward_kernel(
    qlen, plen, xq, xp, wq_h, wk_h, wv_h, wo_h, wi_h, wd_h, bq, bv, bo, n1g, n1b, bi, bd, n2g, n2b,
    yq, yp, q_h, k_h, v_h, o_h, lse_o, xh1_h, rs1_o, h1b_h, g_h, gp_h, x_h, xh2_o, rs2_o, unit_o, mean_o,
    xs, wq, wk, wv, wo, wi, wd, acc, h1, kmask, units, q_o, k_o, v_o, o_o, xh1_o, h1b_o, g_o, gp_o, sems, out_sems,
):
    step = pl.program_id(0)
    width = xs.shape[1]
    copies = [
        pltpu.make_async_copy(src, dst, sems.at[n])
        for n, (src, dst) in enumerate(
            ((wq_h, wq), (wk_h, wk), (wv_h, wv), (wo_h, wo), (wi_h, wi), (wd_h, wd))
        )
    ]

    here = pl.ds(pl.multiple_of(step * PAIR_LEN, PAIR_LEN), PAIR_LEN)
    saved = (
        (q_o, q_h), (k_o, k_h), (v_o, v_h), (o_o, o_h), (xh1_o, xh1_h), (h1b_o, h1b_h), (g_o, g_h), (gp_o, gp_h),
        (xs, x_h),
    )
    saves = [pltpu.make_async_copy(src, dst.at[here], out_sems.at[n]) for n, (src, dst) in enumerate(saved)]

    def free(*which):
        @pl.when(step > 0)
        def _():
            for n in which:
                saves[n].wait()

    @pl.when(step == 0)
    def _():
        for c in copies:
            c.start()
        lse_o[...] = jnp.zeros_like(lse_o)

    def ready(n):
        @pl.when(step == 0)
        def _():
            copies[n].wait()

    free(0, 1, 2, 3, 8)
    xs[:QRY_LEN, :] = xq[...]
    xs[QRY_LEN:, :] = xp[...]
    saves[8].start()
    ready(0)
    q_o[...] = (nn(xs[...], wq[...]) + bq[...]).astype(BF16)
    ready(1)
    k_o[...] = nn(xs[...], wk[...]).astype(BF16)
    ready(2)
    v_o[...] = (nn(xs[...], wv[...]) + bv[...]).astype(BF16)
    for n in range(3):
        saves[n].start()

    lane = lax.broadcasted_iota(jnp.int32, (1, 128), 1)
    low = (lane < 64).astype(F32)
    lanes = (low, 1.0 - low)
    ones = ((lane == 64).astype(F32), (lane == 0).astype(F32))
    q_gain = [(v * 0.125).astype(BF16) for v in lanes]
    keep = [v.astype(BF16) for v in lanes]
    one = [v.astype(BF16) for v in ones]

    q_valid = lax.broadcasted_iota(jnp.int32, (QRY_LEN, 128), 0) < qlen[step]
    p_valid = lax.broadcasted_iota(jnp.int32, (PASS_LEN, 128), 0) < plen[step]
    for side in range(2):
        kmask[side, :QRY_LEN, :] = jnp.where(q_valid, 0.0, NEG * ones[side]).astype(BF16)
        kmask[side, QRY_LEN:, :] = jnp.where(p_valid, 0.0, NEG * ones[side]).astype(BF16)

    def attend(pair, carry):
        cols = pl.ds(pl.multiple_of(pair * 128, 128), 128)
        for rows in (pl.ds(0, QRY_LEN), pl.ds(QRY_LEN, PASS_LEN)):
            qp, kp, vp = q_o[rows, cols], k_o[rows, cols], v_o[rows, cols]
            mixed = []
            scores = [
                nt(qp * q_gain[side] + one[side], kp * keep[side] + kmask[side, rows, :]) for side in range(2)
            ]
            tops = [jnp.max(s, axis=1, keepdims=True) for s in scores]
            probs = [jnp.exp(s - top).astype(BF16) for s, top in zip(scores, tops)]
            outs = [nn(probs[side], vp * keep[side] + one[side]) for side in range(2)]
            for side in range(2):
                oe, top = outs[side], tops[side]
                total = oe[:, 64:65] if side == 0 else oe[:, 0:1]
                mixed.append(oe * (1.0 / total))
                lse = top + jnp.log(total)
                head = 2 * pair + side
                lse_o[rows, :] = jnp.where(lane == head, lse, lse_o[rows, :])
            o_o[rows, cols] = jnp.where(lane < 64, mixed[0], mixed[1]).astype(BF16)
        return carry

    lax.fori_loop(0, HEADS // 2, attend, 0, unroll=3)

    saves[3].start()
    ready(3)
    acc[...] = nn(o_o[...], wo[...])

    def norm(value):
        mean = jnp.mean(value, axis=-1, keepdims=True)
        c = value - mean
        rstd = lax.rsqrt(jnp.mean(c * c, axis=-1, keepdims=True) + EPS)
        return c * rstd, rstd

    CH = 64

    def first_norm(n, carry):
        rows = pl.ds(pl.multiple_of(n * CH, CH), CH)
        xhat, rstd = norm(xs[rows, :].astype(F32) + acc[rows, :] + bo[...])
        hid = xhat * n1g[...] + n1b[...]
        xh1_o[rows, :] = xhat.astype(BF16)
        rs1_o[rows, :] = rstd
        h1[rows, :] = hid
        h1b_o[rows, :] = hid.astype(BF16)
        return carry

    free(4, 5)
    lax.fori_loop(0, PAIR_LEN // CH, first_norm, 0, unroll=3)
    saves[4].start()
    saves[5].start()

    ready(4)
    ready(5)
    free(6, 7)
    g, slope = gelu_parts(nn(h1b_o[...], wi[...]) + bi[...])
    g_o[...] = g.astype(BF16)
    gp_o[...] = slope.astype(BF16)
    h1[...] += nn(g_o[...], wd[...])
    saves[6].start()
    saves[7].start()

    def second_norm(row0, rows_n, out, valid_n):
        def run(n, total):
            at = pl.multiple_of(n * CH, CH)
            rows = pl.ds(row0 + at, CH)
            xhat, rstd = norm(h1[rows, :] + bd[...])
            y = xhat * n2g[...] + n2b[...]
            xh2_o[rows, :] = xhat.astype(BF16)
            rs2_o[rows, :] = rstd
            out[pl.ds(at, CH), :] = y.astype(BF16)
            live = (lax.broadcasted_iota(jnp.int32, (CH, 1), 0) + at) < valid_n
            return total + jnp.sum(jnp.where(live, y, 0.0), axis=0, keepdims=True)

        total = lax.fori_loop(
            0, rows_n // CH, run, jnp.zeros((1, width), F32), unroll=min(4, rows_n // CH)
        )
        return total / valid_n.astype(F32)

    for kind, mean in enumerate(
        (
            second_norm(0, QRY_LEN, yq, qlen[step]),
            second_norm(QRY_LEN, PASS_LEN, yp, plen[step]),
        )
    ):
        at = pl.ds(2 * step + kind, 1)
        mean_o[at, :] = mean
        unit = mean * lax.rsqrt(jnp.sum(mean * mean, axis=-1, keepdims=True) + EPS)
        units[at, :] = unit

    @pl.when(step == pl.num_programs(0) - 1)
    def _():
        unit_o[...] = units[...].astype(BF16)
        for c in saves:
            c.wait()


def forward(xq, xp, qlen, plen, p):
    seqs = qlen.shape[0]
    width = xq.shape[1]
    ff = p["w_in"].shape[1]
    rows = seqs * PAIR_LEN
    whole = lambda shape: pl.BlockSpec(shape, lambda i: (0,) * len(shape))
    smem = pl.BlockSpec(memory_space=pltpu.SMEM)
    hbm = pl.BlockSpec(memory_space=pl.ANY)
    row_block = lambda n, w: pl.BlockSpec((n, w), lambda i: (i, 0))
    outs = [
        ((seqs * QRY_LEN, width), BF16, row_block(QRY_LEN, width)),
        ((seqs * PASS_LEN, width), BF16, row_block(PASS_LEN, width)),
        ((rows, width), BF16, hbm),
        ((rows, width), BF16, hbm),
        ((rows, width), BF16, hbm),
        ((rows, width), BF16, hbm),
        ((rows, 128), F32, row_block(PAIR_LEN, 128)),
        ((rows, width), BF16, hbm),
        ((rows, 1), F32, row_block(PAIR_LEN, 1)),
        ((rows, width), BF16, hbm),
        ((rows, ff), BF16, hbm),
        ((rows, ff), BF16, hbm),
        ((rows, width), BF16, hbm),
        ((rows, width), BF16, row_block(PAIR_LEN, width)),
        ((rows, 1), F32, row_block(PAIR_LEN, 1)),
        ((2 * seqs, width), BF16, whole((2 * seqs, width))),
        ((2 * seqs, width), F32, whole((2 * seqs, width))),
    ]
    return pl.pallas_call(
        forward_kernel,
        grid=(seqs,),
        in_specs=[smem, smem, row_block(QRY_LEN, width), row_block(PASS_LEN, width)]
        + [hbm] * 6
        + [whole((width,))] * 5
        + [whole((ff,))]
        + [whole((width,))] * 3,
        out_specs=[o[2] for o in outs],
        out_shape=[jax.ShapeDtypeStruct(o[0], o[1]) for o in outs],
        scratch_shapes=[
            pltpu.VMEM((PAIR_LEN, width), BF16),
            pltpu.VMEM((width, width), BF16),
            pltpu.VMEM((width, width), BF16),
            pltpu.VMEM((width, width), BF16),
            pltpu.VMEM((width, width), BF16),
            pltpu.VMEM((width, ff), BF16),
            pltpu.VMEM((ff, width), BF16),
            pltpu.VMEM((PAIR_LEN, width), F32),
            pltpu.VMEM((PAIR_LEN, width), F32),
            pltpu.VMEM((2, PAIR_LEN, 128), BF16),
            pltpu.VMEM((2 * seqs, width), F32),
            *[pltpu.VMEM((PAIR_LEN, width), BF16) for _ in range(6)],
            *[pltpu.VMEM((PAIR_LEN, ff), BF16) for _ in range(2)],
            pltpu.SemaphoreType.DMA((6,)),
            pltpu.SemaphoreType.DMA((9,)),
        ],
        compiler_params=pltpu.CompilerParams(
            dimension_semantics=("arbitrary",), vmem_limit_bytes=VMEM_LIMIT
        ),
        cost_estimate=kernel_cost(45),
        name="forward_layer",
    )(
        qlen, plen, xq, xp, p["w_query"], p["w_key"], p["w_value"], p["w_out"], p["w_in"], p["w_down"],
        p["b_query"], p["b_value"], p["b_out"], p["norm1_gain"],
        p["norm1_bias"], p["b_in"], p["b_down"], p["norm2_gain"],
        p["norm2_bias"],
    )


def in_hbm(array):
    return pltpu.with_memory_space_constraint(array, pltpu.HBM)


def loss_kernel(
    qlen, plen, units_0, units_1, positives, row_id, column_id, mean, ogq, ogp, xh2, rs2, n2g,
    dz_o, dr2_o, small_o, loss_o,
    de,
):
    step = pl.program_id(0)
    seqs = pl.num_programs(0)
    width = xh2.shape[1]
    mine = mean.shape[0]

    @pl.when(step == 0)
    def _():
        u = jnp.concatenate([units_0[...], units_1[...]], 0)
        n = u.shape[0]
        row = lax.broadcasted_iota(jnp.int32, (n, n), 0)
        col = lax.broadcasted_iota(jnp.int32, (n, n), 1)
        pairs = ((row & 1) == 0) & ((col & 1) == 1)
        logits = jnp.where(pairs, nt(u, u) / LOGIT_SCALE, NEG)
        top = jnp.max(logits, axis=1, keepdims=True)
        lse = top + jnp.log(jnp.sum(jnp.exp(logits - top), axis=1, keepdims=True))
        count = positives.shape[0]
        query = (row_id[...] == lax.broadcasted_iota(jnp.int32, (n, count), 1)).astype(F32).astype(BF16)
        passage = (positives[...] == column_id[...]).astype(F32).astype(BF16)
        hit = pairs & (nn(query, passage) > 0.5)
        chosen = jnp.sum(jnp.where(hit, logits, 0.0), axis=1, keepdims=True)
        is_query = (lax.broadcasted_iota(jnp.int32, (n, 1), 0) & 1) == 0
        loss_o[...] = jnp.sum(jnp.where(is_query, lse - chosen, 0.0), axis=0, keepdims=True)
        dc = jnp.where(pairs, (jnp.exp(logits - lse) - hit.astype(F32)) / LOGIT_SCALE, 0.0)
        both = (dc + jnp.transpose(dc)).astype(BF16)
        dn = nn(both[:16], u)[:mine]
        e = mean[...]
        square = jnp.sum(e * e, axis=-1, keepdims=True) + EPS
        grad = (dn - e * (jnp.sum(e * dn, axis=-1, keepdims=True) / square)) * lax.rsqrt(square)
        de[...] = jnp.zeros_like(de)
        de[:mine, :] = grad
        small_o[...] = jnp.zeros_like(small_o)

    CH = 64

    def back(row0, rows_n, grads, valid_n, kind):
        shift = de[pl.ds(2 * step + kind, 1), :] / valid_n.astype(F32)

        def run(n, carry):
            at = pl.multiple_of(n * CH, CH)
            rows = pl.ds(row0 + at, CH)
            live = (lax.broadcasted_iota(jnp.int32, (CH, 1), 0) + at) < valid_n
            dy = grads[pl.ds(at, CH), :].astype(F32) + jnp.where(live, shift, 0.0)
            xhat = xh2[rows, :].astype(F32)
            dyg = dy * n2g[...]
            m1 = jnp.mean(dyg, axis=-1, keepdims=True)
            m2 = jnp.mean(dyg * xhat, axis=-1, keepdims=True)
            dr = rs2[rows, :] * (dyg - m1 - xhat * m2)
            db = dr.astype(BF16)
            dr2_o[rows, :] = dr
            dz_o[rows, :] = db
            small_o[0:1, :] += jnp.sum(dy * xhat, axis=0, keepdims=True)
            small_o[1:2, :] += jnp.sum(dy, axis=0, keepdims=True)
            small_o[2:3, :] += jnp.sum(db.astype(F32), axis=0, keepdims=True)
            return carry

        lax.fori_loop(0, rows_n // CH, run, 0, unroll=min(4, rows_n // CH))

    back(0, QRY_LEN, ogq, qlen[step], 0)
    back(QRY_LEN, PASS_LEN, ogp, plen[step], 1)


def loss_and_second_norm(units, positives, row_id, column_id, mean, qlen, plen, ogq, ogp, xh2, rs2, n2g):
    seqs = qlen.shape[0]
    width = ogq.shape[1]
    rows = seqs * PAIR_LEN
    whole = lambda shape: pl.BlockSpec(shape, lambda i: (0,) * len(shape))
    smem = pl.BlockSpec(memory_space=pltpu.SMEM)
    row_block = lambda n, w: pl.BlockSpec((n, w), lambda i: (i, 0))
    return pl.pallas_call(
        loss_kernel,
        grid=(seqs,),
        in_specs=[
            smem, smem, *[whole(t.shape) for t in units], whole(positives.shape), whole(row_id.shape), whole(column_id.shape), whole(mean.shape),
            row_block(QRY_LEN, width), row_block(PASS_LEN, width), row_block(PAIR_LEN, width),
            row_block(PAIR_LEN, 1), whole((width,)),
        ],
        out_specs=[row_block(PAIR_LEN, width), row_block(PAIR_LEN, width), whole((8, width)), whole((1, 1))],
        out_shape=[
            pltpu.HBM((rows, width), BF16),
            pltpu.HBM((rows, width), F32),
            jax.ShapeDtypeStruct((8, width), F32),
            jax.ShapeDtypeStruct((1, 1), F32),
        ],
        scratch_shapes=[pltpu.VMEM((8, width), F32)],
        compiler_params=pltpu.CompilerParams(
            dimension_semantics=("arbitrary",), vmem_limit_bytes=16 * MIB
        ),
        cost_estimate=kernel_cost(8),
        name="loss_norm_back",
    )(qlen, plen, *units, positives, row_id, column_id, *map(in_hbm, (mean, ogq, ogp, xh2, rs2)), n2g)


def ffn_back_kernel(dz, dr2, gp, wd, wi, du_o, bi_o, acc):
    step = pl.program_id(0)
    du = (nt(dz[...], wd[...]) * gp[...].astype(F32)).astype(BF16)
    du_o[...] = du
    bi_o[...] = jnp.sum(du.astype(F32), axis=0, keepdims=True)
    part = nt(du, wi[...])

    @pl.when(step == 0)
    def _():
        acc[...] = dr2[...] + part

    @pl.when(step > 0)
    def _():
        acc[...] += part


def ffn_back(dz, dr2, gp, wd, wi, first, last, into):
    rows, width = dz.shape
    fb = gp.shape[1] // 6
    steps = last - first
    skip = first
    whole = lambda shape: pl.BlockSpec(shape, lambda i: (0,) * len(shape))
    earlier = [] if into is None else [into]

    def body(*refs):
        ffn_back_kernel(*refs[:5], *refs[5 + len(earlier) :])

    return pl.pallas_call(
        body,
        grid=(steps,),
        in_specs=[
            whole((rows, width)), whole((rows, width)),
            pl.BlockSpec((rows, fb), lambda i: (0, i + skip)),
            pl.BlockSpec((fb, width), lambda i: (i + skip, 0)),
            pl.BlockSpec((width, fb), lambda i: (0, i + skip)),
        ]
        + [pl.BlockSpec(memory_space=pl.ANY)] * len(earlier),
        out_specs=[
            pl.BlockSpec((rows, fb), lambda i: (0, i + skip)),
            pl.BlockSpec((1, fb), lambda i: (0, i)),
            whole((rows, width)),
        ],
        out_shape=[
            pltpu.HBM(gp.shape, BF16),
            jax.ShapeDtypeStruct((1, steps * fb), F32),
            jax.ShapeDtypeStruct((rows, width), F32),
        ],
        input_output_aliases={5 + n: n for n in range(len(earlier))},
        compiler_params=pltpu.CompilerParams(
            dimension_semantics=("arbitrary",), vmem_limit_bytes=28 * MIB
        ),
        cost_estimate=kernel_cost(10),
        name="ffn_back",
    )(in_hbm(dz), dr2 if earlier else in_hbm(dr2), *map(in_hbm, (gp, wd, wi)), *earlier)


def first_norm_back_kernel(dh_ref, xh1, rs1, n1g, wo, dr1_o, da_o, do_o, small_o):
    CH = 64

    @pl.when(pl.program_id(0) == 0)
    def _():
        small_o[...] = jnp.zeros_like(small_o)

    def run(n, carry):
        rows = pl.ds(pl.multiple_of(n * CH, CH), CH)
        dh = dh_ref[rows, :]
        xhat = xh1[rows, :].astype(F32)
        dyg = dh * n1g[...]
        m1 = jnp.mean(dyg, axis=-1, keepdims=True)
        m2 = jnp.mean(dyg * xhat, axis=-1, keepdims=True)
        dr = rs1[rows, :] * (dyg - m1 - xhat * m2)
        db = dr.astype(BF16)
        dr1_o[rows, :] = dr
        da_o[rows, :] = db
        small_o[0:1, :] += jnp.sum(dh * xhat, axis=0, keepdims=True)
        small_o[1:2, :] += jnp.sum(dh, axis=0, keepdims=True)
        small_o[2:3, :] += jnp.sum(db.astype(F32), axis=0, keepdims=True)
        return carry

    lax.fori_loop(0, dh_ref.shape[0] // CH, run, 0, unroll=3)
    do_o[...] = nt(da_o[...], wo[...]).astype(BF16)


def first_norm_back(dh, xh1, rs1, n1g, wo):
    rows, width = dh.shape
    step = PAIR_LEN
    whole = lambda shape: pl.BlockSpec(shape, lambda i: (0,) * len(shape))
    block = lambda w: pl.BlockSpec((step, w), lambda i: (i, 0))
    return pl.pallas_call(
        first_norm_back_kernel,
        grid=(rows // step,),
        in_specs=[block(width), block(width), block(1), whole((width,)), whole((width, width))],
        out_specs=[block(width), block(width), block(width), whole((8, width))],
        out_shape=[
            pltpu.HBM((rows, width), F32),
            pltpu.HBM((rows, width), BF16),
            pltpu.HBM((rows, width), BF16),
            jax.ShapeDtypeStruct((8, width), F32),
        ],
        compiler_params=pltpu.CompilerParams(
            dimension_semantics=("arbitrary",), vmem_limit_bytes=24 * MIB
        ),
        cost_estimate=kernel_cost(8),
        name="first_norm_back",
    )(dh, in_hbm(xh1), rs1, n1g, in_hbm(wo))


def down_grad_kernel(half, g, dz, out):
    out[...] = tn(g[...], dz[...]).astype(BF16)


def down_grad(half, g, dz):
    rows, width = dz.shape
    ff = g.shape[1]
    blocks = 2
    size = ff // 2 // blocks
    return pl.pallas_call(
        down_grad_kernel,
        grid_spec=pltpu.PrefetchScalarGridSpec(
            num_scalar_prefetch=1,
            grid=(blocks,),
            in_specs=[
                pl.BlockSpec((rows, size), lambda n, half: (0, half[0] * blocks + n)),
                pl.BlockSpec((rows, width), lambda n, half: (0, 0)),
            ],
            out_specs=pl.BlockSpec((size, width), lambda n, half: (n, 0)),
        ),
        out_shape=jax.ShapeDtypeStruct((ff // 2, width), BF16),
        compiler_params=pltpu.CompilerParams(
            dimension_semantics=("arbitrary",), vmem_limit_bytes=30 * MIB
        ),
        cost_estimate=kernel_cost(5),
        name="down_grad",
    )(half, in_hbm(g), in_hbm(dz))


def in_grad_kernel(half, h, o, du, da, out):
    width = h.shape[1]
    steps = (out.shape[1] - width // 2) // width
    for n in range(steps):

        @pl.when(pl.program_id(0) == n)
        def _():
            out[:, n * width : (n + 1) * width] = tn(h[...], du[...]).astype(BF16)

    @pl.when(pl.program_id(0) == steps)
    def _():
        out[:, steps * width :] = tn(o[...], da[...]).astype(BF16)


def in_grad(half, h, o, du, da):
    rows, width = h.shape
    steps = du.shape[1] // 2 // width
    cols = steps * width + width // 2
    whole = lambda shape: pl.BlockSpec(shape, lambda n, half: (0, 0))
    return pl.pallas_call(
        in_grad_kernel,
        grid_spec=pltpu.PrefetchScalarGridSpec(
            num_scalar_prefetch=1,
            grid=(steps + 1,),
            in_specs=[
                whole((rows, width)),
                whole((rows, width)),
                pl.BlockSpec((rows, width), lambda n, half: (0, half[0] * steps + jnp.minimum(n, steps - 1))),
                pl.BlockSpec((rows, width // 2), lambda n, half: (0, half[0])),
            ],
            out_specs=whole((width, cols)),
        ),
        out_shape=jax.ShapeDtypeStruct((width, cols), BF16),
        compiler_params=pltpu.CompilerParams(
            dimension_semantics=("arbitrary",), vmem_limit_bytes=34 * MIB
        ),
        cost_estimate=kernel_cost(6),
        name="in_grad",
    )(half, *map(in_hbm, (h, o, du, da)))


def proj_cut_kernel(places, x, x_other, d, d_other, a_keep, a_send, b_keep, b_send, total):
    size = d.shape[2]
    half = a_keep.shape[0]
    split = a_keep.shape[1]
    for n in range(3):

        @pl.when(pl.program_id(0) == n)
        def _():
            total[:, n * size : (n + 1) * size] = (tn(x[...], d[0]) + tn(x_other[...], d_other[0])).astype(BF16)

    @pl.when(pl.program_id(0) == 2)
    def _():
        for n, (keep, send) in enumerate(((a_keep, a_send), (b_keep, b_send))):
            cols = slice(n * split, n * split + keep.shape[1])
            for side, out in enumerate((keep, send)):
                at = pl.ds(pl.multiple_of((places[n] ^ side) * half, 16), half)
                out[...] = total[at, cols]


def proj_cut(places, x, x_other, d, d_other, split):
    rows, width = x.shape
    size = d.shape[2]
    whole = lambda shape: pl.BlockSpec(shape, lambda n, places: (0, 0))
    third = pl.BlockSpec((1, rows, size), lambda n, places: (n, 0, 0))
    outs = [(width // 2, w) for w in (split, 3 * size - split) for _ in range(2)]
    got = pl.pallas_call(
        proj_cut_kernel,
        grid_spec=pltpu.PrefetchScalarGridSpec(
            num_scalar_prefetch=1,
            grid=(3,),
            in_specs=[whole((rows, width)), whole((rows, width)), third, third],
            out_specs=[whole(o) for o in outs],
            scratch_shapes=[pltpu.VMEM((width, 3 * size), BF16)],
        ),
        out_shape=[jax.ShapeDtypeStruct(o, BF16) for o in outs],
        compiler_params=pltpu.CompilerParams(
            dimension_semantics=("arbitrary",), vmem_limit_bytes=30 * MIB
        ),
        cost_estimate=kernel_cost(7),
        name="proj_cut",
    )(places, *map(in_hbm, (x, x_other, d, d_other)))
    return [(got[0], got[1]), (got[2], got[3])]


def attention_back_kernel(
    part, qlen, plen, q, k, v, o, do, lse,
    d_o, small_o,
    kmask, lse_p, lse_q, delta_p, delta_q,
):
    step = pl.program_id(0)
    first_head = part[0] * (q.shape[1] // 64)
    width = q.shape[1]
    pairs = width // 128
    lane = lax.broadcasted_iota(jnp.int32, (1, 128), 1)
    low = (lane < 64).astype(F32)
    lanes = (low, 1.0 - low)
    ones = ((lane == 64).astype(F32), (lane == 0).astype(F32))
    q_gain = [(t * 0.125).astype(BF16) for t in lanes]
    keep = [t.astype(BF16) for t in lanes]
    one = [t.astype(BF16) for t in ones]

    q_valid = lax.broadcasted_iota(jnp.int32, (QRY_LEN, 128), 0) < qlen[step]
    p_valid = lax.broadcasted_iota(jnp.int32, (PASS_LEN, 128), 0) < plen[step]
    for side in range(2):
        kmask[side, :QRY_LEN, :] = jnp.where(q_valid, 0.0, NEG * ones[side]).astype(BF16)
        kmask[side, QRY_LEN:, :] = jnp.where(p_valid, 0.0, NEG * ones[side]).astype(BF16)

    q_rows, p_rows = pl.ds(0, QRY_LEN), pl.ds(QRY_LEN, PASS_LEN)
    head_of = (
        lax.broadcasted_iota(jnp.int32, (16, width), 1) // 64
        == lax.broadcasted_iota(jnp.int32, (16, width), 0)
    ).astype(F32).astype(BF16)
    for rows, lse_t, delta_t in ((q_rows, lse_q, delta_q), (p_rows, lse_p, delta_p)):
        lse_t[...] = jnp.transpose(lse[rows, :])
        prod = do[rows, :].astype(F32) * o[rows, :].astype(F32)
        hi = prod.astype(BF16)
        lo = (prod - hi.astype(F32)).astype(BF16)
        delta_t[...] = nt(head_of, hi) + nt(head_of, lo)

    def attend(pair, carry):
        cols = pl.ds(pl.multiple_of(pair * 128, 128), 128)
        for rows, lse_t, delta_t in ((q_rows, lse_q, delta_q), (p_rows, lse_p, delta_p)):
            qp, kp, vp, dop = q[rows, cols], k[rows, cols], v[rows, cols], do[rows, cols]
            qm = [qp * q_gain[side] for side in range(2)]
            km = [kp * q_gain[side] for side in range(2)]
            dm = [dop * keep[side] for side in range(2)]
            st = [nt(kp * keep[side] + kmask[side, rows, :], qm[side] + one[side]) for side in range(2)]
            dpt = [nt(vp, dm[side]) for side in range(2)]
            pt = [
                jnp.exp(st[side] - lse_t[pl.ds(first_head + 2 * pair + side, 1), :]) for side in range(2)
            ]
            dst = [
                (pt[side] * (dpt[side] - delta_t[pl.ds(2 * pair + side, 1), :])).astype(BF16) for side in range(2)
            ]
            d_o[2, rows, cols] = sum(nn(pt[side].astype(BF16), dm[side]) for side in range(2)).astype(BF16)
            d_o[1, rows, cols] = sum(nn(dst[side], qm[side]) for side in range(2)).astype(BF16)
            d_o[0, rows, cols] = sum(tn(dst[side], km[side]) for side in range(2)).astype(BF16)
        return carry

    lax.fori_loop(0, pairs, attend, 0, unroll=pairs)

    @pl.when(step == 0)
    def _():
        small_o[...] = jnp.zeros_like(small_o)

    small_o[0:1, :] += jnp.sum(d_o[0].astype(F32), axis=0, keepdims=True)
    small_o[1:2, :] += jnp.sum(d_o[2].astype(F32), axis=0, keepdims=True)


def attention_back(part, qlen, plen, q, k, v, o, do, lse):
    seqs = qlen.shape[0]
    rows, full = q.shape
    width = full // 2
    whole = lambda shape: pl.BlockSpec(shape, lambda i, part: (0,) * len(shape))
    smem = pl.BlockSpec(memory_space=pltpu.SMEM)
    block = pl.BlockSpec((PAIR_LEN, width), lambda i, part: (i, part[0]))
    return pl.pallas_call(
        attention_back_kernel,
        grid_spec=pltpu.PrefetchScalarGridSpec(
            num_scalar_prefetch=1,
            grid=(seqs,),
            in_specs=[smem, smem] + [block] * 5 + [pl.BlockSpec((PAIR_LEN, 128), lambda i, part: (i, 0))],
            out_specs=[pl.BlockSpec((3, PAIR_LEN, width), lambda i, part: (0, i, 0)), whole((8, width))],
            scratch_shapes=[
                pltpu.VMEM((2, PAIR_LEN, 128), BF16),
                pltpu.VMEM((128, PASS_LEN), F32),
                pltpu.VMEM((128, QRY_LEN), F32),
                pltpu.VMEM((16, PASS_LEN), F32),
                pltpu.VMEM((16, QRY_LEN), F32),
            ],
        ),
        out_shape=[pltpu.HBM((3, rows, width), BF16), jax.ShapeDtypeStruct((8, width), F32)],
        compiler_params=pltpu.CompilerParams(
            dimension_semantics=("arbitrary",), vmem_limit_bytes=28 * MIB
        ),
        cost_estimate=kernel_cost(15),
        name="attention_back",
    )(part, qlen, plen, *map(in_hbm, (q, k, v, o, do, lse)))


def input_grad_kernel(core, dr1, d, d_rest, wq, wk, wv, gq_o, gp_o):
    size = d.shape[2]
    grad = dr1[...]
    for n, w in enumerate((wq, wk, wv)):
        for part, side in ((d, 0), (d_rest, 1)):
            cols = pl.ds(pl.multiple_of((core[0] ^ side) * size, 128), size)
            grad += nt(part[n], w[:, cols])
    gq_o[...] = grad[:QRY_LEN]
    gp_o[...] = grad[QRY_LEN:]


def input_grad(core, dr1, d, d_rest, wq, wk, wv):
    rows, width = dr1.shape
    seqs = rows // PAIR_LEN
    block = pl.BlockSpec((PAIR_LEN, width), lambda i, core: (i, 0))
    thirds = pl.BlockSpec((3, PAIR_LEN, width // 2), lambda i, core: (0, i, 0))
    weight = pl.BlockSpec((width, width), lambda i, core: (0, 0))
    return pl.pallas_call(
        input_grad_kernel,
        grid_spec=pltpu.PrefetchScalarGridSpec(
            num_scalar_prefetch=1,
            grid=(seqs,),
            in_specs=[block, thirds, thirds] + [weight] * 3,
            out_specs=[
                pl.BlockSpec((QRY_LEN, width), lambda i, core: (i, 0)),
                pl.BlockSpec((PASS_LEN, width), lambda i, core: (i, 0)),
            ],
        ),
        out_shape=[
            jax.ShapeDtypeStruct((seqs * QRY_LEN, width), F32),
            jax.ShapeDtypeStruct((seqs * PASS_LEN, width), F32),
        ],
        compiler_params=pltpu.CompilerParams(
            dimension_semantics=("arbitrary",), vmem_limit_bytes=26 * MIB
        ),
        cost_estimate=kernel_cost(10),
        name="input_grad",
    )(core, *map(in_hbm, (dr1, d, d_rest, wq, wk, wv)))


def widen(out, cols, value):
    out[:, cols[0] : cols[1]] = value.astype(F32)


def place_down_kernel(bit, mine, other, out):
    half = pl.program_id(0)

    @pl.when(half == 0)
    def _():
        out[...] = mine[...].astype(F32)

    @pl.when(half == 1)
    def _():
        out[...] = other[...].astype(F32)


def place_down(bit, mine, other):
    rows, cols = mine.shape
    chunks = 4
    step = rows // chunks
    return pl.pallas_call(
        place_down_kernel,
        grid_spec=pltpu.PrefetchScalarGridSpec(
            num_scalar_prefetch=1,
            grid=(2, chunks),
            in_specs=[
                pl.BlockSpec((step, cols), lambda h, n, bit: (jnp.where(h == 0, n, chunks - 1), 0)),
                pl.BlockSpec((step, cols), lambda h, n, bit: (jnp.where(h == 1, n, 0), 0)),
            ],
            out_specs=pl.BlockSpec((step, cols), lambda h, n, bit: ((h ^ bit[0]) * chunks + n, 0)),
        ),
        out_shape=jax.ShapeDtypeStruct((2 * rows, cols), F32),
        compiler_params=pltpu.CompilerParams(
            dimension_semantics=("arbitrary", "arbitrary"), vmem_limit_bytes=16 * MIB
        ),
        cost_estimate=kernel_cost(5),
        name="place_down",
    )(bit, mine, other)


def place_columns(bit, sums, widths, write, name):
    rows = sums[0][0].shape[0]
    chunks = 4
    step = rows // chunks
    arrays = [a for pair in sums for a in pair]

    def kernel(bit, *refs):
        ins, outs = refs[: len(arrays)], refs[len(arrays) :]
        pairs = [(ins[2 * n], ins[2 * n + 1]) for n in range(len(sums))]

        @pl.when(bit[0] == 0)
        def _():
            write(outs, pairs)

        @pl.when(bit[0] == 1)
        def _():
            write(outs, [p[::-1] for p in pairs])

    return pl.pallas_call(
        kernel,
        grid_spec=pltpu.PrefetchScalarGridSpec(
            num_scalar_prefetch=1,
            grid=(chunks,),
            in_specs=[pl.BlockSpec((step, a.shape[1]), lambda n, bit: (n, 0)) for a in arrays],
            out_specs=[pl.BlockSpec((step, w), lambda n, bit: (n, 0)) for w in widths],
        ),
        out_shape=[jax.ShapeDtypeStruct((rows, w), F32) for w in widths],
        compiler_params=pltpu.CompilerParams(
            dimension_semantics=("arbitrary",), vmem_limit_bytes=20 * MIB
        ),
        cost_estimate=kernel_cost(5),
        name=name,
    )(bit, *arrays)


def write_in(outs, pairs):
    for n, half in enumerate(pairs[0]):
        at = 0
        for out in outs:
            size = out.shape[1] // 2
            widen(out, (n * size, (n + 1) * size), half[:, at : at + size])
            at += size


def write_proj(outs, pairs):
    size = outs[0].shape[1] // 2
    for n, half in enumerate(pairs[0]):
        for m, out in enumerate(outs):
            widen(out, (n * size, (n + 1) * size), half[:, m * size : (m + 1) * size])


IN_FLIGHT = 5


def swap_with(value, mask, device_count):
    return lax.ppermute(value, AXES, [(i, i ^ mask) for i in range(device_count)])


def far_groups(device_count):
    masks, mask = [], 4
    while mask < device_count // 2:
        masks.append(mask)
        mask *= 2
    return [masks[n : n + 2] for n in range(0, len(masks), 2)]


def combos_of(group):
    combos = [0]
    for mask in reversed(group):
        combos = combos + [c ^ mask for c in combos]
    return combos


def gather_relative(value, device_count):
    groups = [[device_count // 2, 2]] + far_groups(device_count) + [[1]]
    relative = [0]
    for n, group in enumerate(groups):
        combos = combos_of(group)
        got = [value] + [swap_with(value, c, device_count) for c in combos[1:]]
        relative = [c ^ r for c in combos for r in relative]
        if n < len(groups) - 1:
            value = jnp.concatenate(got, axis=0)
    return got, relative


def whole_call(kernel, scalars, arrays, outs, name):
    spec = lambda shape: pl.BlockSpec(shape, lambda i, s: (0, 0))
    return pl.pallas_call(
        kernel,
        grid_spec=pltpu.PrefetchScalarGridSpec(
            num_scalar_prefetch=1,
            grid=(1,),
            in_specs=[spec(a.shape) for a in arrays],
            out_specs=[spec(o) for o in outs],
        ),
        out_shape=[jax.ShapeDtypeStruct(o, BF16) for o in outs],
        compiler_params=pltpu.CompilerParams(vmem_limit_bytes=24 * MIB),
        cost_estimate=kernel_cost(1),
        name=name,
    )(scalars, *arrays)


def fold(tuples, places, parts, ways=2):
    rows = tuples[0][0].shape[0] // ways
    widths = [sum(c1 - c0 for _, c0, c1 in p) for p in parts]
    arrays = [a for one in tuples for a in one]

    def add(values):
        total = values[0].astype(F32)
        for value in values[1:]:
            total = total + value.astype(F32)
        return total.astype(BF16)

    if rows % 16:
        results = []
        for part, place in zip(parts, places):
            total = jnp.concatenate([add([a[:, c0:c1] for a in tuples[p]]) for p, c0, c1 in part], 1)
            results.append(
                [lax.dynamic_slice_in_dim(total, (place ^ n) * rows, rows, 0) for n in range(ways)]
            )
        return results

    def kernel(place, *refs):
        taken, ref_tuples = 0, []
        for one in tuples:
            ref_tuples.append(refs[taken : taken + len(one)])
            taken += len(one)
        outs = refs[taken:]
        for m, part in enumerate(parts):
            for n in range(ways):
                at = pl.ds(pl.multiple_of((place[m] ^ n) * rows, 16), rows)
                col = 0
                for p, c0, c1 in part:
                    outs[ways * m + n][:, col : col + c1 - c0] = add([r[at, c0:c1] for r in ref_tuples[p]])
                    col += c1 - c0

    got = whole_call(
        kernel, jnp.stack(places), arrays, [(rows, w) for w in widths for _ in range(ways)], "fold"
    )
    return [got[ways * m : ways * (m + 1)] for m in range(len(parts))]


def unfold(tuples, places, parts):
    rows = tuples[0][0].shape[0]
    ways = len(tuples[0])
    widths = [sum(c1 - c0 for _, c0, c1 in p) for p in parts]
    if rows % 16:
        joined = [
            jnp.concatenate([lax.select_n(s, *[t[b ^ n] for n in range(ways)]) for b in range(ways)], 0)
            if ways > 2
            else jnp.where(s == 1, jnp.concatenate([t[1], t[0]], 0), jnp.concatenate([t[0], t[1]], 0))
            for t, s in zip(tuples, places)
        ]
        return [jnp.concatenate([joined[p][:, c0:c1] for p, c0, c1 in part], 1) for part in parts]

    def kernel(place, *refs):
        outs = refs[ways * len(tuples) :]
        for m, part in enumerate(parts):
            col = 0
            for p, c0, c1 in part:
                for n in range(ways):
                    at = pl.ds(pl.multiple_of((place[p] ^ n) * rows, 16), rows)
                    outs[m][at, col : col + c1 - c0] = refs[ways * p + n][:, c0:c1]
                col += c1 - c0

    return whole_call(
        kernel, jnp.stack(places), [a for t in tuples for a in t], [(ways * rows, w) for w in widths], "unfold"
    )


def place_of(group, me):
    pos = jnp.int32(0)
    for mask in group:
        pos = 2 * pos + ((me & mask) != 0).astype(jnp.int32)
    return pos


def reduction(send, kept, split, wide, me, device_count, ready=None):
    top = device_count // 2
    far = far_groups(device_count)
    if not wide:
        far = [[mask] for group in far for mask in group]
    cols = sum(c[0].shape[1] for c in ready) if ready else send.shape[1]
    both = [[(0, 0, split)], [(0, split, cols)]]
    apart = [[(0, 0, split)], [(1, 0, cols - split)]]
    merged = [[(0, 0, split), (1, 0, cols - split)]]
    alone = [[(0, 0, cols)]]

    def place(group):
        return place_of(group, me)

    sums = None
    if not ready:
        got = yield [(send, 1)]
        sums = [(kept[0], got[0])]
    for masks, parts in (((top, 2), both), ((2, top), apart)):
        cut = fold(sums, [place([m]) for m in masks], parts) if sums else ready
        got = yield [(c[1], m) for c, m in zip(cut, masks)]
        sums = [(c[0], g) for c, g in zip(cut, got)]
    for n, group in enumerate(far):
        combos = combos_of(group)
        (cut,) = fold(sums, [place(group)], alone if n else merged, len(combos))
        got = yield list(zip(cut[1:], combos[1:]))
        sums = [(cut[0], *got)]
    total = sums[0][0].astype(F32)
    for value in sums[0][1:]:
        total = total + value.astype(F32)
    mine = total.astype(BF16)
    for group in reversed(far):
        got = yield [(mine, c) for c in combos_of(group)[1:]]
        last = group is far[0]
        mine = unfold([(mine, *got)], [place(group)], both if last else alone)
        mine = mine if last else mine[0]
    for masks, parts in (((2, top), apart), ((top, 2), merged)):
        got = yield [(p, m) for p, m in zip(mine, masks)]
        mine = unfold(list(zip(mine, got)), [place([m]) for m in masks], parts)
    (got,) = yield [(mine[0], 1)]
    return mine[0], got


def exchange(value):
    (got,) = yield [(value, 1)]
    return got


def small_sum(values, device_count):
    mask = 1
    while mask < device_count:
        (got,) = yield [(values, mask)]
        values = values + got
        mask *= 2
    return values


class Line:
    def __init__(self, steps, device_count):
        self.steps = steps
        self.count = device_count
        self.sum = None
        self.want = next(steps)

    def take(self, got):
        try:
            self.want = self.steps.send(got)
        except StopIteration as end:
            self.want, self.sum = None, end.value


def slot(lines, work=None, values=(), kept=None):
    flying = []
    for n in lines:
        if n.want is not None and sum(len(f.want) for f in flying) + len(n.want) <= IN_FLIGHT:
            flying.append(n)
    lines = flying
    arrays = [[a for a, _ in n.want] for n in lines]
    arrays, values = lax.optimization_barrier((arrays, tuple(values)))
    got = [[swap_with(a, m, n.count) for a, (_, m) in zip(sends, n.want)] for sends, n in zip(arrays, lines)]
    out = work(*values) if work is not None else ()
    got, out = lax.optimization_barrier((got, out))
    if kept is not None:
        kept.append(out)
    for n, g in zip(lines, got):
        n.take(g)
    return out


def body(
    query_tokens,
    passage_tokens,
    query_lengths,
    passage_lengths,
    positives,
    w_query,
    b_query,
    w_key,
    w_value,
    b_value,
    w_out,
    b_out,
    norm1_gain,
    norm1_bias,
    w_in,
    b_in,
    w_down,
    b_down,
    norm2_gain,
    norm2_bias,
    query_out_grad,
    passage_out_grad,
):
    seqs = query_lengths.shape[0]
    width = query_tokens.shape[1]
    device_count = lax.axis_size(AXES)
    my_index = lax.axis_index(AXES)
    params = dict(
        w_query=w_query, b_query=b_query, w_key=w_key, w_value=w_value, b_value=b_value, w_out=w_out,
        b_out=b_out, norm1_gain=norm1_gain, norm1_bias=norm1_bias, w_in=w_in, b_in=b_in, w_down=w_down,
        b_down=b_down, norm2_gain=norm2_gain, norm2_bias=norm2_bias,
    )
    (
        query_out, passage_out, q, k, v, o, lse, xhat1, rstd1, h1b, g, gelu_slope, x_rows, xhat2, rstd2, unit, mean,
    ) = forward(query_tokens, passage_tokens, query_lengths, passage_lengths, params)
    units, relative = gather_relative(unit, device_count)
    owner = jnp.array(relative, jnp.int32) ^ my_index
    ids = (owner[:, None] * seqs + jnp.arange(seqs, dtype=jnp.int32)[None, :]).reshape(-1)
    ids = jnp.repeat(ids, 2)
    dz, dr2, small2, loss_sum = loss_and_second_norm(
        units, positives[:, None], ids[:, None], ids[None, :], mean, query_lengths, passage_lengths, query_out_grad, passage_out_grad,
        xhat2, rstd2, norm2_gain,
    )
    loss = loss_sum[0, 0] / (seqs * device_count)
    core = (my_index & 1).astype(jnp.int32)[None]
    other = 1 - core

    def start_line(lines, make, values, wide=False):
        kept = []
        send = slot(lines, lambda *v: make(other, *v), values)
        split = (send.shape[1] + 255) // 256 * 128
        new = Line(reduction(send, kept, split, wide, my_index, device_count), device_count)
        slot(lines + [new], lambda *v: make(core, *v), values, kept)
        return new

    down = start_line([], lambda half, d: down_grad(half, g, d), (dz,))
    x_line = Line(exchange(in_hbm(x_rows)), device_count)
    acc, du, grad_b_in = dr2, None, []
    for first, last in ((0, 4), (4, 6)):
        du, bias, acc = slot(
            [down, x_line],
            lambda *arrays: ffn_back(*arrays[:5], first, last, arrays[5] if first else None),
            (dz, acc, gelu_slope, w_down, w_in, *([du] if first else [])),
        )
        grad_b_in.append(bias)
    dr1, da, do, small1 = slot([down], first_norm_back, (acc, xhat1, rstd1, norm1_gain, w_out))
    up = start_line([down], in_grad, (h1b, o, du, da), wide=True)
    sources = (q, k, v, o, do, lse)
    lengths = (query_lengths, passage_lengths)
    d_rest, small_rest = slot([down, up], lambda *arrays: attention_back(other, *lengths, *arrays), sources)
    d_line = Line(exchange(d_rest), device_count)
    d_own, small_own = slot([down, up, d_line], lambda *arrays: attention_back(core, *lengths, *arrays), sources)
    small0 = jnp.where(
        core == 1, jnp.concatenate([small_rest, small_own], 1), jnp.concatenate([small_own, small_rest], 1)
    )
    packed = jnp.concatenate(
        [small0, small1, small2, jnp.concatenate(grad_b_in, 1).reshape(-1, width)], 0
    )
    small = Line(small_sum(packed, device_count), device_count)
    split = (3 * width // 2 + 255) // 256 * 128
    places = jnp.stack([place_of([mask], my_index) for mask in (device_count // 2, 2)])
    ready = slot(
        [down, up],
        lambda *arrays: proj_cut(places, *arrays, split),
        (x_rows, x_line.sum, d_own, d_line.sum),
    )
    proj = Line(reduction(None, None, split, True, my_index, device_count, ready), device_count)
    query_input_grad, passage_input_grad = slot(
        [up, proj], lambda *arrays: input_grad(core, *arrays), (dr1, d_own, d_rest, w_query, w_key, w_value)
    )
    bit = core
    slot([up, proj, small])
    slot([up, proj])
    while up.want is not None:
        slot([up, proj, small])
    grad_w_in, grad_w_out = slot(
        [proj, down, small],
        lambda bit, *pair: place_columns(bit, [pair], (g.shape[1], width), write_in, "place_in"),
        (bit, *up.sum),
    )
    while down.want is not None:
        slot([proj, down, small])
    grad_w_down = slot([proj, small], place_down, (bit, *down.sum))
    while proj.want is not None or small.want is not None:
        slot([proj, small])
    grad_w_query, grad_w_key, grad_w_value = place_columns(
        bit, [proj.sum], (width,) * 3, write_proj, "place_proj"
    )
    packed = small.sum
    return (
        query_out,
        passage_out,
        query_input_grad,
        passage_input_grad,
        loss,
        grad_w_query,
        packed[0],
        grad_w_key,
        grad_w_value,
        packed[1],
        grad_w_out,
        packed[10],
        packed[8],
        packed[9],
        grad_w_in,
        packed[24:].reshape(-1),
        grad_w_down,
        packed[18],
        packed[16],
        packed[17],
    )


def solution(mesh):
    placed = (
        P(("stream", "batch"), None),
        P(("stream", "batch"), None),
        P(("stream", "batch")),
        P(("stream", "batch")),
        P(),
        P(),
        P(),
        P(),
        P(),
        P(),
        P(),
        P(),
        P(),
        P(),
        P(),
        P(),
        P(),
        P(),
        P(),
        P(),
        P(("stream", "batch"), None),
        P(("stream", "batch"), None),
    )
    return jax.shard_map(
        body,
        mesh=mesh,
        in_specs=placed,
        out_specs=(
            P(("stream", "batch"), None),
            P(("stream", "batch"), None),
            P(("stream", "batch"), None),
            P(("stream", "batch"), None),
            P(),
            P(),
            P(),
            P(),
            P(),
            P(),
            P(),
            P(),
            P(),
            P(),
            P(),
            P(),
            P(),
            P(),
            P(),
            P(),
        ),
        check_vma=False,
    )
```

```python
import functools

import jax
import jax.numpy as jnp
from jax import lax
from jax.experimental import pallas as pl
from jax.experimental.pallas import tpu as pltpu
from jax.sharding import PartitionSpec as P

HEADS = 12
QRY_LEN = 64
PASS_LEN = 512
PAIR_LEN = QRY_LEN + PASS_LEN
LOGIT_SCALE = 0.01
EPS = 1e-06
NEG = -1e30
F32 = jnp.float32
BF16 = jnp.bfloat16
AXES = ("stream", "batch")
MIB = 1024 * 1024
VMEM_LIMIT = 60 * MIB


def kernel_cost(us):
    return pl.CostEstimate(flops=us * 1_000_000_000, bytes_accessed=1_000_000, transcendentals=0)


def nn(a, b):
    return lax.dot_general(a, b, (((1,), (0,)), ((), ())), preferred_element_type=F32)


def nt(a, b):
    return lax.dot_general(a, b, (((1,), (1,)), ((), ())), preferred_element_type=F32)


def tn(a, b):
    return lax.dot_general(a, b, (((0,), (0,)), ((), ())), preferred_element_type=F32)


def gelu_parts(u):
    cdf = 0.5 + 0.5 * lax.erf(u * 0.7071067811865476)
    bell = jnp.exp(-0.5 * (u * u))
    return u * cdf, cdf + u * (bell * 0.3989422804014327)


def forward_kernel(
    qlen, plen, xq, xp, wq_h, wk_h, wv_h, wo_h, wi_h, wd_h, bq, bv, bo, n1g, n1b, bi, bd, n2g, n2b,
    yq, yp, q_h, k_h, v_h, o_h, lse_o, xh1_h, rs1_o, h1b_h, g_h, gp_h, x_h, xh2_o, rs2_o, unit_o, mean_o,
    xs, wq, wk, wv, wo, wi, wd, acc, h1, kmask, units, q_o, k_o, v_o, o_o, xh1_o, h1b_o, g_o, gp_o, sems, out_sems,
):
    step = pl.program_id(0)
    width = xs.shape[1]
    copies = [
        pltpu.make_async_copy(src, dst, sems.at[n])
        for n, (src, dst) in enumerate(
            ((wq_h, wq), (wk_h, wk), (wv_h, wv), (wo_h, wo), (wi_h, wi), (wd_h, wd))
        )
    ]

    here = pl.ds(pl.multiple_of(step * PAIR_LEN, PAIR_LEN), PAIR_LEN)
    saved = (
        (q_o, q_h), (k_o, k_h), (v_o, v_h), (o_o, o_h), (xh1_o, xh1_h), (h1b_o, h1b_h), (g_o, g_h), (gp_o, gp_h),
        (xs, x_h),
    )
    saves = [pltpu.make_async_copy(src, dst.at[here], out_sems.at[n]) for n, (src, dst) in enumerate(saved)]

    def free(*which):
        @pl.when(step > 0)
        def _():
            for n in which:
                saves[n].wait()

    @pl.when(step == 0)
    def _():
        for c in copies:
            c.start()
        lse_o[...] = jnp.zeros_like(lse_o)

    def ready(n):
        @pl.when(step == 0)
        def _():
            copies[n].wait()

    free(0, 1, 2, 3, 8)
    xs[:QRY_LEN, :] = xq[...]
    xs[QRY_LEN:, :] = xp[...]
    saves[8].start()
    ready(0)
    q_o[...] = (nn(xs[...], wq[...]) + bq[...]).astype(BF16)
    ready(1)
    k_o[...] = nn(xs[...], wk[...]).astype(BF16)
    ready(2)
    v_o[...] = (nn(xs[...], wv[...]) + bv[...]).astype(BF16)
    for n in range(3):
        saves[n].start()

    lane = lax.broadcasted_iota(jnp.int32, (1, 128), 1)
    low = (lane < 64).astype(F32)
    lanes = (low, 1.0 - low)
    ones = ((lane == 64).astype(F32), (lane == 0).astype(F32))
    q_gain = [(v * 0.125).astype(BF16) for v in lanes]
    keep = [v.astype(BF16) for v in lanes]
    one = [v.astype(BF16) for v in ones]

    q_valid = lax.broadcasted_iota(jnp.int32, (QRY_LEN, 128), 0) < qlen[step]
    p_valid = lax.broadcasted_iota(jnp.int32, (PASS_LEN, 128), 0) < plen[step]
    for side in range(2):
        kmask[side, :QRY_LEN, :] = jnp.where(q_valid, 0.0, NEG * ones[side]).astype(BF16)
        kmask[side, QRY_LEN:, :] = jnp.where(p_valid, 0.0, NEG * ones[side]).astype(BF16)

    def attend(pair, carry):
        cols = pl.ds(pl.multiple_of(pair * 128, 128), 128)
        for rows in (pl.ds(0, QRY_LEN), pl.ds(QRY_LEN, PASS_LEN)):
            qp, kp, vp = q_o[rows, cols], k_o[rows, cols], v_o[rows, cols]
            mixed = []
            scores = [
                nt(qp * q_gain[side] + one[side], kp * keep[side] + kmask[side, rows, :]) for side in range(2)
            ]
            tops = [jnp.max(s, axis=1, keepdims=True) for s in scores]
            probs = [jnp.exp(s - top).astype(BF16) for s, top in zip(scores, tops)]
            outs = [nn(probs[side], vp * keep[side] + one[side]) for side in range(2)]
            for side in range(2):
                oe, top = outs[side], tops[side]
                total = oe[:, 64:65] if side == 0 else oe[:, 0:1]
                mixed.append(oe * (1.0 / total))
                lse = top + jnp.log(total)
                head = 2 * pair + side
                lse_o[rows, :] = jnp.where(lane == head, lse, lse_o[rows, :])
            o_o[rows, cols] = jnp.where(lane < 64, mixed[0], mixed[1]).astype(BF16)
        return carry

    lax.fori_loop(0, HEADS // 2, attend, 0, unroll=3)

    saves[3].start()
    ready(3)
    acc[...] = nn(o_o[...], wo[...])

    def norm(value):
        mean = jnp.mean(value, axis=-1, keepdims=True)
        c = value - mean
        rstd = lax.rsqrt(jnp.mean(c * c, axis=-1, keepdims=True) + EPS)
        return c * rstd, rstd

    CH = 64

    def first_norm(n, carry):
        rows = pl.ds(pl.multiple_of(n * CH, CH), CH)
        xhat, rstd = norm(xs[rows, :].astype(F32) + acc[rows, :] + bo[...])
        hid = xhat * n1g[...] + n1b[...]
        xh1_o[rows, :] = xhat.astype(BF16)
        rs1_o[rows, :] = rstd
        h1[rows, :] = hid
        h1b_o[rows, :] = hid.astype(BF16)
        return carry

    free(4, 5)
    lax.fori_loop(0, PAIR_LEN // CH, first_norm, 0, unroll=3)
    saves[4].start()
    saves[5].start()

    ready(4)
    ready(5)
    free(6, 7)
    g, slope = gelu_parts(nn(h1b_o[...], wi[...]) + bi[...])
    g_o[...] = g.astype(BF16)
    gp_o[...] = slope.astype(BF16)
    h1[...] += nn(g_o[...], wd[...])
    saves[6].start()
    saves[7].start()

    def second_norm(row0, rows_n, out, valid_n):
        def run(n, total):
            at = pl.multiple_of(n * CH, CH)
            rows = pl.ds(row0 + at, CH)
            xhat, rstd = norm(h1[rows, :] + bd[...])
            y = xhat * n2g[...] + n2b[...]
            xh2_o[rows, :] = xhat.astype(BF16)
            rs2_o[rows, :] = rstd
            out[pl.ds(at, CH), :] = y.astype(BF16)
            live = (lax.broadcasted_iota(jnp.int32, (CH, 1), 0) + at) < valid_n
            return total + jnp.sum(jnp.where(live, y, 0.0), axis=0, keepdims=True)

        total = lax.fori_loop(
            0, rows_n // CH, run, jnp.zeros((1, width), F32), unroll=min(4, rows_n // CH)
        )
        return total / valid_n.astype(F32)

    for kind, mean in enumerate(
        (
            second_norm(0, QRY_LEN, yq, qlen[step]),
            second_norm(QRY_LEN, PASS_LEN, yp, plen[step]),
        )
    ):
        at = pl.ds(2 * step + kind, 1)
        mean_o[at, :] = mean
        unit = mean * lax.rsqrt(jnp.sum(mean * mean, axis=-1, keepdims=True) + EPS)
        units[at, :] = unit

    @pl.when(step == pl.num_programs(0) - 1)
    def _():
        unit_o[...] = units[...].astype(BF16)
        for c in saves:
            c.wait()


def forward(xq, xp, qlen, plen, p):
    seqs = qlen.shape[0]
    width = xq.shape[1]
    ff = p["w_in"].shape[1]
    rows = seqs * PAIR_LEN
    whole = lambda shape: pl.BlockSpec(shape, lambda i: (0,) * len(shape))
    smem = pl.BlockSpec(memory_space=pltpu.SMEM)
    hbm = pl.BlockSpec(memory_space=pl.ANY)
    row_block = lambda n, w: pl.BlockSpec((n, w), lambda i: (i, 0))
    outs = [
        ((seqs * QRY_LEN, width), BF16, row_block(QRY_LEN, width)),
        ((seqs * PASS_LEN, width), BF16, row_block(PASS_LEN, width)),
        ((rows, width), BF16, hbm),
        ((rows, width), BF16, hbm),
        ((rows, width), BF16, hbm),
        ((rows, width), BF16, hbm),
        ((rows, 128), F32, row_block(PAIR_LEN, 128)),
        ((rows, width), BF16, hbm),
        ((rows, 1), F32, row_block(PAIR_LEN, 1)),
        ((rows, width), BF16, hbm),
        ((rows, ff), BF16, hbm),
        ((rows, ff), BF16, hbm),
        ((rows, width), BF16, hbm),
        ((rows, width), BF16, row_block(PAIR_LEN, width)),
        ((rows, 1), F32, row_block(PAIR_LEN, 1)),
        ((2 * seqs, width), BF16, whole((2 * seqs, width))),
        ((2 * seqs, width), F32, whole((2 * seqs, width))),
    ]
    return pl.pallas_call(
        forward_kernel,
        grid=(seqs,),
        in_specs=[smem, smem, row_block(QRY_LEN, width), row_block(PASS_LEN, width)]
        + [hbm] * 6
        + [whole((width,))] * 5
        + [whole((ff,))]
        + [whole((width,))] * 3,
        out_specs=[o[2] for o in outs],
        out_shape=[jax.ShapeDtypeStruct(o[0], o[1]) for o in outs],
        scratch_shapes=[
            pltpu.VMEM((PAIR_LEN, width), BF16),
            pltpu.VMEM((width, width), BF16),
            pltpu.VMEM((width, width), BF16),
            pltpu.VMEM((width, width), BF16),
            pltpu.VMEM((width, width), BF16),
            pltpu.VMEM((width, ff), BF16),
            pltpu.VMEM((ff, width), BF16),
            pltpu.VMEM((PAIR_LEN, width), F32),
            pltpu.VMEM((PAIR_LEN, width), F32),
            pltpu.VMEM((2, PAIR_LEN, 128), BF16),
            pltpu.VMEM((2 * seqs, width), F32),
            *[pltpu.VMEM((PAIR_LEN, width), BF16) for _ in range(6)],
            *[pltpu.VMEM((PAIR_LEN, ff), BF16) for _ in range(2)],
            pltpu.SemaphoreType.DMA((6,)),
            pltpu.SemaphoreType.DMA((9,)),
        ],
        compiler_params=pltpu.CompilerParams(
            dimension_semantics=("arbitrary",), vmem_limit_bytes=VMEM_LIMIT
        ),
        cost_estimate=kernel_cost(45),
        name="forward_layer",
    )(
        qlen, plen, xq, xp, p["w_query"], p["w_key"], p["w_value"], p["w_out"], p["w_in"], p["w_down"],
        p["b_query"], p["b_value"], p["b_out"], p["norm1_gain"],
        p["norm1_bias"], p["b_in"], p["b_down"], p["norm2_gain"],
        p["norm2_bias"],
    )


def in_hbm(array):
    return pltpu.with_memory_space_constraint(array, pltpu.HBM)


def loss_kernel(
    qlen, plen, units_0, units_1, positives, row_id, column_id, mean, ogq, ogp, xh2, rs2, n2g,
    dz_o, dr2_o, small_o, loss_o,
    de,
):
    step = pl.program_id(0)
    seqs = pl.num_programs(0)
    width = xh2.shape[1]
    mine = mean.shape[0]

    @pl.when(step == 0)
    def _():
        u = jnp.concatenate([units_0[...], units_1[...]], 0)
        n = u.shape[0]
        row = lax.broadcasted_iota(jnp.int32, (n, n), 0)
        col = lax.broadcasted_iota(jnp.int32, (n, n), 1)
        pairs = ((row & 1) == 0) & ((col & 1) == 1)
        logits = jnp.where(pairs, nt(u, u) / LOGIT_SCALE, NEG)
        top = jnp.max(logits, axis=1, keepdims=True)
        lse = top + jnp.log(jnp.sum(jnp.exp(logits - top), axis=1, keepdims=True))
        count = positives.shape[0]
        query = (row_id[...] == lax.broadcasted_iota(jnp.int32, (n, count), 1)).astype(F32).astype(BF16)
        passage = (positives[...] == column_id[...]).astype(F32).astype(BF16)
        hit = pairs & (nn(query, passage) > 0.5)
        chosen = jnp.sum(jnp.where(hit, logits, 0.0), axis=1, keepdims=True)
        is_query = (lax.broadcasted_iota(jnp.int32, (n, 1), 0) & 1) == 0
        loss_o[...] = jnp.sum(jnp.where(is_query, lse - chosen, 0.0), axis=0, keepdims=True)
        dc = jnp.where(pairs, (jnp.exp(logits - lse) - hit.astype(F32)) / LOGIT_SCALE, 0.0)
        both = (dc + jnp.transpose(dc)).astype(BF16)
        dn = nn(both[:16], u)[:mine]
        e = mean[...]
        square = jnp.sum(e * e, axis=-1, keepdims=True) + EPS
        grad = (dn - e * (jnp.sum(e * dn, axis=-1, keepdims=True) / square)) * lax.rsqrt(square)
        de[...] = jnp.zeros_like(de)
        de[:mine, :] = grad
        small_o[...] = jnp.zeros_like(small_o)

    CH = 64

    def back(row0, rows_n, grads, valid_n, kind):
        shift = de[pl.ds(2 * step + kind, 1), :] / valid_n.astype(F32)

        def run(n, carry):
            at = pl.multiple_of(n * CH, CH)
            rows = pl.ds(row0 + at, CH)
            live = (lax.broadcasted_iota(jnp.int32, (CH, 1), 0) + at) < valid_n
            dy = grads[pl.ds(at, CH), :].astype(F32) + jnp.where(live, shift, 0.0)
            xhat = xh2[rows, :].astype(F32)
            dyg = dy * n2g[...]
            m1 = jnp.mean(dyg, axis=-1, keepdims=True)
            m2 = jnp.mean(dyg * xhat, axis=-1, keepdims=True)
            dr = rs2[rows, :] * (dyg - m1 - xhat * m2)
            db = dr.astype(BF16)
            dr2_o[rows, :] = dr
            dz_o[rows, :] = db
            small_o[0:1, :] += jnp.sum(dy * xhat, axis=0, keepdims=True)
            small_o[1:2, :] += jnp.sum(dy, axis=0, keepdims=True)
            small_o[2:3, :] += jnp.sum(db.astype(F32), axis=0, keepdims=True)
            return carry

        lax.fori_loop(0, rows_n // CH, run, 0, unroll=min(4, rows_n // CH))

    back(0, QRY_LEN, ogq, qlen[step], 0)
    back(QRY_LEN, PASS_LEN, ogp, plen[step], 1)


def loss_and_second_norm(units, positives, row_id, column_id, mean, qlen, plen, ogq, ogp, xh2, rs2, n2g):
    seqs = qlen.shape[0]
    width = ogq.shape[1]
    rows = seqs * PAIR_LEN
    whole = lambda shape: pl.BlockSpec(shape, lambda i: (0,) * len(shape))
    smem = pl.BlockSpec(memory_space=pltpu.SMEM)
    row_block = lambda n, w: pl.BlockSpec((n, w), lambda i: (i, 0))
    return pl.pallas_call(
        loss_kernel,
        grid=(seqs,),
        in_specs=[
            smem, smem, *[whole(t.shape) for t in units], whole(positives.shape), whole(row_id.shape), whole(column_id.shape), whole(mean.shape),
            row_block(QRY_LEN, width), row_block(PASS_LEN, width), row_block(PAIR_LEN, width),
            row_block(PAIR_LEN, 1), whole((width,)),
        ],
        out_specs=[row_block(PAIR_LEN, width), row_block(PAIR_LEN, width), whole((8, width)), whole((1, 1))],
        out_shape=[
            pltpu.HBM((rows, width), BF16),
            pltpu.HBM((rows, width), F32),
            jax.ShapeDtypeStruct((8, width), F32),
            jax.ShapeDtypeStruct((1, 1), F32),
        ],
        scratch_shapes=[pltpu.VMEM((8, width), F32)],
        compiler_params=pltpu.CompilerParams(
            dimension_semantics=("arbitrary",), vmem_limit_bytes=16 * MIB
        ),
        cost_estimate=kernel_cost(8),
        name="loss_norm_back",
    )(qlen, plen, *units, positives, row_id, column_id, *map(in_hbm, (mean, ogq, ogp, xh2, rs2)), n2g)


def ffn_back_kernel(dz, dr2, gp, wd, wi, du_o, bi_o, acc):
    step = pl.program_id(0)
    du = (nt(dz[...], wd[...]) * gp[...].astype(F32)).astype(BF16)
    du_o[...] = du
    bi_o[...] = jnp.sum(du.astype(F32), axis=0, keepdims=True)
    part = nt(du, wi[...])

    @pl.when(step == 0)
    def _():
        acc[...] = dr2[...] + part

    @pl.when(step > 0)
    def _():
        acc[...] += part


def ffn_back(dz, dr2, gp, wd, wi, first, last, into):
    rows, width = dz.shape
    fb = gp.shape[1] // 6
    steps = last - first
    skip = first
    whole = lambda shape: pl.BlockSpec(shape, lambda i: (0,) * len(shape))
    earlier = [] if into is None else [into]

    def body(*refs):
        ffn_back_kernel(*refs[:5], *refs[5 + len(earlier) :])

    return pl.pallas_call(
        body,
        grid=(steps,),
        in_specs=[
            whole((rows, width)), whole((rows, width)),
            pl.BlockSpec((rows, fb), lambda i: (0, i + skip)),
            pl.BlockSpec((fb, width), lambda i: (i + skip, 0)),
            pl.BlockSpec((width, fb), lambda i: (0, i + skip)),
        ]
        + [pl.BlockSpec(memory_space=pl.ANY)] * len(earlier),
        out_specs=[
            pl.BlockSpec((rows, fb), lambda i: (0, i + skip)),
            pl.BlockSpec((1, fb), lambda i: (0, i)),
            whole((rows, width)),
        ],
        out_shape=[
            pltpu.HBM(gp.shape, BF16),
            jax.ShapeDtypeStruct((1, steps * fb), F32),
            jax.ShapeDtypeStruct((rows, width), F32),
        ],
        input_output_aliases={5 + n: n for n in range(len(earlier))},
        compiler_params=pltpu.CompilerParams(
            dimension_semantics=("arbitrary",), vmem_limit_bytes=28 * MIB
        ),
        cost_estimate=kernel_cost(10),
        name="ffn_back",
    )(in_hbm(dz), dr2 if earlier else in_hbm(dr2), *map(in_hbm, (gp, wd, wi)), *earlier)


def first_norm_back_kernel(dh_ref, xh1, rs1, n1g, wo, dr1_o, da_o, do_o, small_o):
    CH = 64

    @pl.when(pl.program_id(0) == 0)
    def _():
        small_o[...] = jnp.zeros_like(small_o)

    def run(n, carry):
        rows = pl.ds(pl.multiple_of(n * CH, CH), CH)
        dh = dh_ref[rows, :]
        xhat = xh1[rows, :].astype(F32)
        dyg = dh * n1g[...]
        m1 = jnp.mean(dyg, axis=-1, keepdims=True)
        m2 = jnp.mean(dyg * xhat, axis=-1, keepdims=True)
        dr = rs1[rows, :] * (dyg - m1 - xhat * m2)
        db = dr.astype(BF16)
        dr1_o[rows, :] = dr
        da_o[rows, :] = db
        small_o[0:1, :] += jnp.sum(dh * xhat, axis=0, keepdims=True)
        small_o[1:2, :] += jnp.sum(dh, axis=0, keepdims=True)
        small_o[2:3, :] += jnp.sum(db.astype(F32), axis=0, keepdims=True)
        return carry

    lax.fori_loop(0, dh_ref.shape[0] // CH, run, 0, unroll=3)
    do_o[...] = nt(da_o[...], wo[...]).astype(BF16)


def first_norm_back(dh, xh1, rs1, n1g, wo):
    rows, width = dh.shape
    step = PAIR_LEN
    whole = lambda shape: pl.BlockSpec(shape, lambda i: (0,) * len(shape))
    block = lambda w: pl.BlockSpec((step, w), lambda i: (i, 0))
    return pl.pallas_call(
        first_norm_back_kernel,
        grid=(rows // step,),
        in_specs=[block(width), block(width), block(1), whole((width,)), whole((width, width))],
        out_specs=[block(width), block(width), block(width), whole((8, width))],
        out_shape=[
            pltpu.HBM((rows, width), F32),
            pltpu.HBM((rows, width), BF16),
            pltpu.HBM((rows, width), BF16),
            jax.ShapeDtypeStruct((8, width), F32),
        ],
        compiler_params=pltpu.CompilerParams(
            dimension_semantics=("arbitrary",), vmem_limit_bytes=24 * MIB
        ),
        cost_estimate=kernel_cost(8),
        name="first_norm_back",
    )(dh, in_hbm(xh1), rs1, n1g, in_hbm(wo))


def down_grad_kernel(half, g, dz, out):
    out[...] = tn(g[...], dz[...]).astype(BF16)


def down_grad(half, g, dz):
    rows, width = dz.shape
    ff = g.shape[1]
    blocks = 2
    size = ff // 2 // blocks
    return pl.pallas_call(
        down_grad_kernel,
        grid_spec=pltpu.PrefetchScalarGridSpec(
            num_scalar_prefetch=1,
            grid=(blocks,),
            in_specs=[
                pl.BlockSpec((rows, size), lambda n, half: (0, half[0] * blocks + n)),
                pl.BlockSpec((rows, width), lambda n, half: (0, 0)),
            ],
            out_specs=pl.BlockSpec((size, width), lambda n, half: (n, 0)),
        ),
        out_shape=jax.ShapeDtypeStruct((ff // 2, width), BF16),
        compiler_params=pltpu.CompilerParams(
            dimension_semantics=("arbitrary",), vmem_limit_bytes=30 * MIB
        ),
        cost_estimate=kernel_cost(5),
        name="down_grad",
    )(half, in_hbm(g), in_hbm(dz))


def in_grad_kernel(half, h, o, du, da, out):
    width = h.shape[1]
    steps = (out.shape[1] - width // 2) // width
    for n in range(steps):

        @pl.when(pl.program_id(0) == n)
        def _():
            out[:, n * width : (n + 1) * width] = tn(h[...], du[...]).astype(BF16)

    @pl.when(pl.program_id(0) == steps)
    def _():
        out[:, steps * width :] = tn(o[...], da[...]).astype(BF16)


def in_grad(half, h, o, du, da):
    rows, width = h.shape
    steps = du.shape[1] // 2 // width
    cols = steps * width + width // 2
    whole = lambda shape: pl.BlockSpec(shape, lambda n, half: (0, 0))
    return pl.pallas_call(
        in_grad_kernel,
        grid_spec=pltpu.PrefetchScalarGridSpec(
            num_scalar_prefetch=1,
            grid=(steps + 1,),
            in_specs=[
                whole((rows, width)),
                whole((rows, width)),
                pl.BlockSpec((rows, width), lambda n, half: (0, half[0] * steps + jnp.minimum(n, steps - 1))),
                pl.BlockSpec((rows, width // 2), lambda n, half: (0, half[0])),
            ],
            out_specs=whole((width, cols)),
        ),
        out_shape=jax.ShapeDtypeStruct((width, cols), BF16),
        compiler_params=pltpu.CompilerParams(
            dimension_semantics=("arbitrary",), vmem_limit_bytes=34 * MIB
        ),
        cost_estimate=kernel_cost(6),
        name="in_grad",
    )(half, *map(in_hbm, (h, o, du, da)))


def proj_cut_kernel(places, x, x_other, d, d_other, a_keep, a_send, b_keep, b_send, total):
    size = d.shape[2]
    half = a_keep.shape[0]
    split = a_keep.shape[1]
    for n in range(3):

        @pl.when(pl.program_id(0) == n)
        def _():
            total[:, n * size : (n + 1) * size] = (tn(x[...], d[0]) + tn(x_other[...], d_other[0])).astype(BF16)

    @pl.when(pl.program_id(0) == 2)
    def _():
        for n, (keep, send) in enumerate(((a_keep, a_send), (b_keep, b_send))):
            cols = slice(n * split, n * split + keep.shape[1])
            for side, out in enumerate((keep, send)):
                at = pl.ds(pl.multiple_of((places[n] ^ side) * half, 16), half)
                out[...] = total[at, cols]


def proj_cut(places, x, x_other, d, d_other, split):
    rows, width = x.shape
    size = d.shape[2]
    whole = lambda shape: pl.BlockSpec(shape, lambda n, places: (0, 0))
    third = pl.BlockSpec((1, rows, size), lambda n, places: (n, 0, 0))
    outs = [(width // 2, w) for w in (split, 3 * size - split) for _ in range(2)]
    got = pl.pallas_call(
        proj_cut_kernel,
        grid_spec=pltpu.PrefetchScalarGridSpec(
            num_scalar_prefetch=1,
            grid=(3,),
            in_specs=[whole((rows, width)), whole((rows, width)), third, third],
            out_specs=[whole(o) for o in outs],
            scratch_shapes=[pltpu.VMEM((width, 3 * size), BF16)],
        ),
        out_shape=[jax.ShapeDtypeStruct(o, BF16) for o in outs],
        compiler_params=pltpu.CompilerParams(
            dimension_semantics=("arbitrary",), vmem_limit_bytes=30 * MIB
        ),
        cost_estimate=kernel_cost(7),
        name="proj_cut",
    )(places, *map(in_hbm, (x, x_other, d, d_other)))
    return [(got[0], got[1]), (got[2], got[3])]


def attention_back_kernel(
    part, qlen, plen, q, k, v, o, do, lse,
    d_o, small_o,
    kmask, lse_p, lse_q, delta_p, delta_q,
):
    step = pl.program_id(0)
    first_head = part[0] * (q.shape[1] // 64)
    width = q.shape[1]
    pairs = width // 128
    lane = lax.broadcasted_iota(jnp.int32, (1, 128), 1)
    low = (lane < 64).astype(F32)
    lanes = (low, 1.0 - low)
    ones = ((lane == 64).astype(F32), (lane == 0).astype(F32))
    q_gain = [(t * 0.125).astype(BF16) for t in lanes]
    keep = [t.astype(BF16) for t in lanes]
    one = [t.astype(BF16) for t in ones]

    q_valid = lax.broadcasted_iota(jnp.int32, (QRY_LEN, 128), 0) < qlen[step]
    p_valid = lax.broadcasted_iota(jnp.int32, (PASS_LEN, 128), 0) < plen[step]
    for side in range(2):
        kmask[side, :QRY_LEN, :] = jnp.where(q_valid, 0.0, NEG * ones[side]).astype(BF16)
        kmask[side, QRY_LEN:, :] = jnp.where(p_valid, 0.0, NEG * ones[side]).astype(BF16)

    q_rows, p_rows = pl.ds(0, QRY_LEN), pl.ds(QRY_LEN, PASS_LEN)
    head_of = (
        lax.broadcasted_iota(jnp.int32, (16, width), 1) // 64
        == lax.broadcasted_iota(jnp.int32, (16, width), 0)
    ).astype(F32).astype(BF16)
    for rows, lse_t, delta_t in ((q_rows, lse_q, delta_q), (p_rows, lse_p, delta_p)):
        lse_t[...] = jnp.transpose(lse[rows, :])
        prod = do[rows, :].astype(F32) * o[rows, :].astype(F32)
        hi = prod.astype(BF16)
        lo = (prod - hi.astype(F32)).astype(BF16)
        delta_t[...] = nt(head_of, hi) + nt(head_of, lo)

    def attend(pair, carry):
        cols = pl.ds(pl.multiple_of(pair * 128, 128), 128)
        for rows, lse_t, delta_t in ((q_rows, lse_q, delta_q), (p_rows, lse_p, delta_p)):
            qp, kp, vp, dop = q[rows, cols], k[rows, cols], v[rows, cols], do[rows, cols]
            qm = [qp * q_gain[side] for side in range(2)]
            km = [kp * q_gain[side] for side in range(2)]
            dm = [dop * keep[side] for side in range(2)]
            st = [nt(kp * keep[side] + kmask[side, rows, :], qm[side] + one[side]) for side in range(2)]
            dpt = [nt(vp, dm[side]) for side in range(2)]
            pt = [
                jnp.exp(st[side] - lse_t[pl.ds(first_head + 2 * pair + side, 1), :]) for side in range(2)
            ]
            dst = [
                (pt[side] * (dpt[side] - delta_t[pl.ds(2 * pair + side, 1), :])).astype(BF16) for side in range(2)
            ]
            d_o[2, rows, cols] = sum(nn(pt[side].astype(BF16), dm[side]) for side in range(2)).astype(BF16)
            d_o[1, rows, cols] = sum(nn(dst[side], qm[side]) for side in range(2)).astype(BF16)
            d_o[0, rows, cols] = sum(tn(dst[side], km[side]) for side in range(2)).astype(BF16)
        return carry

    lax.fori_loop(0, pairs, attend, 0, unroll=pairs)

    @pl.when(step == 0)
    def _():
        small_o[...] = jnp.zeros_like(small_o)

    small_o[0:1, :] += jnp.sum(d_o[0].astype(F32), axis=0, keepdims=True)
    small_o[1:2, :] += jnp.sum(d_o[2].astype(F32), axis=0, keepdims=True)


def attention_back(part, qlen, plen, q, k, v, o, do, lse):
    seqs = qlen.shape[0]
    rows, full = q.shape
    width = full // 2
    whole = lambda shape: pl.BlockSpec(shape, lambda i, part: (0,) * len(shape))
    smem = pl.BlockSpec(memory_space=pltpu.SMEM)
    block = pl.BlockSpec((PAIR_LEN, width), lambda i, part: (i, part[0]))
    return pl.pallas_call(
        attention_back_kernel,
        grid_spec=pltpu.PrefetchScalarGridSpec(
            num_scalar_prefetch=1,
            grid=(seqs,),
            in_specs=[smem, smem] + [block] * 5 + [pl.BlockSpec((PAIR_LEN, 128), lambda i, part: (i, 0))],
            out_specs=[pl.BlockSpec((3, PAIR_LEN, width), lambda i, part: (0, i, 0)), whole((8, width))],
            scratch_shapes=[
                pltpu.VMEM((2, PAIR_LEN, 128), BF16),
                pltpu.VMEM((128, PASS_LEN), F32),
                pltpu.VMEM((128, QRY_LEN), F32),
                pltpu.VMEM((16, PASS_LEN), F32),
                pltpu.VMEM((16, QRY_LEN), F32),
            ],
        ),
        out_shape=[pltpu.HBM((3, rows, width), BF16), jax.ShapeDtypeStruct((8, width), F32)],
        compiler_params=pltpu.CompilerParams(
            dimension_semantics=("arbitrary",), vmem_limit_bytes=28 * MIB
        ),
        cost_estimate=kernel_cost(15),
        name="attention_back",
    )(part, qlen, plen, *map(in_hbm, (q, k, v, o, do, lse)))


def input_grad_kernel(core, dr1, d, d_rest, wq, wk, wv, gq_o, gp_o):
    size = d.shape[2]
    grad = dr1[...]
    for n, w in enumerate((wq, wk, wv)):
        for part, side in ((d, 0), (d_rest, 1)):
            cols = pl.ds(pl.multiple_of((core[0] ^ side) * size, 128), size)
            grad += nt(part[n], w[:, cols])
    gq_o[...] = grad[:QRY_LEN]
    gp_o[...] = grad[QRY_LEN:]


def input_grad(core, dr1, d, d_rest, wq, wk, wv):
    rows, width = dr1.shape
    seqs = rows // PAIR_LEN
    block = pl.BlockSpec((PAIR_LEN, width), lambda i, core: (i, 0))
    thirds = pl.BlockSpec((3, PAIR_LEN, width // 2), lambda i, core: (0, i, 0))
    weight = pl.BlockSpec((width, width), lambda i, core: (0, 0))
    return pl.pallas_call(
        input_grad_kernel,
        grid_spec=pltpu.PrefetchScalarGridSpec(
            num_scalar_prefetch=1,
            grid=(seqs,),
            in_specs=[block, thirds, thirds] + [weight] * 3,
            out_specs=[
                pl.BlockSpec((QRY_LEN, width), lambda i, core: (i, 0)),
                pl.BlockSpec((PASS_LEN, width), lambda i, core: (i, 0)),
            ],
        ),
        out_shape=[
            jax.ShapeDtypeStruct((seqs * QRY_LEN, width), F32),
            jax.ShapeDtypeStruct((seqs * PASS_LEN, width), F32),
        ],
        compiler_params=pltpu.CompilerParams(
            dimension_semantics=("arbitrary",), vmem_limit_bytes=26 * MIB
        ),
        cost_estimate=kernel_cost(10),
        name="input_grad",
    )(core, *map(in_hbm, (dr1, d, d_rest, wq, wk, wv)))


def widen(out, cols, value):
    out[:, cols[0] : cols[1]] = value.astype(F32)


def place_down_kernel(bit, mine, other, out):
    half = pl.program_id(0)

    @pl.when(half == 0)
    def _():
        out[...] = mine[...].astype(F32)

    @pl.when(half == 1)
    def _():
        out[...] = other[...].astype(F32)


def place_down(bit, mine, other):
    rows, cols = mine.shape
    chunks = 4
    step = rows // chunks
    return pl.pallas_call(
        place_down_kernel,
        grid_spec=pltpu.PrefetchScalarGridSpec(
            num_scalar_prefetch=1,
            grid=(2, chunks),
            in_specs=[
                pl.BlockSpec((step, cols), lambda h, n, bit: (jnp.where(h == 0, n, chunks - 1), 0)),
                pl.BlockSpec((step, cols), lambda h, n, bit: (jnp.where(h == 1, n, 0), 0)),
            ],
            out_specs=pl.BlockSpec((step, cols), lambda h, n, bit: ((h ^ bit[0]) * chunks + n, 0)),
        ),
        out_shape=jax.ShapeDtypeStruct((2 * rows, cols), F32),
        compiler_params=pltpu.CompilerParams(
            dimension_semantics=("arbitrary", "arbitrary"), vmem_limit_bytes=16 * MIB
        ),
        cost_estimate=kernel_cost(5),
        name="place_down",
    )(bit, mine, other)


def place_columns(bit, sums, widths, write, name):
    rows = sums[0][0].shape[0]
    chunks = 4
    step = rows // chunks
    arrays = [a for pair in sums for a in pair]

    def kernel(bit, *refs):
        ins, outs = refs[: len(arrays)], refs[len(arrays) :]
        pairs = [(ins[2 * n], ins[2 * n + 1]) for n in range(len(sums))]

        @pl.when(bit[0] == 0)
        def _():
            write(outs, pairs)

        @pl.when(bit[0] == 1)
        def _():
            write(outs, [p[::-1] for p in pairs])

    return pl.pallas_call(
        kernel,
        grid_spec=pltpu.PrefetchScalarGridSpec(
            num_scalar_prefetch=1,
            grid=(chunks,),
            in_specs=[pl.BlockSpec((step, a.shape[1]), lambda n, bit: (n, 0)) for a in arrays],
            out_specs=[pl.BlockSpec((step, w), lambda n, bit: (n, 0)) for w in widths],
        ),
        out_shape=[jax.ShapeDtypeStruct((rows, w), F32) for w in widths],
        compiler_params=pltpu.CompilerParams(
            dimension_semantics=("arbitrary",), vmem_limit_bytes=20 * MIB
        ),
        cost_estimate=kernel_cost(5),
        name=name,
    )(bit, *arrays)


def write_in(outs, pairs):
    for n, half in enumerate(pairs[0]):
        at = 0
        for out in outs:
            size = out.shape[1] // 2
            widen(out, (n * size, (n + 1) * size), half[:, at : at + size])
            at += size


def write_proj(outs, pairs):
    size = outs[0].shape[1] // 2
    for n, half in enumerate(pairs[0]):
        for m, out in enumerate(outs):
            widen(out, (n * size, (n + 1) * size), half[:, m * size : (m + 1) * size])


IN_FLIGHT = 5


def swap_with(value, mask, device_count):
    return lax.ppermute(value, AXES, [(i, i ^ mask) for i in range(device_count)])


def far_groups(device_count):
    masks, mask = [], 4
    while mask < device_count // 2:
        masks.append(mask)
        mask *= 2
    return [masks[n : n + 2] for n in range(0, len(masks), 2)]


def combos_of(group):
    combos = [0]
    for mask in reversed(group):
        combos = combos + [c ^ mask for c in combos]
    return combos


def gather_relative(value, device_count):
    groups = [[device_count // 2, 2]] + far_groups(device_count) + [[1]]
    relative = [0]
    for n, group in enumerate(groups):
        combos = combos_of(group)
        got = [value] + [swap_with(value, c, device_count) for c in combos[1:]]
        relative = [c ^ r for c in combos for r in relative]
        if n < len(groups) - 1:
            value = jnp.concatenate(got, axis=0)
    return got, relative


def whole_call(kernel, scalars, arrays, outs, name):
    spec = lambda shape: pl.BlockSpec(shape, lambda i, s: (0, 0))
    return pl.pallas_call(
        kernel,
        grid_spec=pltpu.PrefetchScalarGridSpec(
            num_scalar_prefetch=1,
            grid=(1,),
            in_specs=[spec(a.shape) for a in arrays],
            out_specs=[spec(o) for o in outs],
        ),
        out_shape=[jax.ShapeDtypeStruct(o, BF16) for o in outs],
        compiler_params=pltpu.CompilerParams(vmem_limit_bytes=24 * MIB),
        cost_estimate=kernel_cost(1),
        name=name,
    )(scalars, *arrays)


def fold(tuples, places, parts, ways=2):
    rows = tuples[0][0].shape[0] // ways
    widths = [sum(c1 - c0 for _, c0, c1 in p) for p in parts]
    arrays = [a for one in tuples for a in one]

    def add(values):
        total = values[0].astype(F32)
        for value in values[1:]:
            total = total + value.astype(F32)
        return total.astype(BF16)

    if rows % 16:
        results = []
        for part, place in zip(parts, places):
            total = jnp.concatenate([add([a[:, c0:c1] for a in tuples[p]]) for p, c0, c1 in part], 1)
            results.append(
                [lax.dynamic_slice_in_dim(total, (place ^ n) * rows, rows, 0) for n in range(ways)]
            )
        return results

    def kernel(place, *refs):
        taken, ref_tuples = 0, []
        for one in tuples:
            ref_tuples.append(refs[taken : taken + len(one)])
            taken += len(one)
        outs = refs[taken:]
        for m, part in enumerate(parts):
            for n in range(ways):
                at = pl.ds(pl.multiple_of((place[m] ^ n) * rows, 16), rows)
                col = 0
                for p, c0, c1 in part:
                    outs[ways * m + n][:, col : col + c1 - c0] = add([r[at, c0:c1] for r in ref_tuples[p]])
                    col += c1 - c0

    got = whole_call(
        kernel, jnp.stack(places), arrays, [(rows, w) for w in widths for _ in range(ways)], "fold"
    )
    return [got[ways * m : ways * (m + 1)] for m in range(len(parts))]


def unfold(tuples, places, parts):
    rows = tuples[0][0].shape[0]
    ways = len(tuples[0])
    widths = [sum(c1 - c0 for _, c0, c1 in p) for p in parts]
    if rows % 16:
        joined = [
            jnp.concatenate([lax.select_n(s, *[t[b ^ n] for n in range(ways)]) for b in range(ways)], 0)
            if ways > 2
            else jnp.where(s == 1, jnp.concatenate([t[1], t[0]], 0), jnp.concatenate([t[0], t[1]], 0))
            for t, s in zip(tuples, places)
        ]
        return [jnp.concatenate([joined[p][:, c0:c1] for p, c0, c1 in part], 1) for part in parts]

    def kernel(place, *refs):
        outs = refs[ways * len(tuples) :]
        for m, part in enumerate(parts):
            col = 0
            for p, c0, c1 in part:
                for n in range(ways):
                    at = pl.ds(pl.multiple_of((place[p] ^ n) * rows, 16), rows)
                    outs[m][at, col : col + c1 - c0] = refs[ways * p + n][:, c0:c1]
                col += c1 - c0

    return whole_call(
        kernel, jnp.stack(places), [a for t in tuples for a in t], [(ways * rows, w) for w in widths], "unfold"
    )


def place_of(group, me):
    pos = jnp.int32(0)
    for mask in group:
        pos = 2 * pos + ((me & mask) != 0).astype(jnp.int32)
    return pos


def reduction(send, kept, split, wide, me, device_count, ready=None):
    top = device_count // 2
    far = far_groups(device_count)
    back = [[mask] for group in far for mask in group]
    if not wide:
        far = back
    elif wide == "both":
        back = far
    cols = sum(c[0].shape[1] for c in ready) if ready else send.shape[1]
    both = [[(0, 0, split)], [(0, split, cols)]]
    apart = [[(0, 0, split)], [(1, 0, cols - split)]]
    merged = [[(0, 0, split), (1, 0, cols - split)]]
    alone = [[(0, 0, cols)]]

    def place(group):
        return place_of(group, me)

    sums = None
    if not ready:
        got = yield [(send, 1)]
        sums = [(kept[0], got[0])]
    for masks, parts in (((top, 2), both), ((2, top), apart)):
        cut = fold(sums, [place([m]) for m in masks], parts) if sums else ready
        got = yield [(c[1], m) for c, m in zip(cut, masks)]
        sums = [(c[0], g) for c, g in zip(cut, got)]
    for n, group in enumerate(far):
        combos = combos_of(group)
        (cut,) = fold(sums, [place(group)], alone if n else merged, len(combos))
        got = yield list(zip(cut[1:], combos[1:]))
        sums = [(cut[0], *got)]
    total = sums[0][0].astype(F32)
    for value in sums[0][1:]:
        total = total + value.astype(F32)
    mine = total.astype(BF16)
    for group in reversed(back):
        got = yield [(mine, c) for c in combos_of(group)[1:]]
        last = group is back[0]
        mine = unfold([(mine, *got)], [place(group)], both if last else alone)
        mine = mine if last else mine[0]
    for masks, parts in (((2, top), apart), ((top, 2), merged)):
        got = yield [(p, m) for p, m in zip(mine, masks)]
        mine = unfold(list(zip(mine, got)), [place([m]) for m in masks], parts)
    (got,) = yield [(mine[0], 1)]
    return mine[0], got


def exchange(value):
    (got,) = yield [(value, 1)]
    return got


def small_sum(values, device_count):
    mask = 1
    while mask < device_count:
        (got,) = yield [(values, mask)]
        values = values + got
        mask *= 2
    return values


class Line:
    def __init__(self, steps, device_count):
        self.steps = steps
        self.count = device_count
        self.sum = None
        self.want = next(steps)

    def take(self, got):
        try:
            self.want = self.steps.send(got)
        except StopIteration as end:
            self.want, self.sum = None, end.value


def slot(lines, work=None, values=(), kept=None):
    flying = []
    for n in lines:
        if n.want is not None and sum(len(f.want) for f in flying) + len(n.want) <= IN_FLIGHT:
            flying.append(n)
    lines = flying
    arrays = [[a for a, _ in n.want] for n in lines]
    arrays, values = lax.optimization_barrier((arrays, tuple(values)))
    got = [[swap_with(a, m, n.count) for a, (_, m) in zip(sends, n.want)] for sends, n in zip(arrays, lines)]
    out = work(*values) if work is not None else ()
    got, out = lax.optimization_barrier((got, out))
    if kept is not None:
        kept.append(out)
    for n, g in zip(lines, got):
        n.take(g)
    return out


def body(
    query_tokens,
    passage_tokens,
    query_lengths,
    passage_lengths,
    positives,
    w_query,
    b_query,
    w_key,
    w_value,
    b_value,
    w_out,
    b_out,
    norm1_gain,
    norm1_bias,
    w_in,
    b_in,
    w_down,
    b_down,
    norm2_gain,
    norm2_bias,
    query_out_grad,
    passage_out_grad,
):
    seqs = query_lengths.shape[0]
    width = query_tokens.shape[1]
    device_count = lax.axis_size(AXES)
    my_index = lax.axis_index(AXES)
    params = dict(
        w_query=w_query, b_query=b_query, w_key=w_key, w_value=w_value, b_value=b_value, w_out=w_out,
        b_out=b_out, norm1_gain=norm1_gain, norm1_bias=norm1_bias, w_in=w_in, b_in=b_in, w_down=w_down,
        b_down=b_down, norm2_gain=norm2_gain, norm2_bias=norm2_bias,
    )
    (
        query_out, passage_out, q, k, v, o, lse, xhat1, rstd1, h1b, g, gelu_slope, x_rows, xhat2, rstd2, unit, mean,
    ) = forward(query_tokens, passage_tokens, query_lengths, passage_lengths, params)
    units, relative = gather_relative(unit, device_count)
    owner = jnp.array(relative, jnp.int32) ^ my_index
    ids = (owner[:, None] * seqs + jnp.arange(seqs, dtype=jnp.int32)[None, :]).reshape(-1)
    ids = jnp.repeat(ids, 2)
    dz, dr2, small2, loss_sum = loss_and_second_norm(
        units, positives[:, None], ids[:, None], ids[None, :], mean, query_lengths, passage_lengths, query_out_grad, passage_out_grad,
        xhat2, rstd2, norm2_gain,
    )
    loss = loss_sum[0, 0] / (seqs * device_count)
    core = (my_index & 1).astype(jnp.int32)[None]
    other = 1 - core

    def start_line(lines, make, values, wide=""):
        kept = []
        send = slot(lines, lambda *v: make(other, *v), values)
        split = (send.shape[1] + 255) // 256 * 128
        new = Line(reduction(send, kept, split, wide, my_index, device_count), device_count)
        slot(lines + [new], lambda *v: make(core, *v), values, kept)
        return new

    down = start_line([], lambda half, d: down_grad(half, g, d), (dz,))
    x_line = Line(exchange(in_hbm(x_rows)), device_count)
    acc, du, grad_b_in = dr2, None, []
    for first, last in ((0, 4), (4, 6)):
        du, bias, acc = slot(
            [down, x_line],
            lambda *arrays: ffn_back(*arrays[:5], first, last, arrays[5] if first else None),
            (dz, acc, gelu_slope, w_down, w_in, *([du] if first else [])),
        )
        grad_b_in.append(bias)
    dr1, da, do, small1 = slot([down], first_norm_back, (acc, xhat1, rstd1, norm1_gain, w_out))
    up = start_line([down], in_grad, (h1b, o, du, da), wide="out")
    sources = (q, k, v, o, do, lse)
    lengths = (query_lengths, passage_lengths)
    d_rest, small_rest = slot([down, up], lambda *arrays: attention_back(other, *lengths, *arrays), sources)
    d_line = Line(exchange(d_rest), device_count)
    d_own, small_own = slot([down, up, d_line], lambda *arrays: attention_back(core, *lengths, *arrays), sources)
    small0 = jnp.where(
        core == 1, jnp.concatenate([small_rest, small_own], 1), jnp.concatenate([small_own, small_rest], 1)
    )
    packed = jnp.concatenate(
        [small0, small1, small2, jnp.concatenate(grad_b_in, 1).reshape(-1, width)], 0
    )
    small = Line(small_sum(packed, device_count), device_count)
    split = (3 * width // 2 + 255) // 256 * 128
    places = jnp.stack([place_of([mask], my_index) for mask in (device_count // 2, 2)])
    ready = slot(
        [down, up],
        lambda *arrays: proj_cut(places, *arrays, split),
        (x_rows, x_line.sum, d_own, d_line.sum),
    )
    proj = Line(reduction(None, None, split, "both", my_index, device_count, ready), device_count)
    bit = core
    while down.want is not None:
        slot([down, up, proj, small])
    slot([up, proj, small])
    grad_w_down = slot([up, proj], place_down, (bit, *down.sum))
    query_input_grad, passage_input_grad = slot(
        [up, proj], lambda *arrays: input_grad(core, *arrays), (dr1, d_own, d_rest, w_query, w_key, w_value)
    )
    while up.want is not None:
        slot([up, proj, small])
    grad_w_in, grad_w_out = slot(
        [proj, small],
        lambda bit, *pair: place_columns(bit, [pair], (g.shape[1], width), write_in, "place_in"),
        (bit, *up.sum),
    )
    while proj.want is not None or small.want is not None:
        slot([proj, small])
    grad_w_query, grad_w_key, grad_w_value = place_columns(
        bit, [proj.sum], (width,) * 3, write_proj, "place_proj"
    )
    packed = small.sum
    return (
        query_out,
        passage_out,
        query_input_grad,
        passage_input_grad,
        loss,
        grad_w_query,
        packed[0],
        grad_w_key,
        grad_w_value,
        packed[1],
        grad_w_out,
        packed[10],
        packed[8],
        packed[9],
        grad_w_in,
        packed[24:].reshape(-1),
        grad_w_down,
        packed[18],
        packed[16],
        packed[17],
    )


def solution(mesh):
    placed = (
        P(("stream", "batch"), None),
        P(("stream", "batch"), None),
        P(("stream", "batch")),
        P(("stream", "batch")),
        P(),
        P(),
        P(),
        P(),
        P(),
        P(),
        P(),
        P(),
        P(),
        P(),
        P(),
        P(),
        P(),
        P(),
        P(),
        P(),
        P(("stream", "batch"), None),
        P(("stream", "batch"), None),
    )
    return jax.shard_map(
        body,
        mesh=mesh,
        in_specs=placed,
        out_specs=(
            P(("stream", "batch"), None),
            P(("stream", "batch"), None),
            P(("stream", "batch"), None),
            P(("stream", "batch"), None),
            P(),
            P(),
            P(),
            P(),
            P(),
            P(),
            P(),
            P(),
            P(),
            P(),
            P(),
            P(),
            P(),
            P(),
            P(),
            P(),
        ),
        check_vma=False,
    )
```

```python
import functools

import jax
import jax.numpy as jnp
from jax import lax
from jax.experimental import pallas as pl
from jax.experimental.pallas import tpu as pltpu
from jax.sharding import PartitionSpec as P

HEADS = 12
QRY_LEN = 64
PASS_LEN = 512
PAIR_LEN = QRY_LEN + PASS_LEN
LOGIT_SCALE = 0.01
EPS = 1e-06
NEG = -1e30
F32 = jnp.float32
BF16 = jnp.bfloat16
AXES = ("stream", "batch")
MIB = 1024 * 1024
VMEM_LIMIT = 60 * MIB


def kernel_cost(us):
    return pl.CostEstimate(flops=us * 1_000_000_000, bytes_accessed=1_000_000, transcendentals=0)


def nn(a, b):
    return lax.dot_general(a, b, (((1,), (0,)), ((), ())), preferred_element_type=F32)


def nt(a, b):
    return lax.dot_general(a, b, (((1,), (1,)), ((), ())), preferred_element_type=F32)


def tn(a, b):
    return lax.dot_general(a, b, (((0,), (0,)), ((), ())), preferred_element_type=F32)


def gelu_parts(u):
    cdf = 0.5 + 0.5 * lax.erf(u * 0.7071067811865476)
    bell = jnp.exp(-0.5 * (u * u))
    return u * cdf, cdf + u * (bell * 0.3989422804014327)


def forward_kernel(
    qlen, plen, xq, xp, wq_h, wk_h, wv_h, wo_h, wi_h, wd_h, bq, bv, bo, n1g, n1b, bi, bd, n2g, n2b,
    yq, yp, q_h, k_h, v_h, o_h, lse_o, xh1_h, rs1_o, h1b_h, g_h, gp_h, x_h, xh2_o, rs2_o, unit_o, mean_o,
    xs, wq, wk, wv, wo, wi, wd, acc, h1, kmask, units, q_o, k_o, v_o, o_o, xh1_o, h1b_o, g_o, gp_o, sems, out_sems,
):
    step = pl.program_id(0)
    width = xs.shape[1]
    copies = [
        pltpu.make_async_copy(src, dst, sems.at[n])
        for n, (src, dst) in enumerate(
            ((wq_h, wq), (wk_h, wk), (wv_h, wv), (wo_h, wo), (wi_h, wi), (wd_h, wd))
        )
    ]

    here = pl.ds(pl.multiple_of(step * PAIR_LEN, PAIR_LEN), PAIR_LEN)
    saved = (
        (q_o, q_h), (k_o, k_h), (v_o, v_h), (o_o, o_h), (xh1_o, xh1_h), (h1b_o, h1b_h), (g_o, g_h), (gp_o, gp_h),
        (xs, x_h),
    )
    saves = [pltpu.make_async_copy(src, dst.at[here], out_sems.at[n]) for n, (src, dst) in enumerate(saved)]

    def free(*which):
        @pl.when(step > 0)
        def _():
            for n in which:
                saves[n].wait()

    @pl.when(step == 0)
    def _():
        for c in copies:
            c.start()
        lse_o[...] = jnp.zeros_like(lse_o)

    def ready(n):
        @pl.when(step == 0)
        def _():
            copies[n].wait()

    free(0, 1, 2, 3, 8)
    xs[:QRY_LEN, :] = xq[...]
    xs[QRY_LEN:, :] = xp[...]
    saves[8].start()
    ready(0)
    q_o[...] = (nn(xs[...], wq[...]) + bq[...]).astype(BF16)
    ready(1)
    k_o[...] = nn(xs[...], wk[...]).astype(BF16)
    ready(2)
    v_o[...] = (nn(xs[...], wv[...]) + bv[...]).astype(BF16)
    for n in range(3):
        saves[n].start()

    lane = lax.broadcasted_iota(jnp.int32, (1, 128), 1)
    low = (lane < 64).astype(F32)
    lanes = (low, 1.0 - low)
    ones = ((lane == 64).astype(F32), (lane == 0).astype(F32))
    q_gain = [(v * 0.125).astype(BF16) for v in lanes]
    keep = [v.astype(BF16) for v in lanes]
    one = [v.astype(BF16) for v in ones]

    q_valid = lax.broadcasted_iota(jnp.int32, (QRY_LEN, 128), 0) < qlen[step]
    p_valid = lax.broadcasted_iota(jnp.int32, (PASS_LEN, 128), 0) < plen[step]
    for side in range(2):
        kmask[side, :QRY_LEN, :] = jnp.where(q_valid, 0.0, NEG * ones[side]).astype(BF16)
        kmask[side, QRY_LEN:, :] = jnp.where(p_valid, 0.0, NEG * ones[side]).astype(BF16)

    def attend(pair, carry):
        cols = pl.ds(pl.multiple_of(pair * 128, 128), 128)
        for rows in (pl.ds(0, QRY_LEN), pl.ds(QRY_LEN, PASS_LEN)):
            qp, kp, vp = q_o[rows, cols], k_o[rows, cols], v_o[rows, cols]
            mixed = []
            scores = [
                nt(qp * q_gain[side] + one[side], kp * keep[side] + kmask[side, rows, :]) for side in range(2)
            ]
            tops = [jnp.max(s, axis=1, keepdims=True) for s in scores]
            probs = [jnp.exp(s - top).astype(BF16) for s, top in zip(scores, tops)]
            outs = [nn(probs[side], vp * keep[side] + one[side]) for side in range(2)]
            for side in range(2):
                oe, top = outs[side], tops[side]
                total = oe[:, 64:65] if side == 0 else oe[:, 0:1]
                mixed.append(oe * (1.0 / total))
                lse = top + jnp.log(total)
                head = 2 * pair + side
                lse_o[rows, :] = jnp.where(lane == head, lse, lse_o[rows, :])
            o_o[rows, cols] = jnp.where(lane < 64, mixed[0], mixed[1]).astype(BF16)
        return carry

    lax.fori_loop(0, HEADS // 2, attend, 0, unroll=3)

    saves[3].start()
    ready(3)
    acc[...] = nn(o_o[...], wo[...])

    def norm(value):
        mean = jnp.mean(value, axis=-1, keepdims=True)
        c = value - mean
        rstd = lax.rsqrt(jnp.mean(c * c, axis=-1, keepdims=True) + EPS)
        return c * rstd, rstd

    CH = 64

    def first_norm(n, carry):
        rows = pl.ds(pl.multiple_of(n * CH, CH), CH)
        xhat, rstd = norm(xs[rows, :].astype(F32) + acc[rows, :] + bo[...])
        hid = xhat * n1g[...] + n1b[...]
        xh1_o[rows, :] = xhat.astype(BF16)
        rs1_o[rows, :] = rstd
        h1[rows, :] = hid
        h1b_o[rows, :] = hid.astype(BF16)
        return carry

    free(4, 5)
    lax.fori_loop(0, PAIR_LEN // CH, first_norm, 0, unroll=3)
    saves[4].start()
    saves[5].start()

    ready(4)
    ready(5)
    free(6, 7)
    fb = wi.shape[1] // 4
    for n in range(4):
        cols = slice(n * fb, (n + 1) * fb)
        g, slope = gelu_parts(nn(h1b_o[...], wi[:, cols]) + bi[cols])
        g_o[:, cols] = g.astype(BF16)
        gp_o[:, cols] = slope.astype(BF16)
    h1[...] += nn(g_o[...], wd[...])
    saves[6].start()
    saves[7].start()

    def second_norm(row0, rows_n, out, valid_n):
        def run(n, total):
            at = pl.multiple_of(n * CH, CH)
            rows = pl.ds(row0 + at, CH)
            xhat, rstd = norm(h1[rows, :] + bd[...])
            y = xhat * n2g[...] + n2b[...]
            xh2_o[rows, :] = xhat.astype(BF16)
            rs2_o[rows, :] = rstd
            out[pl.ds(at, CH), :] = y.astype(BF16)
            live = (lax.broadcasted_iota(jnp.int32, (CH, 1), 0) + at) < valid_n
            return total + jnp.sum(jnp.where(live, y, 0.0), axis=0, keepdims=True)

        total = lax.fori_loop(
            0, rows_n // CH, run, jnp.zeros((1, width), F32), unroll=min(4, rows_n // CH)
        )
        return total / valid_n.astype(F32)

    for kind, mean in enumerate(
        (
            second_norm(0, QRY_LEN, yq, qlen[step]),
            second_norm(QRY_LEN, PASS_LEN, yp, plen[step]),
        )
    ):
        at = pl.ds(2 * step + kind, 1)
        mean_o[at, :] = mean
        unit = mean * lax.rsqrt(jnp.sum(mean * mean, axis=-1, keepdims=True) + EPS)
        units[at, :] = unit

    @pl.when(step == pl.num_programs(0) - 1)
    def _():
        unit_o[...] = units[...].astype(BF16)
        for c in saves:
            c.wait()


def forward(xq, xp, qlen, plen, p):
    seqs = qlen.shape[0]
    width = xq.shape[1]
    ff = p["w_in"].shape[1]
    rows = seqs * PAIR_LEN
    whole = lambda shape: pl.BlockSpec(shape, lambda i: (0,) * len(shape))
    smem = pl.BlockSpec(memory_space=pltpu.SMEM)
    hbm = pl.BlockSpec(memory_space=pl.ANY)
    row_block = lambda n, w: pl.BlockSpec((n, w), lambda i: (i, 0))
    outs = [
        ((seqs * QRY_LEN, width), BF16, row_block(QRY_LEN, width)),
        ((seqs * PASS_LEN, width), BF16, row_block(PASS_LEN, width)),
        ((rows, width), BF16, hbm),
        ((rows, width), BF16, hbm),
        ((rows, width), BF16, hbm),
        ((rows, width), BF16, hbm),
        ((rows, 128), F32, row_block(PAIR_LEN, 128)),
        ((rows, width), BF16, hbm),
        ((rows, 1), F32, row_block(PAIR_LEN, 1)),
        ((rows, width), BF16, hbm),
        ((rows, ff), BF16, hbm),
        ((rows, ff), BF16, hbm),
        ((rows, width), BF16, hbm),
        ((rows, width), BF16, row_block(PAIR_LEN, width)),
        ((rows, 1), F32, row_block(PAIR_LEN, 1)),
        ((2 * seqs, width), BF16, whole((2 * seqs, width))),
        ((2 * seqs, width), F32, whole((2 * seqs, width))),
    ]
    return pl.pallas_call(
        forward_kernel,
        grid=(seqs,),
        in_specs=[smem, smem, row_block(QRY_LEN, width), row_block(PASS_LEN, width)]
        + [hbm] * 6
        + [whole((width,))] * 5
        + [whole((ff,))]
        + [whole((width,))] * 3,
        out_specs=[o[2] for o in outs],
        out_shape=[jax.ShapeDtypeStruct(o[0], o[1]) for o in outs],
        scratch_shapes=[
            pltpu.VMEM((PAIR_LEN, width), BF16),
            pltpu.VMEM((width, width), BF16),
            pltpu.VMEM((width, width), BF16),
            pltpu.VMEM((width, width), BF16),
            pltpu.VMEM((width, width), BF16),
            pltpu.VMEM((width, ff), BF16),
            pltpu.VMEM((ff, width), BF16),
            pltpu.VMEM((PAIR_LEN, width), F32),
            pltpu.VMEM((PAIR_LEN, width), F32),
            pltpu.VMEM((2, PAIR_LEN, 128), BF16),
            pltpu.VMEM((2 * seqs, width), F32),
            *[pltpu.VMEM((PAIR_LEN, width), BF16) for _ in range(6)],
            *[pltpu.VMEM((PAIR_LEN, ff), BF16) for _ in range(2)],
            pltpu.SemaphoreType.DMA((6,)),
            pltpu.SemaphoreType.DMA((9,)),
        ],
        compiler_params=pltpu.CompilerParams(
            dimension_semantics=("arbitrary",), vmem_limit_bytes=VMEM_LIMIT
        ),
        cost_estimate=kernel_cost(45),
        name="forward_layer",
    )(
        qlen, plen, xq, xp, p["w_query"], p["w_key"], p["w_value"], p["w_out"], p["w_in"], p["w_down"],
        p["b_query"], p["b_value"], p["b_out"], p["norm1_gain"],
        p["norm1_bias"], p["b_in"], p["b_down"], p["norm2_gain"],
        p["norm2_bias"],
    )


def in_hbm(array):
    return pltpu.with_memory_space_constraint(array, pltpu.HBM)


def loss_kernel(
    qlen, plen, units_0, units_1, positives, row_id, column_id, mean, ogq, ogp, xh2, rs2, n2g,
    dz_o, dr2_o, small_o, loss_o,
    de,
):
    step = pl.program_id(0)
    seqs = pl.num_programs(0)
    width = xh2.shape[1]
    mine = mean.shape[0]

    @pl.when(step == 0)
    def _():
        u = jnp.concatenate([units_0[...], units_1[...]], 0)
        n = u.shape[0]
        row = lax.broadcasted_iota(jnp.int32, (n, n), 0)
        col = lax.broadcasted_iota(jnp.int32, (n, n), 1)
        pairs = ((row & 1) == 0) & ((col & 1) == 1)
        logits = jnp.where(pairs, nt(u, u) / LOGIT_SCALE, NEG)
        top = jnp.max(logits, axis=1, keepdims=True)
        lse = top + jnp.log(jnp.sum(jnp.exp(logits - top), axis=1, keepdims=True))
        count = positives.shape[0]
        query = (row_id[...] == lax.broadcasted_iota(jnp.int32, (n, count), 1)).astype(F32).astype(BF16)
        passage = (positives[...] == column_id[...]).astype(F32).astype(BF16)
        hit = pairs & (nn(query, passage) > 0.5)
        chosen = jnp.sum(jnp.where(hit, logits, 0.0), axis=1, keepdims=True)
        is_query = (lax.broadcasted_iota(jnp.int32, (n, 1), 0) & 1) == 0
        loss_o[...] = jnp.sum(jnp.where(is_query, lse - chosen, 0.0), axis=0, keepdims=True)
        dc = jnp.where(pairs, (jnp.exp(logits - lse) - hit.astype(F32)) / LOGIT_SCALE, 0.0)
        both = (dc + jnp.transpose(dc)).astype(BF16)
        dn = nn(both[:16], u)[:mine]
        e = mean[...]
        square = jnp.sum(e * e, axis=-1, keepdims=True) + EPS
        grad = (dn - e * (jnp.sum(e * dn, axis=-1, keepdims=True) / square)) * lax.rsqrt(square)
        de[...] = jnp.zeros_like(de)
        de[:mine, :] = grad
        small_o[...] = jnp.zeros_like(small_o)

    CH = 64

    def back(row0, rows_n, grads, valid_n, kind):
        shift = de[pl.ds(2 * step + kind, 1), :] / valid_n.astype(F32)

        def run(n, carry):
            at = pl.multiple_of(n * CH, CH)
            rows = pl.ds(row0 + at, CH)
            live = (lax.broadcasted_iota(jnp.int32, (CH, 1), 0) + at) < valid_n
            dy = grads[pl.ds(at, CH), :].astype(F32) + jnp.where(live, shift, 0.0)
            xhat = xh2[rows, :].astype(F32)
            dyg = dy * n2g[...]
            m1 = jnp.mean(dyg, axis=-1, keepdims=True)
            m2 = jnp.mean(dyg * xhat, axis=-1, keepdims=True)
            dr = rs2[rows, :] * (dyg - m1 - xhat * m2)
            db = dr.astype(BF16)
            dr2_o[rows, :] = dr
            dz_o[rows, :] = db
            small_o[0:1, :] += jnp.sum(dy * xhat, axis=0, keepdims=True)
            small_o[1:2, :] += jnp.sum(dy, axis=0, keepdims=True)
            small_o[2:3, :] += jnp.sum(db.astype(F32), axis=0, keepdims=True)
            return carry

        lax.fori_loop(0, rows_n // CH, run, 0, unroll=min(4, rows_n // CH))

    back(0, QRY_LEN, ogq, qlen[step], 0)
    back(QRY_LEN, PASS_LEN, ogp, plen[step], 1)


def loss_and_second_norm(units, positives, row_id, column_id, mean, qlen, plen, ogq, ogp, xh2, rs2, n2g):
    seqs = qlen.shape[0]
    width = ogq.shape[1]
    rows = seqs * PAIR_LEN
    whole = lambda shape: pl.BlockSpec(shape, lambda i: (0,) * len(shape))
    smem = pl.BlockSpec(memory_space=pltpu.SMEM)
    row_block = lambda n, w: pl.BlockSpec((n, w), lambda i: (i, 0))
    return pl.pallas_call(
        loss_kernel,
        grid=(seqs,),
        in_specs=[
            smem, smem, *[whole(t.shape) for t in units], whole(positives.shape), whole(row_id.shape), whole(column_id.shape), whole(mean.shape),
            row_block(QRY_LEN, width), row_block(PASS_LEN, width), row_block(PAIR_LEN, width),
            row_block(PAIR_LEN, 1), whole((width,)),
        ],
        out_specs=[row_block(PAIR_LEN, width), row_block(PAIR_LEN, width), whole((8, width)), whole((1, 1))],
        out_shape=[
            pltpu.HBM((rows, width), BF16),
            pltpu.HBM((rows, width), F32),
            jax.ShapeDtypeStruct((8, width), F32),
            jax.ShapeDtypeStruct((1, 1), F32),
        ],
        scratch_shapes=[pltpu.VMEM((8, width), F32)],
        compiler_params=pltpu.CompilerParams(
            dimension_semantics=("arbitrary",), vmem_limit_bytes=16 * MIB
        ),
        cost_estimate=kernel_cost(8),
        name="loss_norm_back",
    )(qlen, plen, *units, positives, row_id, column_id, *map(in_hbm, (mean, ogq, ogp, xh2, rs2)), n2g)


def ffn_back_kernel(dz, dr2, gp, wd, wi, du_o, bi_o, acc):
    step = pl.program_id(0)
    du = (nt(dz[...], wd[...]) * gp[...].astype(F32)).astype(BF16)
    du_o[...] = du
    bi_o[...] = jnp.sum(du.astype(F32), axis=0, keepdims=True)
    part = nt(du, wi[...])

    @pl.when(step == 0)
    def _():
        acc[...] = dr2[...] + part

    @pl.when(step > 0)
    def _():
        acc[...] += part


def ffn_back(dz, dr2, gp, wd, wi, first, last, into):
    rows, width = dz.shape
    fb = gp.shape[1] // 6
    steps = last - first
    skip = first
    whole = lambda shape: pl.BlockSpec(shape, lambda i: (0,) * len(shape))
    once = lambda shape: pl.BlockSpec(shape, lambda i: (0, 0), pipeline_mode=pl.Buffered(1))
    earlier = [] if into is None else [into]

    def body(*refs):
        ffn_back_kernel(*refs[:5], *refs[5 + len(earlier) :])

    return pl.pallas_call(
        body,
        grid=(steps,),
        in_specs=[
            once((rows, width)), once((rows, width)),
            pl.BlockSpec((rows, fb), lambda i: (0, i + skip)),
            pl.BlockSpec((fb, width), lambda i: (i + skip, 0)),
            pl.BlockSpec((width, fb), lambda i: (0, i + skip)),
        ]
        + [pl.BlockSpec(memory_space=pl.ANY)] * len(earlier),
        out_specs=[
            pl.BlockSpec((rows, fb), lambda i: (0, i + skip)),
            pl.BlockSpec((1, fb), lambda i: (0, i)),
            whole((rows, width)),
        ],
        out_shape=[
            pltpu.HBM(gp.shape, BF16),
            jax.ShapeDtypeStruct((1, steps * fb), F32),
            jax.ShapeDtypeStruct((rows, width), F32),
        ],
        input_output_aliases={5 + n: n for n in range(len(earlier))},
        compiler_params=pltpu.CompilerParams(
            dimension_semantics=("arbitrary",), vmem_limit_bytes=23 * MIB
        ),
        cost_estimate=kernel_cost(10),
        name="ffn_back",
    )(in_hbm(dz), dr2 if earlier else in_hbm(dr2), *map(in_hbm, (gp, wd, wi)), *earlier)


def first_norm_back_kernel(dh_ref, xh1, rs1, n1g, wo, dr1_o, da_o, do_o, small_o):
    CH = 64

    @pl.when(pl.program_id(0) == 0)
    def _():
        small_o[...] = jnp.zeros_like(small_o)

    def run(n, carry):
        rows = pl.ds(pl.multiple_of(n * CH, CH), CH)
        dh = dh_ref[rows, :]
        xhat = xh1[rows, :].astype(F32)
        dyg = dh * n1g[...]
        m1 = jnp.mean(dyg, axis=-1, keepdims=True)
        m2 = jnp.mean(dyg * xhat, axis=-1, keepdims=True)
        dr = rs1[rows, :] * (dyg - m1 - xhat * m2)
        db = dr.astype(BF16)
        dr1_o[rows, :] = dr
        da_o[rows, :] = db
        small_o[0:1, :] += jnp.sum(dh * xhat, axis=0, keepdims=True)
        small_o[1:2, :] += jnp.sum(dh, axis=0, keepdims=True)
        small_o[2:3, :] += jnp.sum(db.astype(F32), axis=0, keepdims=True)
        return carry

    lax.fori_loop(0, dh_ref.shape[0] // CH, run, 0, unroll=3)
    do_o[...] = nt(da_o[...], wo[...]).astype(BF16)


def first_norm_back(dh, xh1, rs1, n1g, wo):
    rows, width = dh.shape
    step = PAIR_LEN
    whole = lambda shape: pl.BlockSpec(shape, lambda i: (0,) * len(shape))
    block = lambda w: pl.BlockSpec((step, w), lambda i: (i, 0))
    return pl.pallas_call(
        first_norm_back_kernel,
        grid=(rows // step,),
        in_specs=[block(width), block(width), block(1), whole((width,)), whole((width, width))],
        out_specs=[block(width), block(width), block(width), whole((8, width))],
        out_shape=[
            pltpu.HBM((rows, width), F32),
            pltpu.HBM((rows, width), BF16),
            pltpu.HBM((rows, width), BF16),
            jax.ShapeDtypeStruct((8, width), F32),
        ],
        compiler_params=pltpu.CompilerParams(
            dimension_semantics=("arbitrary",), vmem_limit_bytes=24 * MIB
        ),
        cost_estimate=kernel_cost(8),
        name="first_norm_back",
    )(dh, in_hbm(xh1), rs1, n1g, in_hbm(wo))


def down_grad_kernel(half, g, dz, out):
    out[...] = tn(g[...], dz[...]).astype(BF16)


def down_grad(half, g, dz):
    rows, width = dz.shape
    ff = g.shape[1]
    blocks = 2
    size = ff // 2 // blocks
    return pl.pallas_call(
        down_grad_kernel,
        grid_spec=pltpu.PrefetchScalarGridSpec(
            num_scalar_prefetch=1,
            grid=(blocks,),
            in_specs=[
                pl.BlockSpec((rows, size), lambda n, half: (0, half[0] * blocks + n)),
                pl.BlockSpec((rows, width), lambda n, half: (0, 0)),
            ],
            out_specs=pl.BlockSpec((size, width), lambda n, half: (n, 0)),
        ),
        out_shape=jax.ShapeDtypeStruct((ff // 2, width), BF16),
        compiler_params=pltpu.CompilerParams(
            dimension_semantics=("arbitrary",), vmem_limit_bytes=30 * MIB
        ),
        cost_estimate=kernel_cost(5),
        name="down_grad",
    )(half, in_hbm(g), in_hbm(dz))


def in_grad_kernel(half, h, o, du, da, out):
    width = h.shape[1]
    steps = (out.shape[1] - width // 2) // width
    for n in range(steps):

        @pl.when(pl.program_id(0) == n)
        def _():
            out[:, n * width : (n + 1) * width] = tn(h[...], du[...]).astype(BF16)

    @pl.when(pl.program_id(0) == steps)
    def _():
        out[:, steps * width :] = tn(o[...], da[...]).astype(BF16)


def in_grad(half, h, o, du, da):
    rows, width = h.shape
    steps = du.shape[1] // 2 // width
    cols = steps * width + width // 2
    whole = lambda shape: pl.BlockSpec(shape, lambda n, half: (0, 0))
    return pl.pallas_call(
        in_grad_kernel,
        grid_spec=pltpu.PrefetchScalarGridSpec(
            num_scalar_prefetch=1,
            grid=(steps + 1,),
            in_specs=[
                whole((rows, width)),
                whole((rows, width)),
                pl.BlockSpec((rows, width), lambda n, half: (0, half[0] * steps + jnp.minimum(n, steps - 1))),
                pl.BlockSpec((rows, width // 2), lambda n, half: (0, half[0])),
            ],
            out_specs=whole((width, cols)),
        ),
        out_shape=jax.ShapeDtypeStruct((width, cols), BF16),
        compiler_params=pltpu.CompilerParams(
            dimension_semantics=("arbitrary",), vmem_limit_bytes=34 * MIB
        ),
        cost_estimate=kernel_cost(6),
        name="in_grad",
    )(half, *map(in_hbm, (h, o, du, da)))


def proj_cut_kernel(places, x, x_other, d, d_other, a_keep, a_send, b_keep, b_send, total):
    size = d.shape[2]
    half = a_keep.shape[0]
    split = a_keep.shape[1]
    for n in range(3):

        @pl.when(pl.program_id(0) == n)
        def _():
            total[:, n * size : (n + 1) * size] = (tn(x[...], d[0]) + tn(x_other[...], d_other[0])).astype(BF16)

    @pl.when(pl.program_id(0) == 2)
    def _():
        for n, (keep, send) in enumerate(((a_keep, a_send), (b_keep, b_send))):
            cols = slice(n * split, n * split + keep.shape[1])
            for side, out in enumerate((keep, send)):
                at = pl.ds(pl.multiple_of((places[n] ^ side) * half, 16), half)
                out[...] = total[at, cols]


def proj_cut(places, x, x_other, d, d_other, split):
    rows, width = x.shape
    size = d.shape[2]
    whole = lambda shape: pl.BlockSpec(shape, lambda n, places: (0, 0))
    third = pl.BlockSpec((1, rows, size), lambda n, places: (n, 0, 0))
    outs = [(width // 2, w) for w in (split, 3 * size - split) for _ in range(2)]
    got = pl.pallas_call(
        proj_cut_kernel,
        grid_spec=pltpu.PrefetchScalarGridSpec(
            num_scalar_prefetch=1,
            grid=(3,),
            in_specs=[whole((rows, width)), whole((rows, width)), third, third],
            out_specs=[whole(o) for o in outs],
            scratch_shapes=[pltpu.VMEM((width, 3 * size), BF16)],
        ),
        out_shape=[jax.ShapeDtypeStruct(o, BF16) for o in outs],
        compiler_params=pltpu.CompilerParams(
            dimension_semantics=("arbitrary",), vmem_limit_bytes=30 * MIB
        ),
        cost_estimate=kernel_cost(7),
        name="proj_cut",
    )(places, *map(in_hbm, (x, x_other, d, d_other)))
    return [(got[0], got[1]), (got[2], got[3])]


def attention_back_kernel(
    part, qlen, plen, q, k, v, o, do, lse,
    d_o, small_o,
    kmask, lse_p, lse_q, delta_p, delta_q,
):
    step = pl.program_id(0)
    first_head = part[0] * (q.shape[1] // 64)
    width = q.shape[1]
    pairs = width // 128
    lane = lax.broadcasted_iota(jnp.int32, (1, 128), 1)
    low = (lane < 64).astype(F32)
    lanes = (low, 1.0 - low)
    ones = ((lane == 64).astype(F32), (lane == 0).astype(F32))
    q_gain = [(t * 0.125).astype(BF16) for t in lanes]
    keep = [t.astype(BF16) for t in lanes]
    one = [t.astype(BF16) for t in ones]

    q_valid = lax.broadcasted_iota(jnp.int32, (QRY_LEN, 128), 0) < qlen[step]
    p_valid = lax.broadcasted_iota(jnp.int32, (PASS_LEN, 128), 0) < plen[step]
    for side in range(2):
        kmask[side, :QRY_LEN, :] = jnp.where(q_valid, 0.0, NEG * ones[side]).astype(BF16)
        kmask[side, QRY_LEN:, :] = jnp.where(p_valid, 0.0, NEG * ones[side]).astype(BF16)

    q_rows, p_rows = pl.ds(0, QRY_LEN), pl.ds(QRY_LEN, PASS_LEN)
    head_of = (
        lax.broadcasted_iota(jnp.int32, (16, width), 1) // 64
        == lax.broadcasted_iota(jnp.int32, (16, width), 0)
    ).astype(F32).astype(BF16)
    for rows, lse_t, delta_t in ((q_rows, lse_q, delta_q), (p_rows, lse_p, delta_p)):
        lse_t[...] = jnp.transpose(lse[rows, :])
        prod = do[rows, :].astype(F32) * o[rows, :].astype(F32)
        hi = prod.astype(BF16)
        lo = (prod - hi.astype(F32)).astype(BF16)
        delta_t[...] = nt(head_of, hi) + nt(head_of, lo)

    def attend(pair, carry):
        cols = pl.ds(pl.multiple_of(pair * 128, 128), 128)
        for rows, lse_t, delta_t in ((q_rows, lse_q, delta_q), (p_rows, lse_p, delta_p)):
            qp, kp, vp, dop = q[rows, cols], k[rows, cols], v[rows, cols], do[rows, cols]
            qm = [qp * q_gain[side] for side in range(2)]
            km = [kp * q_gain[side] for side in range(2)]
            dm = [dop * keep[side] for side in range(2)]
            st = [nt(kp * keep[side] + kmask[side, rows, :], qm[side] + one[side]) for side in range(2)]
            dpt = [nt(vp, dm[side]) for side in range(2)]
            pt = [
                jnp.exp(st[side] - lse_t[pl.ds(first_head + 2 * pair + side, 1), :]) for side in range(2)
            ]
            dst = [
                (pt[side] * (dpt[side] - delta_t[pl.ds(2 * pair + side, 1), :])).astype(BF16) for side in range(2)
            ]
            d_o[2, rows, cols] = sum(nn(pt[side].astype(BF16), dm[side]) for side in range(2)).astype(BF16)
            d_o[1, rows, cols] = sum(nn(dst[side], qm[side]) for side in range(2)).astype(BF16)
            d_o[0, rows, cols] = sum(tn(dst[side], km[side]) for side in range(2)).astype(BF16)
        return carry

    lax.fori_loop(0, pairs, attend, 0, unroll=pairs)

    @pl.when(step == 0)
    def _():
        small_o[...] = jnp.zeros_like(small_o)

    small_o[0:1, :] += jnp.sum(d_o[0].astype(F32), axis=0, keepdims=True)
    small_o[1:2, :] += jnp.sum(d_o[2].astype(F32), axis=0, keepdims=True)


def attention_back(part, qlen, plen, q, k, v, o, do, lse):
    seqs = qlen.shape[0]
    rows, full = q.shape
    width = full // 2
    whole = lambda shape: pl.BlockSpec(shape, lambda i, part: (0,) * len(shape))
    smem = pl.BlockSpec(memory_space=pltpu.SMEM)
    block = pl.BlockSpec((PAIR_LEN, width), lambda i, part: (i, part[0]))
    return pl.pallas_call(
        attention_back_kernel,
        grid_spec=pltpu.PrefetchScalarGridSpec(
            num_scalar_prefetch=1,
            grid=(seqs,),
            in_specs=[smem, smem] + [block] * 5 + [pl.BlockSpec((PAIR_LEN, 128), lambda i, part: (i, 0))],
            out_specs=[pl.BlockSpec((3, PAIR_LEN, width), lambda i, part: (0, i, 0)), whole((8, width))],
            scratch_shapes=[
                pltpu.VMEM((2, PAIR_LEN, 128), BF16),
                pltpu.VMEM((128, PASS_LEN), F32),
                pltpu.VMEM((128, QRY_LEN), F32),
                pltpu.VMEM((16, PASS_LEN), F32),
                pltpu.VMEM((16, QRY_LEN), F32),
            ],
        ),
        out_shape=[pltpu.HBM((3, rows, width), BF16), jax.ShapeDtypeStruct((8, width), F32)],
        compiler_params=pltpu.CompilerParams(
            dimension_semantics=("arbitrary",), vmem_limit_bytes=22 * MIB
        ),
        cost_estimate=kernel_cost(15),
        name="attention_back",
    )(part, qlen, plen, *map(in_hbm, (q, k, v, o, do, lse)))


def input_grad_kernel(core, dr1, d, d_rest, wq, wk, wv, gq_o, gp_o):
    size = d.shape[2]
    grad = dr1[...]
    for n, w in enumerate((wq, wk, wv)):
        for part, side in ((d, 0), (d_rest, 1)):
            cols = pl.ds(pl.multiple_of((core[0] ^ side) * size, 128), size)
            grad += nt(part[n], w[:, cols])
    gq_o[...] = grad[:QRY_LEN]
    gp_o[...] = grad[QRY_LEN:]


def input_grad(core, dr1, d, d_rest, wq, wk, wv):
    rows, width = dr1.shape
    seqs = rows // PAIR_LEN
    block = pl.BlockSpec((PAIR_LEN, width), lambda i, core: (i, 0))
    thirds = pl.BlockSpec((3, PAIR_LEN, width // 2), lambda i, core: (0, i, 0))
    weight = pl.BlockSpec((width, width), lambda i, core: (0, 0))
    return pl.pallas_call(
        input_grad_kernel,
        grid_spec=pltpu.PrefetchScalarGridSpec(
            num_scalar_prefetch=1,
            grid=(seqs,),
            in_specs=[block, thirds, thirds] + [weight] * 3,
            out_specs=[
                pl.BlockSpec((QRY_LEN, width), lambda i, core: (i, 0)),
                pl.BlockSpec((PASS_LEN, width), lambda i, core: (i, 0)),
            ],
        ),
        out_shape=[
            jax.ShapeDtypeStruct((seqs * QRY_LEN, width), F32),
            jax.ShapeDtypeStruct((seqs * PASS_LEN, width), F32),
        ],
        compiler_params=pltpu.CompilerParams(
            dimension_semantics=("arbitrary",), vmem_limit_bytes=26 * MIB
        ),
        cost_estimate=kernel_cost(10),
        name="input_grad",
    )(core, *map(in_hbm, (dr1, d, d_rest, wq, wk, wv)))


def widen(out, cols, value):
    out[:, cols[0] : cols[1]] = value.astype(F32)


def place_down_kernel(bit, mine, other, out):
    half = pl.program_id(0)

    @pl.when(half == 0)
    def _():
        out[...] = mine[...].astype(F32)

    @pl.when(half == 1)
    def _():
        out[...] = other[...].astype(F32)


def place_down(bit, mine, other):
    rows, cols = mine.shape
    chunks = 4
    step = rows // chunks
    return pl.pallas_call(
        place_down_kernel,
        grid_spec=pltpu.PrefetchScalarGridSpec(
            num_scalar_prefetch=1,
            grid=(2, chunks),
            in_specs=[
                pl.BlockSpec((step, cols), lambda h, n, bit: (jnp.where(h == 0, n, chunks - 1), 0)),
                pl.BlockSpec((step, cols), lambda h, n, bit: (jnp.where(h == 1, n, 0), 0)),
            ],
            out_specs=pl.BlockSpec((step, cols), lambda h, n, bit: ((h ^ bit[0]) * chunks + n, 0)),
        ),
        out_shape=jax.ShapeDtypeStruct((2 * rows, cols), F32),
        compiler_params=pltpu.CompilerParams(
            dimension_semantics=("arbitrary", "arbitrary"), vmem_limit_bytes=16 * MIB
        ),
        cost_estimate=kernel_cost(5),
        name="place_down",
    )(bit, mine, other)


def place_columns(bit, sums, widths, write, name):
    rows = sums[0][0].shape[0]
    chunks = 4
    step = rows // chunks
    arrays = [a for pair in sums for a in pair]

    def kernel(bit, *refs):
        ins, outs = refs[: len(arrays)], refs[len(arrays) :]
        pairs = [(ins[2 * n], ins[2 * n + 1]) for n in range(len(sums))]

        @pl.when(bit[0] == 0)
        def _():
            write(outs, pairs)

        @pl.when(bit[0] == 1)
        def _():
            write(outs, [p[::-1] for p in pairs])

    return pl.pallas_call(
        kernel,
        grid_spec=pltpu.PrefetchScalarGridSpec(
            num_scalar_prefetch=1,
            grid=(chunks,),
            in_specs=[pl.BlockSpec((step, a.shape[1]), lambda n, bit: (n, 0)) for a in arrays],
            out_specs=[pl.BlockSpec((step, w), lambda n, bit: (n, 0)) for w in widths],
        ),
        out_shape=[jax.ShapeDtypeStruct((rows, w), F32) for w in widths],
        compiler_params=pltpu.CompilerParams(
            dimension_semantics=("arbitrary",), vmem_limit_bytes=20 * MIB
        ),
        cost_estimate=kernel_cost(5),
        name=name,
    )(bit, *arrays)


def write_in(outs, pairs):
    for n, half in enumerate(pairs[0]):
        at = 0
        for out in outs:
            size = out.shape[1] // 2
            widen(out, (n * size, (n + 1) * size), half[:, at : at + size])
            at += size


def write_proj(outs, pairs):
    size = outs[0].shape[1] // 2
    for n, half in enumerate(pairs[0]):
        for m, out in enumerate(outs):
            widen(out, (n * size, (n + 1) * size), half[:, m * size : (m + 1) * size])


IN_FLIGHT = 5


def swap_with(value, mask, device_count):
    return lax.ppermute(value, AXES, [(i, i ^ mask) for i in range(device_count)])


def far_groups(device_count):
    masks, mask = [], 4
    while mask < device_count // 2:
        masks.append(mask)
        mask *= 2
    return [masks[n : n + 2] for n in range(0, len(masks), 2)]


def combos_of(group):
    combos = [0]
    for mask in reversed(group):
        combos = combos + [c ^ mask for c in combos]
    return combos


def gather_relative(value, device_count):
    groups = [[device_count // 2, 2]] + far_groups(device_count) + [[1]]
    relative = [0]
    for n, group in enumerate(groups):
        combos = combos_of(group)
        got = [value] + [swap_with(value, c, device_count) for c in combos[1:]]
        relative = [c ^ r for c in combos for r in relative]
        if n < len(groups) - 1:
            value = jnp.concatenate(got, axis=0)
    return got, relative


def whole_call(kernel, scalars, arrays, outs, name):
    spec = lambda shape: pl.BlockSpec(shape, lambda i, s: (0, 0))
    return pl.pallas_call(
        kernel,
        grid_spec=pltpu.PrefetchScalarGridSpec(
            num_scalar_prefetch=1,
            grid=(1,),
            in_specs=[spec(a.shape) for a in arrays],
            out_specs=[spec(o) for o in outs],
        ),
        out_shape=[jax.ShapeDtypeStruct(o, BF16) for o in outs],
        compiler_params=pltpu.CompilerParams(vmem_limit_bytes=24 * MIB),
        cost_estimate=kernel_cost(1),
        name=name,
    )(scalars, *arrays)


def fold(tuples, places, parts, ways=2):
    rows = tuples[0][0].shape[0] // ways
    widths = [sum(c1 - c0 for _, c0, c1 in p) for p in parts]
    arrays = [a for one in tuples for a in one]

    def add(values):
        total = values[0].astype(F32)
        for value in values[1:]:
            total = total + value.astype(F32)
        return total.astype(BF16)

    if rows % 16:
        results = []
        for part, place in zip(parts, places):
            total = jnp.concatenate([add([a[:, c0:c1] for a in tuples[p]]) for p, c0, c1 in part], 1)
            results.append(
                [lax.dynamic_slice_in_dim(total, (place ^ n) * rows, rows, 0) for n in range(ways)]
            )
        return results

    def kernel(place, *refs):
        taken, ref_tuples = 0, []
        for one in tuples:
            ref_tuples.append(refs[taken : taken + len(one)])
            taken += len(one)
        outs = refs[taken:]
        for m, part in enumerate(parts):
            for n in range(ways):
                at = pl.ds(pl.multiple_of((place[m] ^ n) * rows, 16), rows)
                col = 0
                for p, c0, c1 in part:
                    outs[ways * m + n][:, col : col + c1 - c0] = add([r[at, c0:c1] for r in ref_tuples[p]])
                    col += c1 - c0

    got = whole_call(
        kernel, jnp.stack(places), arrays, [(rows, w) for w in widths for _ in range(ways)], "fold"
    )
    return [got[ways * m : ways * (m + 1)] for m in range(len(parts))]


def unfold(tuples, places, parts):
    rows = tuples[0][0].shape[0]
    ways = len(tuples[0])
    widths = [sum(c1 - c0 for _, c0, c1 in p) for p in parts]
    if rows % 16:
        joined = [
            jnp.concatenate([lax.select_n(s, *[t[b ^ n] for n in range(ways)]) for b in range(ways)], 0)
            if ways > 2
            else jnp.where(s == 1, jnp.concatenate([t[1], t[0]], 0), jnp.concatenate([t[0], t[1]], 0))
            for t, s in zip(tuples, places)
        ]
        return [jnp.concatenate([joined[p][:, c0:c1] for p, c0, c1 in part], 1) for part in parts]

    def kernel(place, *refs):
        outs = refs[ways * len(tuples) :]
        for m, part in enumerate(parts):
            col = 0
            for p, c0, c1 in part:
                for n in range(ways):
                    at = pl.ds(pl.multiple_of((place[p] ^ n) * rows, 16), rows)
                    outs[m][at, col : col + c1 - c0] = refs[ways * p + n][:, c0:c1]
                col += c1 - c0

    return whole_call(
        kernel, jnp.stack(places), [a for t in tuples for a in t], [(ways * rows, w) for w in widths], "unfold"
    )


def place_of(group, me):
    pos = jnp.int32(0)
    for mask in group:
        pos = 2 * pos + ((me & mask) != 0).astype(jnp.int32)
    return pos


def reduction(send, kept, split, wide, me, device_count, ready=None):
    top = device_count // 2
    far = far_groups(device_count)
    back = [[mask] for group in far for mask in group]
    if not wide:
        far = back
    elif wide == "both":
        back = far
    cols = sum(c[0].shape[1] for c in ready) if ready else send.shape[1]
    both = [[(0, 0, split)], [(0, split, cols)]]
    apart = [[(0, 0, split)], [(1, 0, cols - split)]]
    merged = [[(0, 0, split), (1, 0, cols - split)]]
    alone = [[(0, 0, cols)]]

    def place(group):
        return place_of(group, me)

    sums = None
    if not ready:
        got = yield [(send, 1)]
        sums = [(kept[0], got[0])]
    for masks, parts in (((top, 2), both), ((2, top), apart)):
        cut = fold(sums, [place([m]) for m in masks], parts) if sums else ready
        got = yield [(c[1], m) for c, m in zip(cut, masks)]
        sums = [(c[0], g) for c, g in zip(cut, got)]
    for n, group in enumerate(far):
        combos = combos_of(group)
        (cut,) = fold(sums, [place(group)], alone if n else merged, len(combos))
        got = yield list(zip(cut[1:], combos[1:]))
        sums = [(cut[0], *got)]
    total = sums[0][0].astype(F32)
    for value in sums[0][1:]:
        total = total + value.astype(F32)
    mine = total.astype(BF16)
    for group in reversed(back):
        got = yield [(mine, c) for c in combos_of(group)[1:]]
        last = group is back[0]
        mine = unfold([(mine, *got)], [place(group)], both if last else alone)
        mine = mine if last else mine[0]
    for masks, parts in (((2, top), apart), ((top, 2), merged)):
        got = yield [(p, m) for p, m in zip(mine, masks)]
        mine = unfold(list(zip(mine, got)), [place([m]) for m in masks], parts)
    (got,) = yield [(mine[0], 1)]
    return mine[0], got


def exchange(value):
    (got,) = yield [(value, 1)]
    return got


def small_sum(values, device_count):
    mask = 1
    while mask < device_count:
        (got,) = yield [(values, mask)]
        values = values + got
        mask *= 2
    return values


class Line:
    def __init__(self, steps, device_count):
        self.steps = steps
        self.count = device_count
        self.sum = None
        self.want = next(steps)

    def take(self, got):
        try:
            self.want = self.steps.send(got)
        except StopIteration as end:
            self.want, self.sum = None, end.value


def slot(lines, work=None, values=(), kept=None):
    flying = []
    for n in lines:
        if n.want is not None and sum(len(f.want) for f in flying) + len(n.want) <= IN_FLIGHT:
            flying.append(n)
    lines = flying
    arrays = [[a for a, _ in n.want] for n in lines]
    arrays, values = lax.optimization_barrier((arrays, tuple(values)))
    got = [[swap_with(a, m, n.count) for a, (_, m) in zip(sends, n.want)] for sends, n in zip(arrays, lines)]
    out = work(*values) if work is not None else ()
    got, out = lax.optimization_barrier((got, out))
    if kept is not None:
        kept.append(out)
    for n, g in zip(lines, got):
        n.take(g)
    return out


def body(
    query_tokens,
    passage_tokens,
    query_lengths,
    passage_lengths,
    positives,
    w_query,
    b_query,
    w_key,
    w_value,
    b_value,
    w_out,
    b_out,
    norm1_gain,
    norm1_bias,
    w_in,
    b_in,
    w_down,
    b_down,
    norm2_gain,
    norm2_bias,
    query_out_grad,
    passage_out_grad,
):
    seqs = query_lengths.shape[0]
    width = query_tokens.shape[1]
    device_count = lax.axis_size(AXES)
    my_index = lax.axis_index(AXES)
    params = dict(
        w_query=w_query, b_query=b_query, w_key=w_key, w_value=w_value, b_value=b_value, w_out=w_out,
        b_out=b_out, norm1_gain=norm1_gain, norm1_bias=norm1_bias, w_in=w_in, b_in=b_in, w_down=w_down,
        b_down=b_down, norm2_gain=norm2_gain, norm2_bias=norm2_bias,
    )
    (
        query_out, passage_out, q, k, v, o, lse, xhat1, rstd1, h1b, g, gelu_slope, x_rows, xhat2, rstd2, unit, mean,
    ) = forward(query_tokens, passage_tokens, query_lengths, passage_lengths, params)
    units, relative = gather_relative(unit, device_count)
    owner = jnp.array(relative, jnp.int32) ^ my_index
    ids = (owner[:, None] * seqs + jnp.arange(seqs, dtype=jnp.int32)[None, :]).reshape(-1)
    ids = jnp.repeat(ids, 2)
    dz, dr2, small2, loss_sum = loss_and_second_norm(
        units, positives[:, None], ids[:, None], ids[None, :], mean, query_lengths, passage_lengths, query_out_grad, passage_out_grad,
        xhat2, rstd2, norm2_gain,
    )
    loss = loss_sum[0, 0] / (seqs * device_count)
    core = (my_index & 1).astype(jnp.int32)[None]
    other = 1 - core

    def start_line(lines, make, values, wide=""):
        kept = []
        send = slot(lines, lambda *v: make(other, *v), values)
        split = (send.shape[1] + 255) // 256 * 128
        new = Line(reduction(send, kept, split, wide, my_index, device_count), device_count)
        slot(lines + [new], lambda *v: make(core, *v), values, kept)
        return new

    down = start_line([], lambda half, d: down_grad(half, g, d), (dz,))
    x_line = Line(exchange(in_hbm(x_rows)), device_count)
    acc, du, grad_b_in = dr2, None, []
    for first, last in ((0, 4), (4, 6)):
        du, bias, acc = slot(
            [down, x_line],
            lambda *arrays: ffn_back(*arrays[:5], first, last, arrays[5] if first else None),
            (dz, acc, gelu_slope, w_down, w_in, *([du] if first else [])),
        )
        grad_b_in.append(bias)
    dr1, da, do, small1 = slot([down], first_norm_back, (acc, xhat1, rstd1, norm1_gain, w_out))
    up = start_line([down], in_grad, (h1b, o, du, da), wide="out")
    sources = (q, k, v, o, do, lse)
    lengths = (query_lengths, passage_lengths)
    d_rest, small_rest = slot([down, up], lambda *arrays: attention_back(other, *lengths, *arrays), sources)
    d_line = Line(exchange(d_rest), device_count)
    d_own, small_own = slot([down, up, d_line], lambda *arrays: attention_back(core, *lengths, *arrays), sources)
    small0 = jnp.where(
        core == 1, jnp.concatenate([small_rest, small_own], 1), jnp.concatenate([small_own, small_rest], 1)
    )
    packed = jnp.concatenate(
        [small0, small1, small2, jnp.concatenate(grad_b_in, 1).reshape(-1, width)], 0
    )
    small = Line(small_sum(packed, device_count), device_count)
    split = (3 * width // 2 + 255) // 256 * 128
    places = jnp.stack([place_of([mask], my_index) for mask in (device_count // 2, 2)])
    ready = slot(
        [down, up],
        lambda *arrays: proj_cut(places, *arrays, split),
        (x_rows, x_line.sum, d_own, d_line.sum),
    )
    proj = Line(reduction(None, None, split, "both", my_index, device_count, ready), device_count)
    bit = core
    while down.want is not None:
        slot([down, up, proj, small])
    grad_w_down = slot([up, proj, small], place_down, (bit, *down.sum))
    slot([up, proj])
    query_input_grad, passage_input_grad = slot(
        [up, proj], lambda *arrays: input_grad(core, *arrays), (dr1, d_own, d_rest, w_query, w_key, w_value)
    )
    while up.want is not None:
        slot([up, proj, small])
    grad_w_in, grad_w_out = slot(
        [proj, small],
        lambda bit, *pair: place_columns(bit, [pair], (g.shape[1], width), write_in, "place_in"),
        (bit, *up.sum),
    )
    while proj.want is not None or small.want is not None:
        slot([proj, small])
    grad_w_query, grad_w_key, grad_w_value = place_columns(
        bit, [proj.sum], (width,) * 3, write_proj, "place_proj"
    )
    packed = small.sum
    return (
        query_out,
        passage_out,
        query_input_grad,
        passage_input_grad,
        loss,
        grad_w_query,
        packed[0],
        grad_w_key,
        grad_w_value,
        packed[1],
        grad_w_out,
        packed[10],
        packed[8],
        packed[9],
        grad_w_in,
        packed[24:].reshape(-1),
        grad_w_down,
        packed[18],
        packed[16],
        packed[17],
    )


def solution(mesh):
    placed = (
        P(("stream", "batch"), None),
        P(("stream", "batch"), None),
        P(("stream", "batch")),
        P(("stream", "batch")),
        P(),
        P(),
        P(),
        P(),
        P(),
        P(),
        P(),
        P(),
        P(),
        P(),
        P(),
        P(),
        P(),
        P(),
        P(),
        P(),
        P(("stream", "batch"), None),
        P(("stream", "batch"), None),
    )
    return jax.shard_map(
        body,
        mesh=mesh,
        in_specs=placed,
        out_specs=(
            P(("stream", "batch"), None),
            P(("stream", "batch"), None),
            P(("stream", "batch"), None),
            P(("stream", "batch"), None),
            P(),
            P(),
            P(),
            P(),
            P(),
            P(),
            P(),
            P(),
            P(),
            P(),
            P(),
            P(),
            P(),
            P(),
            P(),
            P(),
        ),
        check_vma=False,
    )
```
